32 devices in a mesh: dp: 16 (over z, x, core), tensor: 2 (over y).
Axes of the slice: x: 2, y: 2, z: 4, core: 2. Of those that a mesh axis runs over, the one named last changes fastest.
Arguments:
- tokens: bfloat16 [8192, 1536], P('dp'), may hold values from -6 to 6
- cotangent: bfloat16 [8192, 1536], P('dp'), may hold values from -6 to 6
- doc_ids: int32 [8192], P('dp'), may hold values from -1 to 3, as said below
- norm_gains: float32 [2, 1536], replicated, may hold values from 0.5 to 1.5
- qkv_weight: float32 [1536, 2048], P('dp', 'tensor'), may hold values from -0.15625 to 0.15625
- qkv_bias: float32 [2048], P('tensor'), may hold values from -7 to 7
- out_weight: float32 [1536, 1536], P('dp', 'tensor'), may hold values from -0.4375 to 0.4375
- gate_up_weight: float32 [2, 1536, 8960], P(None, 'dp', 'tensor'), may hold values from -0.15625 to 0.15625
- down_weight: float32 [1536, 8960], P('dp', 'tensor'), may hold values from -0.0625 to 0.0625
- gains_moment: float32 [2, 1536], replicated, may hold values from -256 to 256
- qkv_moment: float32 [1536, 2048], P('dp', 'tensor'), may hold values from -320 to 320
- bias_moment: float32 [2048], P('tensor'), may hold values from -56 to 56
- out_moment: float32 [1536, 1536], P('dp', 'tensor'), may hold values from -28 to 28
- gate_up_moment: float32 [2, 1536, 8960], P(None, 'dp', 'tensor'), may hold values from -28 to 28
- down_moment: float32 [1536, 8960], P('dp', 'tensor'), may hold values from -56 to 56
Outputs:
- layer_out: float32 [8192, 1536], P('dp')
- tokens_grad: float32 [8192, 1536], P('dp')
- gains_grad: float32 [2, 1536], replicated
- qkv_grad: float32 [1536, 2048], P('dp', 'tensor')
- bias_grad: float32 [2048], P('tensor')
- out_grad: float32 [1536, 1536], P('dp', 'tensor')
- gate_up_grad: float32 [2, 1536, 8960], P(None, 'dp', 'tensor')
- down_grad: float32 [1536, 8960], P('dp', 'tensor')
- gains_new: float32 [2, 1536], replicated
- qkv_new: float32 [1536, 2048], P('dp', 'tensor')
- bias_new: float32 [2048], P('tensor')
- out_new: float32 [1536, 1536], P('dp', 'tensor')
- gate_up_new: float32 [2, 1536, 8960], P(None, 'dp', 'tensor')
- down_new: float32 [1536, 8960], P('dp', 'tensor')
- gains_moment_new: float32 [2, 1536], replicated
- qkv_moment_new: float32 [1536, 2048], P('dp', 'tensor')
- bias_moment_new: float32 [2048], P('tensor')
- out_moment_new: float32 [1536, 1536], P('dp', 'tensor')
- gate_up_moment_new: float32 [2, 1536, 8960], P(None, 'dp', 'tensor')
- down_moment_new: float32 [1536, 8960], P('dp', 'tensor')
The draws below stay inside these ranges and needn't reach their ends.
Inputs may be any that keep to these rules, and one draw needn't show every extreme that they name: `doc_ids`: within each block of 512 slots (one index of dp) the filled slots come first, as whole sequences numbered upward from 0 (numbers may be skipped), followed by empty slots marked -1; a block holds at most 4 sequences; in every draw one block is a single sequence of 512 tokens and one block holds 4 sequences.
All inputs are finite; a program needn't handle non-finite values.
Results may differ from the reference program's by a relative error of at most 0.018.
The reference program's roundings to bfloat16 on the way count: a program that leaves them out, or rounds other values in their place, can miss the bound.
Values may be sent and summed in bfloat16 or wider, within the bound.
A program may use at most 384 MiB of HBM per device.

```python
import jax
import jax.numpy as jnp
from jax import lax

D = 1536
H = 12
KVH = 2
HD = 128
FF = 8960
FFB = 896
C = 512
MAXSEQ = 4
NSI = 5
HT = 6
KT = 1
GW = 1024
NBF = 5
TOKENS = 8192
N_DP = 16
N_TENSOR = 2


def draw_doc_ids(key, part):
    fill_key, count_key, cut_key, full_key, other_key = jax.random.split(jax.random.fold_in(key, 17), 5)
    fills = jax.random.randint(fill_key, (N_DP,), C // 4, C + 1).astype(jnp.int32)
    counts = jax.random.randint(count_key, (N_DP,), 1, MAXSEQ + 1).astype(jnp.int32)
    full = jax.random.randint(full_key, (), 0, N_DP).astype(jnp.int32)
    other = ((full + jax.random.randint(other_key, (), 1, N_DP)) % N_DP).astype(jnp.int32)
    ranks = jnp.arange(N_DP, dtype=jnp.int32)
    fills = jnp.where(ranks == full, C, fills)
    counts = jnp.where(ranks == full, 1, jnp.where(ranks == other, MAXSEQ, counts))
    cuts = jax.random.randint(cut_key, (N_DP, MAXSEQ - 1), 1, C).astype(jnp.int32)
    cuts = 1 + (cuts - 1) * (fills[:, None] - 1) // (C - 1)
    slots = jnp.arange(MAXSEQ - 1, dtype=jnp.int32)
    even_cuts = (slots[None, :] + 1) * fills[:, None] // MAXSEQ
    cuts = jnp.where(ranks[:, None] == other, even_cuts, cuts)
    cuts = jnp.where(slots[None, :] < counts[:, None] - 1, cuts, C + 1)
    cuts = jnp.sort(cuts, axis=-1)
    places = jnp.arange(C, dtype=jnp.int32)
    ids = jnp.sum((places[None, :, None] >= cuts[:, None, :]).astype(jnp.int32), axis=-1)
    ids = jnp.where(places[None, :] < fills[:, None], ids, -1)
    return ids.reshape(N_DP * C).astype(jnp.int32)


def draw_qkv_bias(key, part):
    noise_key, sign_key, order_key = jax.random.split(jax.random.fold_in(key, 29), 3)
    base_noise = jnp.clip(0.5 * jax.random.normal(noise_key, (N_TENSOR, HT + 2 * KT, HD), jnp.float32), -1.5, 1.5)
    query_level = 5.0
    key_level = 4.0
    sign_pattern = (2 * jax.random.randint(sign_key, (N_TENSOR, 1, HD), 0, 2) - 1).astype(jnp.float32)
    head_order = jax.vmap(lambda subkey: jax.random.permutation(subkey, HT))(jax.random.split(order_key, N_TENSOR))
    strength = query_level * jnp.maximum(0.0, 1.0 - head_order.astype(jnp.float32) / 3.0)
    head_scale = jnp.concatenate([strength, jnp.full((N_TENSOR, KT), key_level, jnp.float32), jnp.zeros((N_TENSOR, KT), jnp.float32)], axis=1)
    drawn = base_noise + head_scale[:, :, None] * sign_pattern
    return drawn.reshape(N_TENSOR * (HT + 2 * KT) * HD).astype(jnp.float32)


def shard_levels(key, extent, cuts, low, high):
    level, own = 1.0, jax.random.fold_in(key, 6)
    for axis_at, parts in cuts:
        draws = jnp.exp(jax.random.uniform(jax.random.fold_in(own, axis_at), (parts,), jnp.float32, low / len(cuts), high / len(cuts)))
        level = level * jnp.repeat(draws, extent[axis_at] // parts).reshape([-1 if axis == axis_at else 1 for axis in range(len(extent))])
    return level


def noise(rng, shape, deviation, bound, pieces=(), kind=jnp.bfloat16):
    result = jax.random.normal(rng, shape, jnp.float32) * deviation
    if len(pieces) > 0:
        result = shard_levels(rng, shape, pieces, -0.22, 0.18) * result
    return jnp.clip(result, min=-bound, max=bound).astype(kind)


def setup_inputs(seed: int = 0) -> dict:
    key_of = jax.random.split(jax.random.key(seed), 16)
    return {
        "tokens": noise(key_of[0], (TOKENS, D), 1.0, 6.0, ((0, 16),)),
        "cotangent": noise(key_of[1], (TOKENS, D), 1.0, 6.0, ((0, 16),)),
        "doc_ids": draw_doc_ids(jax.random.fold_in(key_of[15], 71), 0),
        "norm_gains": jnp.clip(1.0 + 0.1 * jax.random.normal(key_of[3], (2, D), jnp.float32), 0.5, 1.5),
        "qkv_weight": noise(key_of[4], (D, N_TENSOR * GW), D ** -0.5, 0.15625, ((0, 16), (1, 2)), jnp.float32),
        "qkv_bias": draw_qkv_bias(jax.random.fold_in(key_of[15], 71), 0),
        "out_weight": noise(key_of[6], (D, H * HD), (H * HD // 8) ** -0.5, 0.4375, ((0, 16), (1, 2)), jnp.float32),
        "gate_up_weight": noise(key_of[7], (2, D, FF), D ** -0.5, 0.15625, ((1, 16), (2, 2)), jnp.float32),
        "down_weight": noise(key_of[8], (D, FF), FF ** -0.5, 0.0625, ((0, 16), (1, 2)), jnp.float32),
        "gains_moment": noise(key_of[9], (2, D), (0.5 * TOKENS ** 0.5), 256.0, (), jnp.float32),
        "qkv_moment": noise(key_of[10], (D, N_TENSOR * GW), (0.6 * TOKENS ** 0.5), 320.0, ((0, 16), (1, 2)), jnp.float32),
        "bias_moment": noise(key_of[11], (N_TENSOR * GW,), (0.1 * TOKENS ** 0.5), 56.0, ((0, 2),), jnp.float32),
        "out_moment": noise(key_of[12], (D, H * HD), (0.05 * TOKENS ** 0.5), 28.0, ((0, 16), (1, 2)), jnp.float32),
        "gate_up_moment": noise(key_of[13], (2, D, FF), (0.05 * TOKENS ** 0.5), 28.0, ((1, 16), (2, 2)), jnp.float32),
        "down_moment": noise(key_of[14], (D, FF), (0.1 * TOKENS ** 0.5), 56.0, ((0, 16), (1, 2)), jnp.float32),
    }


@jax.custom_vjp
def low(v):
    return lax.optimization_barrier(v.astype(jnp.bfloat16)).astype(jnp.float32)

@jax.custom_vjp
def low_back(v):
    return v

def low_keep(v):
    return (low(v), None)

def low_pass(kept, grad):
    return (grad,)

def back_keep(v):
    return (v, None)

def back_low(kept, grad):
    return (low(grad),)
low.defvjp(low_keep, low_pass)
low_back.defvjp(back_keep, back_low)
HIGH = lax.Precision.HIGHEST
EPS = 1e-06
THETA = 1000000.0
MOMENTUM = 0.5
LR_MATRIX = 0.2
LR_OUT = 0.8
LR_VECTOR = 0.1
LR_BIAS = 1.0
NS_A = 3.4445
NS_B = -4.775
NS_C = 2.0315

def matmul(left, right):
    return jnp.dot(left, right, precision=HIGH, preferred_element_type=jnp.float32)

def positions_of(block_ids):
    index = jnp.arange(block_ids.shape[0], dtype=jnp.int32)
    change = jnp.concatenate([jnp.ones((1,), dtype=bool), block_ids[1:] != block_ids[:-1]])
    start = lax.cummax(jnp.where(change, index, jnp.zeros_like(index)), axis=0)
    return index - start

def rotate(values, cosine, sine):
    half = values.shape[-1] // 2
    first = values[..., :half]
    second = values[..., half:]
    cosine = cosine[:, None, :]
    sine = sine[:, None, :]
    return jnp.concatenate([first * cosine - second * sine, second * cosine + first * sine], axis=-1)

def rms_norm(values, gain):
    return values * lax.rsqrt(lax.optimization_barrier(jnp.mean(values * values, axis=-1, keepdims=True)) + EPS) * gain

def attend(query, keys, values, block_ids):
    share = H // KVH
    keys_all = jnp.repeat(keys, share, axis=1)
    values_all = jnp.repeat(values, share, axis=1)
    scores = jnp.einsum('qhd,khd->hqk', query, keys_all, precision=HIGH) * HD ** (-0.5)
    scores = low_back(scores)
    index = jnp.arange(block_ids.shape[0])
    allowed = (block_ids[:, None] == block_ids[None, :]) & (index[None, :] <= index[:, None])
    scores = jnp.where(allowed[None], scores, -1e+30)
    top = lax.optimization_barrier(jnp.max(scores, axis=-1, keepdims=True))
    expo = jnp.exp(scores - top)
    probs = low(expo / lax.optimization_barrier(jnp.sum(expo, axis=-1, keepdims=True)))
    return jnp.einsum('hqk,khd->qhd', probs, values_all, precision=HIGH)

def forward(tokens32, norm_gains, qkv_weight, qkv_bias, out_weight, gate_up_weight, down_weight, doc_ids, cosine, sine):
    normed = low(rms_norm(tokens32, norm_gains[0]))
    qkv = low_back(matmul(normed, low(qkv_weight)) + qkv_bias)
    grouped = qkv.reshape(TOKENS, N_TENSOR, HT + 2 * KT, HD)
    query = grouped[:, :, :HT].reshape(TOKENS, H, HD)
    keys = grouped[:, :, HT:HT + KT].reshape(TOKENS, KVH, HD)
    values = grouped[:, :, HT + KT:].reshape(TOKENS, KVH, HD)
    query = low(rotate(query, cosine, sine))
    keys = low(rotate(keys, cosine, sine))
    values = low(values)
    block_fn = jax.checkpoint(attend)
    attn = lax.map(lambda items: block_fn(*items), (query.reshape(N_DP, C, H, HD), keys.reshape(N_DP, C, KVH, HD), values.reshape(N_DP, C, KVH, HD), doc_ids.reshape(N_DP, C)))
    attn = low(low_back(attn.reshape(TOKENS, H * HD)))
    branch = low_back(matmul(attn, low(out_weight).T))
    hidden1 = tokens32 + branch
    normed2 = low(rms_norm(hidden1, norm_gains[1]))
    gate = low_back(matmul(normed2, low(gate_up_weight[0])))
    up = low_back(matmul(normed2, low(gate_up_weight[1])))
    hid = low(jax.nn.silu(gate) * up)
    down = low_back(matmul(hid, low(down_weight).T))
    return hidden1 + down

def newton(block):
    ortho = block / (jnp.sqrt(jnp.sum(block * block)) + 1e-07)
    for step in range(NSI):
        gram = matmul(ortho.T, ortho)
        polynomial = NS_B * gram + NS_C * matmul(gram, gram)
        ortho = NS_A * ortho + matmul(ortho, polynomial)
    return ortho

def pack_blocks(qkv_m, out_m, gate_up_m, down_m):
    grouped = qkv_m.reshape(D, N_TENSOR, HT + 2 * KT, HD)

    def side(part, width):
        part = jnp.transpose(part.reshape(D, N_TENSOR, width), (1, 0, 2))
        return jnp.pad(part, ((0, 0), (0, 0), (0, FFB - width)))[:, None]

    def runs(matrix):
        return jnp.transpose(matrix.reshape(D, N_TENSOR, NBF, FFB), (1, 2, 0, 3))
    return jnp.concatenate([side(grouped[:, :, :HT], HT * HD), side(grouped[:, :, HT:HT + KT], KT * HD), side(grouped[:, :, HT + KT:], KT * HD), side(out_m, HT * HD), runs(gate_up_m[0]), runs(gate_up_m[1]), runs(down_m)], axis=1)

def unpack_blocks(ortho):

    def take(index, width):
        return jnp.transpose(ortho[:, index, :, :width], (1, 0, 2))
    qkv_u = jnp.concatenate([take(0, HT * HD).reshape(D, N_TENSOR, HT, HD), take(1, KT * HD).reshape(D, N_TENSOR, KT, HD), take(2, KT * HD).reshape(D, N_TENSOR, KT, HD)], axis=2).reshape(D, N_TENSOR * GW)
    out_u = take(3, HT * HD).reshape(D, H * HD)

    def runs_back(start):
        return jnp.transpose(ortho[:, start:start + NBF], (2, 0, 1, 3)).reshape(D, FF)
    gate_up_u = jnp.stack([runs_back(4), runs_back(4 + NBF)])
    return (qkv_u, out_u, gate_up_u, runs_back(4 + 2 * NBF))

def vector_step(param, moment_new, rate):
    return param - rate * moment_new * lax.rsqrt(lax.optimization_barrier(jnp.mean(moment_new * moment_new, axis=-1, keepdims=True)) + EPS)

def reference(tokens, cotangent, doc_ids, norm_gains, qkv_weight, qkv_bias, out_weight, gate_up_weight, down_weight, gains_moment, qkv_moment, bias_moment, out_moment, gate_up_moment, down_moment):
    positions = jax.vmap(positions_of)(doc_ids.reshape(N_DP, C)).reshape(TOKENS)
    freq = THETA ** (-(2.0 / HD) * jnp.arange(HD // 2, dtype=jnp.float32))
    angle = positions.astype(jnp.float32)[:, None] * freq[None, :]
    cosine = jnp.cos(angle)
    sine = jnp.sin(angle)
    tokens32 = tokens.astype(jnp.float32)

    def apply(x, gains, wqkv, bqkv, wout, wgu, wdown):
        return forward(x, gains, wqkv, bqkv, wout, wgu, wdown, doc_ids, cosine, sine)
    layer_out, pullback = jax.vjp(apply, tokens32, norm_gains, qkv_weight, qkv_bias, out_weight, gate_up_weight, down_weight)
    live = (doc_ids >= 0).astype(jnp.float32)
    grads = pullback(cotangent.astype(jnp.float32) * live[:, None])
    tokens_grad, gains_grad, qkv_grad, bias_grad, out_grad, gate_up_grad, down_grad = grads
    gains_m = MOMENTUM * gains_moment + gains_grad
    qkv_m = MOMENTUM * qkv_moment + qkv_grad
    bias_m = MOMENTUM * bias_moment + bias_grad
    out_m = MOMENTUM * out_moment + out_grad
    gate_up_m = MOMENTUM * gate_up_moment + gate_up_grad
    down_m = MOMENTUM * down_moment + down_grad
    packed = pack_blocks(qkv_m, out_m, gate_up_m, down_m)
    ortho = lax.map(newton, packed.reshape(-1, D, FFB)).reshape(packed.shape)
    qkv_u, out_u, gate_up_u, down_u = unpack_blocks(ortho)
    gains_new = vector_step(norm_gains, gains_m, LR_VECTOR)
    bias_new = vector_step(qkv_bias.reshape(N_TENSOR, GW), bias_m.reshape(N_TENSOR, GW), LR_BIAS).reshape(N_TENSOR * GW)
    return (layer_out, tokens_grad, gains_grad, qkv_grad, bias_grad, out_grad, gate_up_grad, down_grad, gains_new, qkv_weight - LR_MATRIX * qkv_u, bias_new, out_weight - LR_OUT * out_u, gate_up_weight - LR_MATRIX * gate_up_u, down_weight - LR_MATRIX * down_u, gains_m, qkv_m, bias_m, out_m, gate_up_m, down_m)
```

```python
import jax
import jax.numpy as jnp
from jax import lax
from jax.sharding import PartitionSpec as P

HD = 128
FFB = 896
NSI = 5


EPS = 1e-06
THETA = 1000000.0
MOMENTUM = 0.5
LR_MATRIX = 0.2
LR_OUT = 0.8
LR_VECTOR = 0.1
LR_BIAS = 1.0
NS_A = 3.4445
NS_B = -4.775
NS_C = 2.0315
HIGH = lax.Precision.HIGHEST
FLOAT = jnp.float32
BFLOAT = jnp.bfloat16


def contract(left, right, left_dim, right_dim):
    return lax.dot_general(
        left, right, (((left_dim,), (right_dim,)), ((), ())), preferred_element_type=FLOAT
    )


def positions_of(block_ids):
    index = jnp.arange(block_ids.shape[0], dtype=jnp.int32)
    change = jnp.concatenate([jnp.ones((1,), dtype=bool), block_ids[1:] != block_ids[:-1]])
    start = lax.cummax(jnp.where(change, index, jnp.zeros_like(index)), axis=0)
    return index - start


def rotate(values, cosine, sine, direction):
    half = values.shape[-1] // 2
    first = values[..., :half]
    second = values[..., half:]
    cosine = cosine[:, None, :]
    sine = sine[:, None, :] * direction
    return jnp.concatenate(
        [first * cosine - second * sine, second * cosine + first * sine], axis=-1
    )


def rms_scale(values):
    return lax.rsqrt(jnp.mean(values * values, axis=-1, keepdims=True) + EPS)


def norm_back(grad, values, scale, gain):
    scaled = grad * gain
    return scale * scaled - values * scale * scale * scale * jnp.mean(
        scaled * values, axis=-1, keepdims=True
    )


def low_dot(left, right, left_dim):
    return lax.dot_general(
        left.astype(BFLOAT),
        right.astype(BFLOAT),
        (((left_dim,), (0,)), ((), ())),
        preferred_element_type=FLOAT,
    )


def newton(block, group):
    same = (group[:, None] == group[None, :]).astype(FLOAT)
    width = jnp.sum(same, axis=0)
    eye = jnp.eye(same.shape[0], dtype=FLOAT)

    def squares(value):
        return jnp.dot(jnp.sum(value * value, axis=0), same, precision=HIGH)

    ortho = block.astype(FLOAT)
    ortho = ortho / (jnp.sqrt(squares(ortho)) + 1e-07)
    for step in range(NSI):
        shift = squares(ortho) / width
        gram = low_dot(ortho, ortho, 0) * same - eye * shift
        polynomial = (NS_B + 2.0 * NS_C * shift) * gram + NS_C * low_dot(gram, gram, 1)
        ortho = (NS_A + NS_B * shift + NS_C * shift * shift) * ortho + low_dot(
            ortho, polynomial, 1
        )
    return ortho


def vector_step(param, moment_new, rate):
    return param - rate * moment_new * lax.rsqrt(
        jnp.mean(moment_new * moment_new, axis=-1, keepdims=True) + EPS
    )


def bits_of(count):
    return [1 << bit for bit in range(count.bit_length() - 1)]


def swap(value, axis, stride):
    count = lax.axis_size(axis)
    return lax.ppermute(value, axis, [(at, at ^ stride) for at in range(count)])


def total_over(value, axis):
    for stride in bits_of(lax.axis_size(axis)):
        value = jax.tree.map(lambda a: a + swap(a, axis, stride), value)
    return value


def tensor_sum(value):
    value = value.astype(BFLOAT)
    if lax.axis_size("tensor") != 2:
        return lax.psum(value, "tensor").astype(FLOAT)
    return value.astype(FLOAT) + swap(value, "tensor", 1).astype(FLOAT)


def by_distance(value, order):
    count = lax.axis_size("dp")
    me = lax.axis_index("dp")
    bits = len(order)
    value = value.reshape((2,) * bits + (value.shape[0] // count,) + value.shape[1:])
    for at in range(bits):
        mine = (me >> (bits - 1 - at)) & 1
        value = jnp.where(mine == 1, jnp.flip(value, at), value)
    places = [bits - stride.bit_length() for stride in order]
    value = value.transpose(tuple(places) + tuple(range(bits, value.ndim)))
    return value.reshape((-1,) + value.shape[bits + 1 :])


def low_add(one, other):
    return (one.astype(FLOAT) + other.astype(FLOAT)).astype(BFLOAT)


def reduce_rows(left, right, order):
    half = left.shape[0] // 2
    sent = jnp.dot(left[half:], right, preferred_element_type=FLOAT).astype(BFLOAT)
    kept = jnp.dot(left[:half], right, preferred_element_type=FLOAT).astype(BFLOAT)
    for at, stride in enumerate(order):
        came = swap(sent, "dp", stride)
        if at == len(order) - 1:
            return kept.astype(FLOAT) + came.astype(FLOAT)
        half = kept.shape[0] // 2
        sent = low_add(kept[half:], came[half:])
        kept = low_add(kept[:half], came[:half])


def shards(
    tokens,
    cotangent,
    doc_ids,
    norm_gains,
    qkv_weight,
    qkv_bias,
    out_weight,
    gate_up_weight,
    down_weight,
    gains_moment,
    qkv_moment,
    bias_moment,
    out_moment,
    gate_up_moment,
    down_moment,
):
    rows = qkv_weight.shape[0]
    count = tokens.shape[0]
    query_width = out_weight.shape[1]
    heads = query_width // HD
    group_width = qkv_weight.shape[1]
    kv_heads = (group_width - query_width) // (2 * HD)
    share = heads // kv_heads
    kv_width = kv_heads * HD
    scale = HD ** (-0.5)
    devices = lax.axis_size("dp")
    me = lax.axis_index("dp")
    strides = bits_of(devices)
    x_first = tuple(strides)
    z_first = tuple(strides[:1] + strides[2:] + strides[1:2])
    attention_full = lax.all_gather(
        jnp.concatenate([qkv_weight.astype(BFLOAT), out_weight.astype(BFLOAT)], axis=1),
        "dp",
        axis=0,
        tiled=True,
    )
    qkv_full = attention_full[:, :group_width]
    out_full = attention_full[:, group_width:]
    gate_up_full = lax.all_gather(gate_up_weight.astype(BFLOAT), "dp", axis=1, tiled=True)
    down_full = lax.all_gather(down_weight.astype(BFLOAT), "dp", axis=0, tiled=True)
    live = (doc_ids >= 0).astype(FLOAT)
    grad_out = cotangent.astype(FLOAT) * live[:, None]
    grad_low = grad_out.astype(BFLOAT)
    grad_rows = by_distance(grad_low.T, x_first)
    positions = positions_of(doc_ids)
    freq = THETA ** (-(2.0 / HD) * jnp.arange(HD // 2, dtype=FLOAT))
    angle = positions.astype(FLOAT)[:, None] * freq[None, :]
    cosine = jnp.cos(angle)
    sine = jnp.sin(angle)
    index = jnp.arange(count)
    allowed = (doc_ids[:, None] == doc_ids[None, :]) & (index[None, :] <= index[:, None])
    inputs = tokens.astype(FLOAT)
    scale_one = rms_scale(inputs)
    normed = (inputs * scale_one * norm_gains[0]).astype(BFLOAT)
    normed_rows = by_distance(normed.T, z_first)
    qkv = (jnp.dot(normed, qkv_full, preferred_element_type=FLOAT) + qkv_bias).reshape(
        count, heads + 2 * kv_heads, HD
    )
    query = (
        rotate(qkv[:, :heads], cosine, sine, 1.0).astype(BFLOAT).reshape(count, kv_heads, share, HD)
    )
    keys = rotate(qkv[:, heads : heads + kv_heads], cosine, sine, 1.0).astype(BFLOAT)
    values = qkv[:, heads + kv_heads :].astype(BFLOAT)

    def scores_of():
        raw = jnp.einsum("qngd,knd->ngqk", query, keys, preferred_element_type=FLOAT) * scale
        return jnp.where(allowed[None, None], raw, -1e30)

    scores = scores_of()
    top = jnp.max(scores, axis=-1, keepdims=True)
    log_total = top + jnp.log(jnp.sum(jnp.exp(scores - top), axis=-1, keepdims=True))
    probs_low = jnp.exp(scores - log_total).astype(BFLOAT)
    attn = jnp.einsum("ngqk,knd->qngd", probs_low, values, preferred_element_type=FLOAT)
    attn = attn.reshape(count, query_width).astype(BFLOAT)
    branch = tensor_sum(contract(attn, out_full, 1, 1))
    hidden1 = inputs + branch
    scale_two = rms_scale(hidden1)
    normed2 = (hidden1 * scale_two * norm_gains[1]).astype(BFLOAT)
    normed2_rows = by_distance(normed2.T, x_first)
    gate = jnp.dot(normed2, gate_up_full[0], preferred_element_type=FLOAT)
    up = jnp.dot(normed2, gate_up_full[1], preferred_element_type=FLOAT)
    sigma = jax.nn.sigmoid(gate)
    activated = gate * sigma
    hid = (activated * up).astype(BFLOAT)
    down_shard = reduce_rows(grad_rows, hid, x_first)
    dhid = jnp.dot(grad_low, down_full, preferred_element_type=FLOAT)
    dgate = (dhid * up * sigma * (1.0 + gate * (1.0 - sigma))).astype(BFLOAT)
    dup = (dhid * activated).astype(BFLOAT)
    gate_shard = reduce_rows(normed2_rows, dgate, x_first)
    up_shard = reduce_rows(normed2_rows, dup, x_first)
    dnormed2 = contract(dgate, gate_up_full[0], 1, 1) + contract(dup, gate_up_full[1], 1, 1)
    dnormed2 = tensor_sum(dnormed2)
    layer_out = hidden1 + tensor_sum(contract(hid, down_full, 1, 1))
    dhidden1 = grad_out + norm_back(dnormed2, hidden1, scale_two, norm_gains[1])
    gain_two = jnp.sum(dnormed2 * hidden1 * scale_two, axis=0)
    dbranch = dhidden1.astype(BFLOAT)
    out_shard = reduce_rows(by_distance(dbranch.T, z_first), attn, z_first)
    dattn = (
        jnp.dot(dbranch, out_full, preferred_element_type=FLOAT)
        .astype(BFLOAT)
        .reshape(count, kv_heads, share, HD)
    )
    scores = scores_of()
    probs = jnp.exp(scores - log_total)
    probs_low = probs.astype(BFLOAT)
    dprobs = jnp.einsum("qngd,knd->ngqk", dattn, values, preferred_element_type=FLOAT)
    dscores = (probs * (dprobs - jnp.sum(probs * dprobs, axis=-1, keepdims=True))).astype(BFLOAT)
    dquery = jnp.einsum("ngqk,knd->qngd", dscores, keys, preferred_element_type=FLOAT) * scale
    dkeys = jnp.einsum("ngqk,qngd->knd", dscores, query, preferred_element_type=FLOAT) * scale
    dvalues = jnp.einsum("ngqk,qngd->knd", probs_low, dattn, preferred_element_type=FLOAT)
    dquery = rotate(dquery.reshape(count, heads, HD), cosine, sine, -1.0)
    dkeys = rotate(dkeys, cosine, sine, -1.0)
    dqkv = (
        jnp.concatenate([dquery, dkeys, dvalues], axis=1).reshape(count, group_width).astype(BFLOAT)
    )
    bias_term = jnp.sum(dqkv.astype(FLOAT), axis=0)
    qkv_shard = reduce_rows(normed_rows, dqkv, z_first)
    dnormed = tensor_sum(contract(dqkv, qkv_full, 1, 1))
    tokens_grad = dhidden1 + norm_back(dnormed, inputs, scale_one, norm_gains[0])
    gain_one = jnp.sum(dnormed * inputs * scale_one, axis=0)
    vectors = total_over(jnp.concatenate([gain_one, gain_two, bias_term]), "dp")
    gains_grad = vectors[: 2 * inputs.shape[1]].reshape(2, -1)
    bias_grad = vectors[2 * inputs.shape[1] :]
    gate_up_shard = jnp.stack([gate_shard, up_shard])
    gains_m = MOMENTUM * gains_moment + gains_grad
    bias_m = MOMENTUM * bias_moment + bias_grad
    qkv_m = MOMENTUM * qkv_moment + qkv_shard
    out_m = MOMENTUM * out_moment + out_shard
    gate_up_m = MOMENTUM * gate_up_moment + gate_up_shard
    down_m = MOMENTUM * down_moment + down_shard
    units = down_m.shape[1]
    runs = units // FFB

    def runs_of(matrix):
        return matrix.astype(BFLOAT).reshape(rows, runs, FFB).transpose(1, 0, 2)

    def unit_of(one, other):
        both = jnp.concatenate([one, other], axis=1).astype(BFLOAT)
        return jnp.pad(both, ((0, 0), (0, FFB - both.shape[1])))

    value_m = qkv_m[:, query_width + kv_width :]
    packed = jnp.concatenate(
        [
            runs_of(gate_up_m[0]),
            runs_of(gate_up_m[1]),
            runs_of(down_m),
            unit_of(out_m, value_m)[None],
        ]
    )
    total = packed.shape[0]
    per_owner = (total + devices - 1) // devices
    packed = jnp.pad(packed, ((0, per_owner * devices - total), (0, 0), (0, 0)))
    column = jnp.arange(FFB)
    paired = (column >= query_width).astype(jnp.int32) + (column >= query_width + kv_width).astype(jnp.int32)
    solved = []
    for turn in range(per_owner):
        unit = me + turn * devices
        block = lax.all_to_all(
            packed[turn * devices : (turn + 1) * devices], "dp", split_axis=0, concat_axis=0, tiled=True
        )
        group = jnp.where(unit == total - 1, paired, 0)
        ortho = newton(block.reshape(devices * rows, FFB), group)
        solved.append(
            lax.all_to_all(
                ortho.astype(BFLOAT).reshape(devices, rows, FFB), "dp", split_axis=0, concat_axis=0, tiled=True
            )
        )
    returned = jnp.concatenate(solved) if per_owner > 1 else solved[0]
    pair = newton(
        lax.all_gather(
            unit_of(qkv_m[:, :query_width], qkv_m[:, query_width : query_width + kv_width]),
            "dp",
            axis=0,
            tiled=True,
        ),
        paired,
    )
    pair = lax.dynamic_slice_in_dim(pair, me * rows, rows, 0)
    returned = returned.astype(FLOAT)

    def rows_of(first):
        return returned[first : first + runs].transpose(1, 0, 2).reshape(rows, units)

    last = returned[total - 1]
    qkv_update = jnp.concatenate(
        [pair[:, : query_width + kv_width], last[:, query_width : query_width + kv_width]], axis=1
    )
    out_update = last[:, :query_width]
    gate_up_update = jnp.stack([rows_of(0), rows_of(runs)])
    down_update = rows_of(2 * runs)
    gains_new = vector_step(norm_gains, gains_m, LR_VECTOR)
    bias_new = vector_step(qkv_bias, bias_m, LR_BIAS)
    return (
        layer_out,
        tokens_grad,
        gains_grad,
        qkv_shard,
        bias_grad,
        out_shard,
        gate_up_shard,
        down_shard,
        gains_new,
        qkv_weight - LR_MATRIX * qkv_update,
        bias_new,
        out_weight - LR_OUT * out_update,
        gate_up_weight - LR_MATRIX * gate_up_update,
        down_weight - LR_MATRIX * down_update,
        gains_m,
        qkv_m,
        bias_m,
        out_m,
        gate_up_m,
        down_m,
    )


def solution(mesh):
    placed = (
        P("dp", None),
        P("dp", None),
        P("dp"),
        P(),
        P("dp", "tensor"),
        P("tensor"),
        P("dp", "tensor"),
        P(None, "dp", "tensor"),
        P("dp", "tensor"),
        P(),
        P("dp", "tensor"),
        P("tensor"),
        P("dp", "tensor"),
        P(None, "dp", "tensor"),
        P("dp", "tensor"),
    )
    return jax.shard_map(
        shards,
        mesh=mesh,
        in_specs=placed,
        out_specs=(
            P("dp", None),
            P("dp", None),
            P(),
            P("dp", "tensor"),
            P("tensor"),
            P("dp", "tensor"),
            P(None, "dp", "tensor"),
            P("dp", "tensor"),
            P(),
            P("dp", "tensor"),
            P("tensor"),
            P("dp", "tensor"),
            P(None, "dp", "tensor"),
            P("dp", "tensor"),
            P(),
            P("dp", "tensor"),
            P("tensor"),
            P("dp", "tensor"),
            P(None, "dp", "tensor"),
            P("dp", "tensor"),
        ),
        check_vma=False,
    )
```

```python
import functools

import jax
import jax.numpy as jnp
from jax import lax
from jax.experimental import pallas as pl
from jax.experimental.pallas import tpu as pltpu
from jax.sharding import PartitionSpec as P

HD = 128
FFB = 896
NSI = 5


EPS = 1e-06
THETA = 1000000.0
MOMENTUM = 0.5
LR_MATRIX = 0.2
LR_OUT = 0.8
LR_VECTOR = 0.1
LR_BIAS = 1.0
NS_A = 3.4445
NS_B = -4.775
NS_C = 2.0315
FLOAT = jnp.float32
BFLOAT = jnp.bfloat16


def contract(left, right, left_dim, right_dim):
    return lax.dot_general(
        left, right, (((left_dim,), (right_dim,)), ((), ())), preferred_element_type=FLOAT
    )


def positions_of(block_ids):
    index = jnp.arange(block_ids.shape[0], dtype=jnp.int32)
    change = jnp.concatenate([jnp.ones((1,), dtype=bool), block_ids[1:] != block_ids[:-1]])
    start = lax.cummax(jnp.where(change, index, jnp.zeros_like(index)), axis=0)
    return index - start


def rms_scale(values):
    return lax.rsqrt(jnp.mean(values * values, axis=-1, keepdims=True) + EPS)


def norm_back(grad, values, scale, gain):
    scaled = grad * gain
    return scale * scaled - values * scale * scale * scale * jnp.mean(
        scaled * values, axis=-1, keepdims=True
    )


def solve(width, split, depth, wide, tall, tall_low, gram, poly):
    tile = width // 2
    chunk = depth // 3

    def both(sums):
        if split:
            return sums
        total = sums[0] + sums[1]
        return total, total

    def squares(part):
        return jnp.sum(part[:tile] * part[:tile]), jnp.sum(part[tile:] * part[tile:])

    def rows_of(pair, columns):
        if not split:
            return pair[0]
        at = lax.broadcasted_iota(jnp.int32, (width, columns), 0)
        return jnp.where(at < tile, pair[0], pair[1])

    sums = (jnp.float32(0), jnp.float32(0))
    for at in range(3):
        part = wide[at * chunk : (at + 1) * chunk, :width].T
        tall[:width, at * chunk : (at + 1) * chunk] = part
        found = squares(part)
        sums = (sums[0] + found[0], sums[1] + found[1])
    sums = both(sums)
    inverse = tuple(1.0 / (jnp.sqrt(one) + 1e-07) for one in sums)
    factor = rows_of(inverse, chunk)
    for at in range(3):
        part = tall[:width, at * chunk : (at + 1) * chunk] * factor
        tall[:width, at * chunk : (at + 1) * chunk] = part
        tall_low[:width, at * chunk : (at + 1) * chunk] = part.astype(BFLOAT)
    start = tuple(one * by * by for one, by in zip(sums, inverse))

    def step(turn, sums):
        shifts = tuple(one / (tile if split else width) for one in sums)
        for at in range(2):
            mine = slice(at * tile, (at + 1) * tile)
            product = lax.dot_general(
                tall_low[mine, :],
                tall_low[:width, :],
                (((1,), (1,)), ((), ())),
                preferred_element_type=FLOAT,
            )
            row = lax.broadcasted_iota(jnp.int32, (tile, width), 0) + at * tile
            column = lax.broadcasted_iota(jnp.int32, (tile, width), 1)
            product = jnp.where(row == column, product - shifts[at], product)
            if split:
                product = jnp.where((column < tile) == (at == 0), product, 0.0)
            gram[mine, :width] = product.astype(BFLOAT)
        for at in range(2):
            mine = slice(at * tile, (at + 1) * tile)
            product = jnp.dot(
                gram[mine, :width], gram[:width, :width], preferred_element_type=FLOAT
            )
            linear = NS_B + 2.0 * NS_C * shifts[at]
            poly[mine, :width] = (
                linear * gram[mine, :width].astype(FLOAT) + NS_C * product
            ).astype(BFLOAT)
        factor = rows_of(tuple(NS_A + NS_B * s + NS_C * s * s for s in shifts), chunk)
        sums = (jnp.float32(0), jnp.float32(0))
        for at in range(3):
            span = slice(at * chunk, (at + 1) * chunk)
            part = factor * tall[:width, span] + jnp.dot(
                poly[:width, :width], tall_low[:width, span], preferred_element_type=FLOAT
            )
            tall[:width, span] = part
            tall_low[:width, span] = part.astype(BFLOAT)
            found = squares(part)
            sums = (sums[0] + found[0], sums[1] + found[1])
        return both(sums)

    lax.fori_loop(0, NSI, step, start)
    for at in range(3):
        wide[at * chunk : (at + 1) * chunk, :width] = tall[
            :width, at * chunk : (at + 1) * chunk
        ].T


def muon_kernel(
    devices,
    rows,
    blocks,
    query_width,
    keeper,
    units,
    vectors,
    units_new,
    vectors_sum,
    all_vectors,
    first,
    second,
    first_back,
    second_back,
    wide,
    tall,
    tall_low,
    gram,
    poly,
    here_sem,
    go_sem,
    come_sem,
    back_sem,
    home_sem,
    go_vector,
    come_vector,
):
    me = lax.axis_index("dp")
    depth = devices * rows
    mine = jnp.where(me < keeper, me, me - 1)
    keeps = me == keeper
    holds = jnp.logical_and(me != keeper, mine < blocks)
    key_width = FFB - query_width

    def block_of(device):
        return jnp.where(device < keeper, device, device - 1)

    def owner_of(block):
        return jnp.where(block < keeper, block, block + 1)

    def rows_of(array, unit):
        return array.at[:, pl.ds(pl.multiple_of(unit * FFB, 128), FFB)]

    def remote(source, target, send, receive, device):
        return pltpu.make_async_remote_copy(
            src_ref=source,
            dst_ref=target,
            send_sem=send,
            recv_sem=receive,
            device_id={"dp": device},
            device_id_type=pl.DeviceIdType.MESH,
        )

    def others(body):
        def step(turn, carry):
            body(lax.rem(me + turn, devices))
            return carry

        lax.fori_loop(1, devices, step, 0)

    barrier = pltpu.get_barrier_semaphore()

    def greet(device):
        pl.semaphore_signal(
            barrier, inc=1, device_id={"dp": device}, device_id_type=pl.DeviceIdType.MESH
        )

    others(greet)
    pl.semaphore_wait(barrier, devices - 1)

    def way_in(unit, at, sender, device):
        return remote(
            rows_of(units, unit),
            (first, second)[at].at[sender],
            go_sem.at[device, at],
            come_sem.at[sender, at],
            device,
        )

    def to_owner(device, what):
        @pl.when(device == keeper)
        def _():
            what(way_in(blocks, 0, me, device))
            what(way_in(blocks + 1, 1, me, device))

        @pl.when(jnp.logical_and(device != keeper, block_of(device) < blocks))
        def _():
            what(way_in(block_of(device), 0, me, device))

    def share(sender, device):
        return remote(
            vectors, all_vectors.at[sender], go_vector.at[device], come_vector.at[sender], device
        )

    others(lambda device: to_owner(device, lambda copy: copy.start()))
    others(lambda device: share(me, device).start())

    def own_in(what):
        @pl.when(keeps)
        def _():
            what(pltpu.make_async_copy(rows_of(units, blocks), first.at[me], here_sem.at[0]))
            what(pltpu.make_async_copy(rows_of(units, blocks + 1), second.at[me], here_sem.at[1]))

        @pl.when(holds)
        def _():
            what(pltpu.make_async_copy(rows_of(units, mine), first.at[me], here_sem.at[0]))

    own_in(lambda copy: copy.start())
    own_in(lambda copy: copy.wait())

    def arrived(device):
        @pl.when(jnp.logical_or(keeps, holds))
        def _():
            way_in(0, 0, device, me).wait_recv()

        @pl.when(keeps)
        def _():
            way_in(0, 1, device, me).wait_recv()

    others(arrived)

    def load(buffer, source_at, size, target_at):
        def step(at, carry):
            wide[pl.ds(pl.multiple_of(at * rows, 8), rows), target_at : target_at + size] = buffer[
                at, :, source_at : source_at + size
            ].astype(FLOAT)
            return carry

        lax.fori_loop(0, devices, step, 0)

    def store(buffer, source_at, size, target_at):
        def step(at, carry):
            buffer[at, :, target_at : target_at + size] = wide[
                pl.ds(pl.multiple_of(at * rows, 8), rows), source_at : source_at + size
            ].astype(buffer.dtype)
            return carry

        lax.fori_loop(0, devices, step, 0)

    def way_back(unit, at, device):
        return remote(
            (first_back, second_back)[at].at[device],
            rows_of(units_new, unit),
            back_sem.at[device, at],
            home_sem.at[unit],
            device,
        )

    def own_back(unit, at):
        return pltpu.make_async_copy(
            (first_back, second_back)[at].at[me], rows_of(units_new, unit), here_sem.at[at]
        )

    @pl.when(holds)
    def _():
        load(first, 0, FFB, 0)
        solve(FFB, False, depth, wide, tall, tall_low, gram, poly)
        store(first_back, 0, FFB, 0)
        others(lambda device: way_back(mine, 0, device).start())
        own_back(mine, 0).start()
        own_back(mine, 0).wait()

    @pl.when(keeps)
    def _():
        load(first, query_width, key_width, 0)
        load(second, query_width, key_width, key_width)
        solve(2 * key_width, True, depth, wide, tall, tall_low, gram, poly)
        store(first_back, 0, key_width, query_width)
        store(second_back, key_width, key_width, query_width)
        for at, buffer, back in ((0, first, first_back), (1, second, second_back)):
            load(buffer, 0, query_width, 0)
            solve(query_width, False, depth, wide, tall, tall_low, gram, poly)
            store(back, 0, query_width, 0)
            others(lambda device: way_back(blocks + at, at, device).start())
            own_back(blocks + at, at).start()
        own_back(blocks, 0).wait()
        own_back(blocks + 1, 1).wait()

    own_vectors = pltpu.make_async_copy(vectors, all_vectors.at[me], here_sem.at[2])
    own_vectors.start()
    own_vectors.wait()
    others(lambda device: share(device, me).wait_recv())
    vectors_sum[...] = lax.fori_loop(
        1, devices, lambda at, total: total + all_vectors[at], all_vectors[0]
    )
    others(lambda device: share(me, device).wait_send())

    def home(block, carry):
        @pl.when(owner_of(block) != me)
        def _():
            way_back(block, 0, me).wait_recv()

        return carry

    lax.fori_loop(0, blocks, home, 0)

    @pl.when(jnp.logical_not(keeps))
    def _():
        way_back(blocks, 0, me).wait_recv()
        way_back(blocks + 1, 1, me).wait_recv()

    others(lambda device: to_owner(device, lambda copy: copy.wait_send()))

    @pl.when(jnp.logical_or(keeps, holds))
    def _():
        others(lambda device: way_back(0, 0, device).wait_send())

    @pl.when(keeps)
    def _():
        others(lambda device: way_back(0, 1, device).wait_send())


def orthogonalize(units, vectors, query_width, devices):
    rows = units.shape[0]
    blocks = units.shape[1] // FFB - 2
    depth = devices * rows
    wire = units.dtype
    kernel = functools.partial(
        muon_kernel, devices, rows, blocks, query_width, min(devices // 2, blocks)
    )
    hbm = pl.BlockSpec(memory_space=pltpu.HBM)
    return pl.pallas_call(
        kernel,
        out_shape=[
            jax.ShapeDtypeStruct(units.shape, wire),
            jax.ShapeDtypeStruct(vectors.shape, FLOAT),
        ],
        in_specs=[hbm, pl.BlockSpec(memory_space=pltpu.VMEM)],
        out_specs=[hbm, pl.BlockSpec(memory_space=pltpu.VMEM)],
        scratch_shapes=[
            pltpu.VMEM((devices,) + vectors.shape, FLOAT),
            pltpu.VMEM((devices, rows, FFB), wire),
            pltpu.VMEM((devices, rows, FFB), wire),
            pltpu.VMEM((devices, rows, FFB), wire),
            pltpu.VMEM((devices, rows, FFB), wire),
            pltpu.VMEM((depth, FFB), FLOAT),
            pltpu.VMEM((FFB, depth), FLOAT),
            pltpu.VMEM((FFB, depth), BFLOAT),
            pltpu.VMEM((FFB, FFB), BFLOAT),
            pltpu.VMEM((FFB, FFB), BFLOAT),
            pltpu.SemaphoreType.DMA((3,)),
            pltpu.SemaphoreType.DMA((devices, 2)),
            pltpu.SemaphoreType.DMA((devices, 2)),
            pltpu.SemaphoreType.DMA((devices, 2)),
            pltpu.SemaphoreType.DMA((blocks + 2,)),
            pltpu.SemaphoreType.DMA((devices,)),
            pltpu.SemaphoreType.DMA((devices,)),
        ],
        compiler_params=pltpu.CompilerParams(
            collective_id=0, has_side_effects=True, vmem_limit_bytes=52 * 2**20
        ),
        cost_estimate=pl.CostEstimate(
            flops=64 * 10**9, bytes_accessed=16 * 2**20, transcendentals=0
        ),
    )(units, vectors)


LIGHT = pl.CostEstimate(flops=1024, bytes_accessed=1024, transcendentals=0)


def call_light(body, grid, ins, outs):
    return pl.pallas_call(
        body,
        grid=grid,
        in_specs=[pl.BlockSpec(block, at) for _, block, at in ins],
        out_specs=[pl.BlockSpec(block, at) for _, _, block, at in outs],
        out_shape=[jax.ShapeDtypeStruct(shape, dtype) for shape, dtype, _, _ in outs],
        compiler_params=pltpu.CompilerParams(vmem_limit_bytes=56 * 2**20),
        cost_estimate=LIGHT,
    )(*[array for array, _, _ in ins])


def spans(size, step):
    return [slice(at, min(at + step, size)) for at in range(0, size, step)]


def hidden_units(tokens, grads, weights, block=256):
    count, depth = tokens.shape
    part = weights.shape[1] // 3

    def body(x, y, w_gate, w_up, gate, up, hid, turned_x, turned_y):
        turned_x[...] = x[...].astype(FLOAT).T.astype(BFLOAT)
        turned_y[...] = y[...].astype(FLOAT).T.astype(BFLOAT)
        for span in spans(part, 512):
            g = jnp.dot(x[...], w_gate[:, span], preferred_element_type=FLOAT)
            u = jnp.dot(x[...], w_up[:, span], preferred_element_type=FLOAT)
            gate[:, span] = g
            up[:, span] = u
            hid[:, span] = (g * jax.nn.sigmoid(g) * u).astype(BFLOAT)

    rows = lambda at: (at, 0)
    columns = lambda at: (0, at)
    return call_light(
        body,
        (count // block,),
        [
            (tokens, (block, depth), rows),
            (grads, (block, depth), rows),
            (weights, (depth, part), lambda at: (0, 0)),
            (weights, (depth, part), lambda at: (0, 1)),
        ],
        [
            ((count, part), FLOAT, (block, part), rows),
            ((count, part), FLOAT, (block, part), rows),
            ((count, part), BFLOAT, (block, part), rows),
            ((depth, count), BFLOAT, (depth, block), columns),
            ((depth, count), BFLOAT, (depth, block), columns),
        ],
    )


def hidden_back(grads, weights, gate, up, block=256):
    count, depth = grads.shape
    part = weights.shape[1] // 3

    def body(x, w, gate, up, both):
        for span in spans(part, 512):
            dhid = jnp.dot(x[...], w[:, span], preferred_element_type=FLOAT)
            g = gate[:, span]
            sigma = jax.nn.sigmoid(g)
            both[:, span] = (dhid * up[:, span] * sigma * (1.0 + g * (1.0 - sigma))).astype(BFLOAT)
            both[:, part + span.start : part + span.stop] = (dhid * (g * sigma)).astype(BFLOAT)

    rows = lambda at: (at, 0)
    return call_light(
        body,
        (count // block,),
        [
            (grads, (block, depth), rows),
            (weights, (depth, part), lambda at: (0, 2)),
            (gate, (block, part), rows),
            (up, (block, part), rows),
        ],
        [((count, 2 * part), BFLOAT, (block, 2 * part), rows)],
    )[0]


def rows_by_width(units, weights, places, first, last, block=256):
    width = weights.shape[0]
    part = weights.shape[1] // 3

    def body(x, *refs):
        out = refs[-1]
        for span in spans(width, 512):
            out[:, span] = sum(
                lax.dot_general(
                    x[:, at * part : (at + 1) * part],
                    refs[at][span, :],
                    (((1,), (1,)), ((), ())),
                    preferred_element_type=FLOAT,
                )
                for at in range(len(places))
            ).astype(BFLOAT)

    def column(place):
        return (weights, (width, part), lambda at: (0, place))

    return call_light(
        body,
        ((last - first) // block,),
        [(units, (block, len(places) * part), lambda at: (at + first // block, 0))]
        + [column(place) for place in places],
        [((last - first, width), BFLOAT, (block, width), lambda at: (at, 0))],
    )[0]


def weight_term(left, right, blocks, place, width):
    count = left.shape[1]
    picked = blocks.shape[0]
    tall = left.shape[0] // (2 * picked)

    def body(blocks, x, y, out):
        for span in spans(width, 512):
            out[:, span] = jnp.dot(
                x[...], y[:, span], preferred_element_type=FLOAT
            ).astype(BFLOAT)

    return pl.pallas_call(
        body,
        grid_spec=pltpu.PrefetchScalarGridSpec(
            num_scalar_prefetch=1,
            grid=(picked,),
            in_specs=[
                pl.BlockSpec((tall, count), lambda at, blocks: (blocks[at], 0)),
                pl.BlockSpec((count, width), lambda at, blocks: (0, place)),
            ],
            out_specs=pl.BlockSpec((tall, width), lambda at, blocks: (at, 0)),
        ),
        out_shape=jax.ShapeDtypeStruct((picked * tall, width), BFLOAT),
        compiler_params=pltpu.CompilerParams(vmem_limit_bytes=48 * 2**20),
        cost_estimate=LIGHT,
    )(blocks, left, right)


def turned(value, cosine, sine):
    return value * cosine + pltpu.roll(value, HD // 2, 1) * sine


def softmax_of(query, keys, ids, key_ids, first):
    scores = lax.dot_general(
        query, keys, (((1,), (1,)), ((), ())), preferred_element_type=FLOAT
    ) * (HD ** (-0.5))
    row = lax.broadcasted_iota(jnp.int32, scores.shape, 0) + first
    column = lax.broadcasted_iota(jnp.int32, scores.shape, 1)
    scores = jnp.where((ids == key_ids) & (column <= row), scores, -1e30)
    expo = jnp.exp(scores - jnp.max(scores, axis=-1, keepdims=True))
    return expo / jnp.sum(expo, axis=-1, keepdims=True)


def attend(qkv, cosine, sine, doc_ids, heads, kv_heads):
    count = qkv.shape[0]
    share = heads // kv_heads
    half = count // 2

    def body(q, k, v, cosine, sine, ids, key_ids, attn, query, keys, values):
        query[...] = turned(q[...], cosine[...], sine[...]).astype(BFLOAT)
        keys[...] = turned(k[...], cosine[...], sine[...]).astype(BFLOAT)
        values[...] = v[...].astype(BFLOAT)
        for first in (0, half):
            last = first + half
            probs = softmax_of(
                query[first:last, :], keys[:last, :], ids[first:last, :], key_ids[:, :last], first
            )
            attn[first:last, :] = jnp.dot(
                probs.astype(BFLOAT), values[:last, :], preferred_element_type=FLOAT
            ).astype(BFLOAT)

    one = lambda at: (0, 0)
    head = lambda at: (0, at)
    group = lambda at: (0, at // share)
    block = (count, HD)
    return pl.pallas_call(
        body,
        grid=(heads,),
        in_specs=[
            pl.BlockSpec(block, head),
            pl.BlockSpec(block, lambda at: (0, heads + at // share)),
            pl.BlockSpec(block, lambda at: (0, heads + kv_heads + at // share)),
            pl.BlockSpec(block, one),
            pl.BlockSpec(block, one),
            pl.BlockSpec((count, 1), one),
            pl.BlockSpec((1, count), one),
        ],
        out_specs=[
            pl.BlockSpec(block, head),
            pl.BlockSpec(block, head),
            pl.BlockSpec(block, group),
            pl.BlockSpec(block, group),
        ],
        out_shape=[
            jax.ShapeDtypeStruct((count, heads * HD), BFLOAT),
            jax.ShapeDtypeStruct((count, heads * HD), BFLOAT),
            jax.ShapeDtypeStruct((count, kv_heads * HD), BFLOAT),
            jax.ShapeDtypeStruct((count, kv_heads * HD), BFLOAT),
        ],
        compiler_params=pltpu.CompilerParams(vmem_limit_bytes=32 * 2**20),
        cost_estimate=LIGHT,
    )(qkv, qkv, qkv, cosine, sine, doc_ids[:, None], doc_ids[None, :])


def forward_kernel(
    devices,
    heads,
    kv_heads,
    tokens,
    gains,
    bias,
    cosine,
    sine,
    ids,
    key_ids,
    shard,
    units,
    grads,
    normed,
    hidden,
    attn,
    query,
    keys,
    values,
    attention_out,
    ffn_full,
    tokens_all,
    grads_all,
    attention_full,
    qkv,
    branch,
    branch_came,
    normed_two,
    here_sem,
    z_send,
    z_come,
    x_send,
    x_come,
    core_send,
    core_come,
    group_send,
    group_come,
    right_send,
    left_send,
    plane_come,
    pair_send,
    pair_come,
):
    me = lax.axis_index("dp")
    side = lax.axis_index("tensor")
    planes = devices // 4
    rows = shard.shape[0]
    count = tokens.shape[0]
    place, plane = lax.rem(me, 4), me // 4
    across = me + 2 - 4 * (place // 2)
    beside = me + 1 - 2 * lax.rem(me, 2)
    part = ffn_full.shape[1] // 3
    share = heads // kv_heads
    depth = tokens.shape[1]
    half = count // 2

    def remote(source, target, send, come, device):
        return pltpu.make_async_remote_copy(
            src_ref=source,
            dst_ref=target,
            send_sem=send,
            recv_sem=come,
            device_id={"dp": device},
            device_id_type=pl.DeviceIdType.MESH,
        )

    def loop(first, last, body):
        def step(turn, carry):
            body(turn)
            return carry

        lax.fori_loop(first, last, step, 0)

    barrier = pltpu.get_barrier_semaphore()

    def greet(where):
        pl.semaphore_signal(barrier, inc=1, device_id=where, device_id_type=pl.DeviceIdType.MESH)

    def peer(turn):
        return lax.rem(plane + turn, planes) * 4 + place

    def plane_peer(turn):
        return plane * 4 + lax.rem(place + turn, 4)

    loop(1, planes, lambda turn: greet({"dp": peer(turn)}))
    loop(1, 4, lambda turn: greet({"dp": plane_peer(turn)}))
    greet({"tensor": 1 - side})
    pl.semaphore_wait(barrier, planes + 3)

    def block(owner):
        return attention_full.at[pl.ds(pl.multiple_of(owner * rows, 16), rows)]

    def owner_at(turn):
        return lax.rem(plane + planes - turn, planes) * 4

    def to_column(turn):
        return remote(shard, block(me), z_send.at[turn], z_come.at[turn], peer(turn))

    def from_column(turn):
        owner = owner_at(turn) + place
        return remote(block(owner), block(owner), z_send.at[turn], z_come.at[turn], me)

    def x_copy(turn):
        owner = owner_at(turn) + place
        return remote(block(owner), block(owner), x_send.at[turn], x_come.at[turn], across)

    def x_wait(turn):
        owner = owner_at(turn) + lax.rem(across, 4)
        return remote(block(owner), block(owner), x_send.at[turn], x_come.at[turn], across)

    def core_copy(turn, far):
        owner = owner_at(turn) + (lax.rem(across, 4) if far else place)
        return remote(
            block(owner), block(owner), core_send.at[turn, far], core_come.at[turn, far], beside
        )

    def core_wait(turn, far):
        owner = owner_at(turn) + lax.rem(beside, 4) + (2 - 4 * (place // 2) if far else 0)
        return remote(
            block(owner), block(owner), core_send.at[turn, far], core_come.at[turn, far], beside
        )

    def unit_rows(owner):
        return ffn_full.at[pl.ds(pl.multiple_of(owner * rows, 16), rows)]

    def group_copy(turn):
        return remote(
            units.at[lax.rem(place + turn, 4)],
            unit_rows(me),
            group_send.at[turn],
            group_come.at[turn],
            plane_peer(turn),
        )

    def group_wait(turn):
        owner = plane * 4 + lax.rem(place + 4 - turn, 4)
        return remote(
            units.at[0], unit_rows(owner), group_send.at[turn], group_come.at[turn], me
        )

    def slab(origin, third):
        return ffn_full.at[
            pl.ds(pl.multiple_of(origin * 4 * rows, 16), 4 * rows), third * part : (third + 1) * part
        ]

    def move(origin, third, right):
        send = right_send if right else left_send
        return remote(
            slab(origin, third),
            slab(origin, third),
            send.at[origin, third],
            plane_come.at[origin, third],
            me + 4 if right else me - 4,
        )

    def pump(hop, third):
        behind, ahead = plane - hop, plane + hop

        @pl.when(behind >= 0)
        def _():
            move(behind, third, True).wait_recv()

            @pl.when(plane < planes - 1)
            def _():
                move(behind, third, True).start()

        @pl.when(ahead < planes)
        def _():
            move(ahead, third, False).wait_recv()

            @pl.when(plane > 0)
            def _():
                move(ahead, third, False).start()

    def x_rows(array, at):
        return remote(
            array.at[0:count], array.at[count : 2 * count], pair_send.at[at], pair_come.at[at], across
        )

    def core_rows(array, at):
        return remote(
            array.at[0 : 2 * count],
            array.at[2 * count : 4 * count],
            pair_send.at[at],
            pair_come.at[at],
            beside,
        )

    loop(1, planes, lambda turn: to_column(turn).start())
    own_block = pltpu.make_async_copy(shard, block(me), here_sem.at[0])
    own_block.start()
    loop(1, 4, lambda turn: group_copy(turn).start())
    own_units = pltpu.make_async_copy(units.at[place], unit_rows(me), here_sem.at[1])
    own_units.start()
    own_grads = pltpu.make_async_copy(grads, grads_all.at[0:count], here_sem.at[2])
    own_grads.start()

    def norm(value, gain):
        scale = lax.rsqrt(jnp.mean(value * value, axis=-1, keepdims=True) + EPS)
        return (value * scale * gain).astype(BFLOAT)

    for first in range(0, count, 128):
        normed[first : first + 128, :] = norm(
            tokens[first : first + 128, :].astype(FLOAT), gains[0:1, :]
        )

    own_block.wait()
    x_copy(0).start()
    core_copy(0, 0).start()

    def forward(turn):
        from_column(turn).wait_recv()
        x_copy(turn).start()
        core_copy(turn, 0).start()

    loop(1, planes, forward)
    own_units.wait()
    loop(1, 4, lambda turn: group_wait(turn).wait_recv())
    for third in range(3):

        @pl.when(plane < planes - 1)
        def _():
            move(plane, third, True).start()

        @pl.when(plane > 0)
        def _():
            move(plane, third, False).start()

    own_grads.wait()
    x_rows(grads_all, 0).start()

    def forward_far(turn):
        x_wait(turn).wait_recv()
        core_copy(turn, 1).start()

    loop(0, planes, forward_far)
    pump(1, 0)

    def arrive(turn):
        core_wait(turn, 0).wait_recv()
        core_wait(turn, 1).wait_recv()

    loop(0, planes, arrive)
    attention_copy = pltpu.make_async_copy(attention_full, attention_out, here_sem.at[0])
    attention_copy.start()

    query_width = heads * HD
    group_width = qkv.shape[1]
    for first in range(0, group_width, 256):
        qkv[:, first : first + 256] = (
            jnp.dot(
                normed[...], attention_full[:, first : first + 256], preferred_element_type=FLOAT
            )
            + bias[:, first : first + 256]
        )

    def columns(at):
        return pl.ds(pl.multiple_of(at * HD, HD), HD)

    def key_head(at):
        keys[:, columns(at)] = turned(
            qkv[:, columns(heads + at)], cosine[...], sine[...]
        ).astype(BFLOAT)
        values[:, columns(at)] = qkv[:, columns(heads + kv_heads + at)].astype(BFLOAT)

    loop(0, kv_heads, key_head)

    def head(at):
        query[:, columns(at)] = turned(qkv[:, columns(at)], cosine[...], sine[...]).astype(BFLOAT)
        group = columns(at // share)
        for first in (0, half):
            last = first + half
            probs = softmax_of(
                query[first:last, columns(at)],
                keys[:last, group],
                ids[first:last, :],
                key_ids[:, :last],
                first,
            )
            attn[first:last, columns(at)] = jnp.dot(
                probs.astype(BFLOAT), values[:last, group], preferred_element_type=FLOAT
            ).astype(BFLOAT)

    loop(0, heads, head)
    for first in range(0, depth, 256):
        branch[:, first : first + 256] = lax.dot_general(
            attn[...],
            attention_full[first : first + 256, group_width:],
            (((1,), (1,)), ((), ())),
            preferred_element_type=FLOAT,
        ).astype(BFLOAT)
    sum_copy = pltpu.make_async_remote_copy(
        src_ref=branch,
        dst_ref=branch_came,
        send_sem=here_sem.at[3],
        recv_sem=here_sem.at[4],
        device_id={"tensor": 1 - side},
        device_id_type=pl.DeviceIdType.MESH,
    )
    sum_copy.start()
    pump(1, 1)
    pump(1, 2)
    x_rows(grads_all, 0).wait()
    core_rows(grads_all, 1).start()
    pump(2, 0)
    sum_copy.wait()
    for first in range(0, count, 128):
        span = slice(first, first + 128)
        value = tokens[span, :].astype(FLOAT) + (
            branch[span, :].astype(FLOAT) + branch_came[span, :].astype(FLOAT)
        )
        hidden[span, :] = value
        normed_two[span, :] = norm(value, gains[1:2, :])
    own_tokens = pltpu.make_async_copy(normed_two, tokens_all.at[0:count], here_sem.at[1])
    own_tokens.start()
    own_tokens.wait()
    x_rows(tokens_all, 2).start()
    pump(2, 1)
    pump(2, 2)
    x_rows(tokens_all, 2).wait()
    core_rows(tokens_all, 3).start()
    for hop in range(3, planes):
        for third in range(3):
            pump(hop, third)
    core_rows(grads_all, 1).wait()
    core_rows(tokens_all, 3).wait()
    attention_copy.wait()

    loop(1, planes, lambda turn: to_column(turn).wait_send())

    def sent(turn):
        x_copy(turn).wait_send()
        core_copy(turn, 0).wait_send()
        core_copy(turn, 1).wait_send()

    loop(0, planes, sent)
    loop(1, 4, lambda turn: group_copy(turn).wait_send())
    for third in range(3):

        @pl.when(plane < planes - 1)
        def _():
            loop(0, plane + 1, lambda origin: move(origin, third, True).wait_send())

        @pl.when(plane > 0)
        def _():
            loop(plane, planes, lambda origin: move(origin, third, False).wait_send())


def forward_part(
    tokens, gains, bias, cosine, sine, doc_ids, shard, units, grads, devices, heads, kv_heads
):
    count, depth = tokens.shape
    rows, width = shard.shape
    planes = devices // 4
    group_width = bias.shape[0]
    query_width = heads * HD
    hbm = pl.BlockSpec(memory_space=pltpu.HBM)
    vmem = pl.BlockSpec(memory_space=pltpu.VMEM)
    dma = pltpu.SemaphoreType.DMA
    return pl.pallas_call(
        functools.partial(forward_kernel, devices, heads, kv_heads),
        out_shape=[
            jax.ShapeDtypeStruct((count, depth), BFLOAT),
            jax.ShapeDtypeStruct((count, depth), FLOAT),
            jax.ShapeDtypeStruct((count, query_width), BFLOAT),
            jax.ShapeDtypeStruct((count, query_width), BFLOAT),
            jax.ShapeDtypeStruct((count, kv_heads * HD), BFLOAT),
            jax.ShapeDtypeStruct((count, kv_heads * HD), BFLOAT),
            jax.ShapeDtypeStruct((devices * rows, width), BFLOAT),
            jax.ShapeDtypeStruct((devices * rows, units.shape[2]), BFLOAT),
            jax.ShapeDtypeStruct((4 * count, depth), BFLOAT),
            jax.ShapeDtypeStruct((4 * count, depth), BFLOAT),
        ],
        in_specs=[vmem] * 7 + [hbm] * 3,
        out_specs=[vmem] * 6 + [hbm] * 4,
        scratch_shapes=[
            pltpu.VMEM((devices * rows, width), BFLOAT),
            pltpu.VMEM((count, group_width), FLOAT),
            pltpu.VMEM((count, depth), BFLOAT),
            pltpu.VMEM((count, depth), BFLOAT),
            pltpu.VMEM((count, depth), BFLOAT),
            dma((5,)),
            dma((planes,)),
            dma((planes,)),
            dma((planes,)),
            dma((planes,)),
            dma((planes, 2)),
            dma((planes, 2)),
            dma((4,)),
            dma((4,)),
            dma((planes, 3)),
            dma((planes, 3)),
            dma((planes, 3)),
            dma((4,)),
            dma((4,)),
        ],
        compiler_params=pltpu.CompilerParams(
            collective_id=1, has_side_effects=True, vmem_limit_bytes=48 * 2**20
        ),
        cost_estimate=LIGHT,
    )(
        tokens,
        gains,
        bias[None, :],
        cosine,
        sine,
        doc_ids[:, None],
        doc_ids[None, :],
        shard,
        units,
        grads,
    )


def backward_part(
    back,
    came,
    hidden,
    cotangent,
    live,
    gain,
    weights,
    normed,
    attn,
    query,
    keys,
    values,
    cosine,
    sine,
    doc_ids,
    devices,
    order,
):
    count, depth = hidden.shape
    rows = depth // devices
    heads, kv_heads = query.shape[1] // HD, keys.shape[1] // HD
    share = heads // kv_heads
    query_width = heads * HD
    group_width = (heads + 2 * kv_heads) * HD
    width = weights.shape[1]
    half = count // 2
    scale = HD ** (-0.5)

    def body(
        back,
        came,
        hidden,
        cotangent,
        live,
        gain,
        weights,
        normed,
        attn,
        query,
        keys,
        values,
        cosine,
        sine,
        ids,
        key_ids,
        dhidden,
        gain_term,
        bias_term,
        dnormed,
        near,
        far,
        dbranch,
        dattn,
        dqkv,
        dkeys,
        dvalues,
        term,
    ):
        total = jnp.zeros((1, depth), FLOAT)
        for first in range(0, count, 128):
            span = slice(first, first + 128)
            grad = back[span, :].astype(FLOAT) + came[span, :].astype(FLOAT)
            value = hidden[span, :]
            root = lax.rsqrt(jnp.mean(value * value, axis=-1, keepdims=True) + EPS)
            scaled = grad * gain[...]
            result = cotangent[span, :].astype(FLOAT) * live[span, :] + (
                root * scaled
                - value * root * root * root * jnp.mean(scaled * value, axis=-1, keepdims=True)
            )
            dhidden[span, :] = result
            dbranch[span, :] = result.astype(BFLOAT)
            total = total + jnp.sum(grad * value * root, axis=0, keepdims=True)
        gain_term[...] = total
        for first in range(0, query_width, 256):
            dattn[:, first : first + 256] = jnp.dot(
                dbranch[...],
                weights[:, group_width + first : group_width + first + 256],
                preferred_element_type=FLOAT,
            ).astype(BFLOAT)

        def columns(at):
            return pl.ds(pl.multiple_of(at * HD, HD), HD)

        def one_head(at, carry):
            group = at // share

            @pl.when(lax.rem(at, share) == 0)
            def _():
                dkeys[...] = jnp.zeros_like(dkeys)
                dvalues[...] = jnp.zeros_like(dvalues)

            for first in (0, half):
                last = first + half
                rows_here = slice(first, last)
                probs = softmax_of(
                    query[rows_here, columns(at)],
                    keys[:last, columns(group)],
                    ids[rows_here, :],
                    key_ids[:, :last],
                    first,
                )
                dprobs = lax.dot_general(
                    dattn[rows_here, columns(at)],
                    values[:last, columns(group)],
                    (((1,), (1,)), ((), ())),
                    preferred_element_type=FLOAT,
                )
                dscores = (
                    probs * (dprobs - jnp.sum(probs * dprobs, axis=-1, keepdims=True))
                ).astype(BFLOAT)
                dquery = scale * jnp.dot(
                    dscores, keys[:last, columns(group)], preferred_element_type=FLOAT
                )
                dqkv[rows_here, columns(at)] = turned(
                    dquery, cosine[rows_here, :], -sine[rows_here, :]
                ).astype(BFLOAT)
                dkeys[:last, :] += lax.dot_general(
                    dscores,
                    query[rows_here, columns(at)],
                    (((0,), (0,)), ((), ())),
                    preferred_element_type=FLOAT,
                )
                dvalues[:last, :] += lax.dot_general(
                    probs.astype(BFLOAT),
                    dattn[rows_here, columns(at)],
                    (((0,), (0,)), ((), ())),
                    preferred_element_type=FLOAT,
                )

            @pl.when(lax.rem(at, share) == share - 1)
            def _():
                dqkv[:, columns(heads + group)] = turned(
                    dkeys[...] * scale, cosine[...], -sine[...]
                ).astype(BFLOAT)
                dqkv[:, columns(heads + kv_heads + group)] = dvalues[...].astype(BFLOAT)

            return carry

        lax.fori_loop(0, heads, one_head, 0)
        bias_term[...] = jnp.sum(dqkv[...].astype(FLOAT), axis=0, keepdims=True)
        for first in range(0, depth, 256):
            span = slice(first, first + 256)
            dnormed[:, span] = lax.dot_general(
                dqkv[...],
                weights[span, :group_width],
                (((1,), (1,)), ((), ())),
                preferred_element_type=FLOAT,
            ).astype(BFLOAT)
            term[span, :group_width] = lax.dot_general(
                normed[:, span], dqkv[...], (((0,), (0,)), ((), ())), preferred_element_type=FLOAT
            )
            term[span, group_width:] = lax.dot_general(
                dbranch[:, span], attn[...], (((0,), (0,)), ((), ())), preferred_element_type=FLOAT
            )
        me = lax.axis_index("dp")
        for place in range(devices):
            block = 0
            for at, stride in enumerate(order):
                bit = (place >> (len(order) - 1 - at)) & 1
                block = block + lax.rem(me // stride + bit, 2) * stride
            target = near if place < devices // 2 else far
            target[place % (devices // 2)] = term[
                pl.ds(pl.multiple_of(block * rows, 8), rows), :
            ].astype(BFLOAT)

    vmem = pl.BlockSpec(memory_space=pltpu.VMEM)
    outs = pl.pallas_call(
        body,
        out_shape=[
            jax.ShapeDtypeStruct((count, depth), FLOAT),
            jax.ShapeDtypeStruct((1, depth), FLOAT),
            jax.ShapeDtypeStruct((1, group_width), FLOAT),
            jax.ShapeDtypeStruct((count, depth), BFLOAT),
            jax.ShapeDtypeStruct((devices // 2, rows, width), BFLOAT),
            jax.ShapeDtypeStruct((devices // 2, rows, width), BFLOAT),
        ],
        in_specs=[vmem] * 16,
        out_specs=[vmem] * 6,
        scratch_shapes=[
            pltpu.VMEM((count, depth), BFLOAT),
            pltpu.VMEM((count, query_width), BFLOAT),
            pltpu.VMEM((count, group_width), BFLOAT),
            pltpu.VMEM((count, HD), FLOAT),
            pltpu.VMEM((count, HD), FLOAT),
            pltpu.VMEM((depth, width), FLOAT),
        ],
        compiler_params=pltpu.CompilerParams(vmem_limit_bytes=56 * 2**20),
        cost_estimate=LIGHT,
    )(
        back,
        came,
        hidden,
        cotangent,
        live,
        gain,
        weights,
        normed,
        attn,
        query,
        keys,
        values,
        cosine,
        sine,
        doc_ids[:, None],
        doc_ids[None, :],
    )
    dhidden, gain_term, bias_term, dnormed, near, far = outs
    return (
        dhidden,
        gain_term[0],
        bias_term[0],
        dnormed,
        near.reshape(-1, width),
        far.reshape(-1, width),
    )


def vector_step(param, moment_new, rate):
    return param - rate * moment_new * lax.rsqrt(
        jnp.mean(moment_new * moment_new, axis=-1, keepdims=True) + EPS
    )


def bits_of(count):
    return [1 << bit for bit in range(count.bit_length() - 1)]


def swap(value, axis, stride):
    count = lax.axis_size(axis)
    return lax.ppermute(value, axis, [(at, at ^ stride) for at in range(count)])


def low_add(one, other):
    return (one.astype(FLOAT) + other.astype(FLOAT)).astype(BFLOAT)


def after(value, *others):
    return lax.optimization_barrier((value,) + others)[0]


def by_distance(value, order):
    me = lax.axis_index("dp")
    down = sorted(order, reverse=True)
    bits = len(order)
    value = value.reshape((2,) * bits + (value.shape[0] >> bits,) + value.shape[1:])
    for at, stride in enumerate(down):
        value = jnp.where((me // stride) % 2 == 1, jnp.flip(value, at), value)
    places = [down.index(stride) for stride in order]
    value = value.transpose(tuple(places) + tuple(range(bits, value.ndim)))
    return value.reshape((-1,) + value.shape[bits + 1 :])


def by_index(value, order):
    me = lax.axis_index("dp")
    down = sorted(order, reverse=True)
    bits = len(order)
    value = value.reshape((2,) * bits + (value.shape[0] >> bits,) + value.shape[1:])
    places = [order.index(stride) for stride in down]
    value = value.transpose(tuple(places) + tuple(range(bits, value.ndim)))
    for at, stride in enumerate(down):
        value = jnp.where((me // stride) % 2 == 1, jnp.flip(value, at), value)
    return value.reshape((-1,) + value.shape[bits + 1 :])


def gather_plane(value, strides):
    for stride in reversed(strides):
        value = jnp.concatenate([value, swap(value, "dp", stride)])
    return value


def regroup(value, strides):
    order = tuple(reversed(strides))
    count = value.shape[0]
    value = by_distance(value, order)
    came = [value[:1]] + [swap(value[at : at + 1], "dp", at) for at in range(1, count)]
    return by_distance(jnp.concatenate(came), order)


def halves_by_distance(order):
    me = lax.axis_index("dp")
    down = sorted(order, reverse=True)
    blocks = []
    for place in range(1 << len(order)):
        block = 0
        for at, stride in enumerate(order):
            far = (place >> (len(order) - 1 - at)) & 1
            bit = (me // stride + far) % 2
            block = block + (bit << (len(order) - 1 - down.index(stride)))
        blocks.append(block)
    blocks = jnp.stack(blocks).astype(jnp.int32)
    half = len(order) and (1 << (len(order) - 1))
    return blocks[:half], blocks[half:]


class Chain:
    def __init__(self, kept, sent, order):
        self.kept, self.order = kept, list(order)
        self.send(sent)

    def send(self, sent):
        self.sent = sent
        self.coming = swap(sent, "dp", self.order.pop(0))

    def come(self, *others):
        came = after(self.coming, *others)
        if not self.order:
            self.total = self.kept.astype(FLOAT) + came.astype(FLOAT)
            return self.total
        half = self.kept.shape[0] // 2
        sent = low_add(self.kept[half:], came[half:])
        self.kept = low_add(self.kept[:half], came[:half])
        self.send(sent)
        return sent

    def finish(self, *others):
        while self.order:
            self.come(*others)
            others = ()
        return self.come(*others)


def shards(
    tokens,
    cotangent,
    doc_ids,
    norm_gains,
    qkv_weight,
    qkv_bias,
    out_weight,
    gate_up_weight,
    down_weight,
    gains_moment,
    qkv_moment,
    bias_moment,
    out_moment,
    gate_up_moment,
    down_moment,
):
    rows = qkv_weight.shape[0]
    count = tokens.shape[0]
    query_width = out_weight.shape[1]
    heads = query_width // HD
    group_width = qkv_weight.shape[1]
    kv_heads = (group_width - query_width) // (2 * HD)
    devices = lax.axis_size("dp")
    me = lax.axis_index("dp")
    strides = bits_of(devices)
    every = tuple(strides)
    plane = 4
    near = strides[:2]
    far = tuple(strides[2:])
    units = down_weight.shape[1]
    part = -(-units // (plane * 128)) * 128
    extra = part * plane - units

    def fetch_rows(value, order):
        for stride in reversed(order):
            value = jnp.concatenate([value, swap(value, "dp", stride)])
        return by_index(value, order)

    def split_units(matrix):
        matrix = jnp.pad(matrix, ((0, 0), (0, extra)))
        return matrix.reshape(rows, plane, part).transpose(1, 0, 2)

    def join_units(value):
        value = value.transpose(1, 0, 2).reshape(rows, plane * part)
        return value[:, :units]

    attention_low = jnp.concatenate([qkv_weight.astype(BFLOAT), out_weight.astype(BFLOAT)], axis=1)
    unit_weights = jnp.concatenate(
        [split_units(one.astype(BFLOAT)) for one in (gate_up_weight[0], gate_up_weight[1], down_weight)],
        axis=2,
    )
    live = (doc_ids >= 0).astype(FLOAT)
    grad_out = cotangent.astype(FLOAT) * live[:, None]
    grad_low = grad_out.astype(BFLOAT)
    near_blocks, far_blocks = halves_by_distance(far)
    positions = positions_of(doc_ids)
    freq = THETA ** (-(2.0 / HD) * jnp.arange(HD // 2, dtype=FLOAT))
    angle = positions.astype(FLOAT)[:, None] * freq[None, :]
    cosine = jnp.cos(angle)
    sine = jnp.sin(angle)
    cosine_two = jnp.concatenate([cosine, cosine], axis=1)
    sine_two = jnp.concatenate([-sine, sine], axis=1)
    inputs = tokens.astype(FLOAT)
    scale_one = rms_scale(inputs)
    if rows % 16 == 0:
        (
            normed,
            hidden1,
            attn,
            query,
            keys,
            values,
            attention_full,
            ffn_full,
            normed2_all,
            grad_all,
        ) = forward_part(
            tokens,
            norm_gains,
            qkv_bias,
            cosine_two,
            sine_two,
            doc_ids,
            attention_low,
            unit_weights,
            grad_low,
            devices,
            heads,
            kv_heads,
        )
    else:
        attention_full = fetch_rows(attention_low, every)
        ffn_full = fetch_rows(regroup(unit_weights, near).reshape(plane * rows, -1), far)
        normed = (inputs * scale_one * norm_gains[0]).astype(BFLOAT)
        qkv = contract(normed, attention_full[:, :group_width], 1, 0) + qkv_bias
        attn, query, keys, values = attend(qkv, cosine_two, sine_two, doc_ids, heads, kv_heads)
        branch = contract(attn, attention_full[:, group_width:], 1, 1).astype(BFLOAT)
        hidden1 = inputs + (branch.astype(FLOAT) + swap(branch, "tensor", 1).astype(FLOAT))
        normed2_all = gather_plane(
            (hidden1 * rms_scale(hidden1) * norm_gains[1]).astype(BFLOAT), near
        )
        grad_all = gather_plane(grad_low, near)
    gate, up, hid, normed2_rows, grad_rows = hidden_units(normed2_all, grad_all, ffn_full)
    down_sent = weight_term(grad_rows, hid, far_blocks, 0, part)
    down_kept = weight_term(grad_rows, after(hid, down_sent), near_blocks, 0, part)
    down_chain = Chain(down_kept, down_sent, far)
    both = hidden_back(after(grad_all, down_kept), ffn_full, gate, up)
    gate_sent = weight_term(normed2_rows, both, far_blocks, 0, part)
    up_sent = weight_term(after(normed2_rows, gate_sent), both, far_blocks, 1, part)
    down_sent = down_chain.come(up_sent)
    both = after(both, down_sent)
    half = plane * count // 2
    back_sent = rows_by_width(both, ffn_full, (0, 1), half, 2 * half)
    back_kept = rows_by_width(after(both, back_sent), ffn_full, (0, 1), 0, half)
    back_chain = Chain(back_kept, back_sent, near)
    back_sent = back_chain.come(back_kept)
    gate_kept = weight_term(after(normed2_rows, back_sent), both, near_blocks, 0, part)
    gate_chain = Chain(gate_kept, gate_sent, far)
    gate_sent = gate_chain.come(gate_kept)
    up_kept = weight_term(after(normed2_rows, gate_sent), both, near_blocks, 1, part)
    up_chain = Chain(up_kept, up_sent, far)
    back = back_chain.come(up_kept).astype(BFLOAT)
    back_came = swap(back, "tensor", 1)
    layer_sent = rows_by_width(after(hid, back), ffn_full, (2,), half, 2 * half)
    layer_kept = rows_by_width(after(hid, layer_sent), ffn_full, (2,), 0, half)
    layer_chain = Chain(layer_kept, layer_sent, near)
    layer_sent = layer_chain.come(layer_kept)
    down_total = down_chain.finish(layer_sent)
    up_sent = up_chain.come(down_total)

    def own_rows(value):
        return join_units(regroup(value.astype(BFLOAT).reshape(plane, rows, part), near)).astype(FLOAT)

    down_shard = own_rows(down_total)
    dhidden1, gain_two, bias_term, dnormed, kept, sent = backward_part(
        back,
        after(back_came, up_sent),
        hidden1,
        cotangent,
        live[:, None],
        norm_gains[1:2],
        attention_full,
        normed,
        attn,
        query,
        keys,
        values,
        cosine_two,
        sine_two,
        doc_ids,
        devices,
        every,
    )
    chain = Chain(kept, sent, every)
    dnormed_came = swap(dnormed, "tensor", 1)
    gate_total = gate_chain.finish(dnormed)
    token = chain.come(gate_total)
    gate_shard = own_rows(gate_total)
    layer = layer_chain.come(token).astype(BFLOAT)
    layer_came = swap(layer, "tensor", 1)
    up_total = up_chain.finish(layer)
    token = chain.come(up_total)
    up_shard = own_rows(up_total)
    token = chain.come(token)
    dnormed = dnormed.astype(FLOAT) + after(dnormed_came, token).astype(FLOAT)
    attention_shard = chain.finish(dnormed)
    qkv_shard = attention_shard[:, :group_width]
    out_shard = attention_shard[:, group_width:]
    tokens_grad = dhidden1 + norm_back(dnormed, inputs, scale_one, norm_gains[0])
    gain_one = jnp.sum(dnormed * inputs * scale_one, axis=0)
    gate_up_shard = jnp.stack([gate_shard, up_shard])
    qkv_m = MOMENTUM * qkv_moment + qkv_shard
    out_m = MOMENTUM * out_moment + out_shard
    gate_up_m = MOMENTUM * gate_up_moment + gate_up_shard
    down_m = MOMENTUM * down_moment + down_shard
    wire = BFLOAT if rows % 16 == 0 else FLOAT
    pair = query_width + (group_width - query_width) // 2
    vectors = jnp.concatenate([gain_one, gain_two, bias_term])
    solved, vectors = orthogonalize(
        jnp.concatenate(
            [gate_up_m[0], gate_up_m[1], down_m, qkv_m[:, :pair], out_m, qkv_m[:, pair:]], axis=1
        ).astype(wire),
        vectors.reshape(-1, 128),
        query_width,
        devices,
    )
    vectors = vectors.reshape(-1)
    gains_grad = vectors[: 2 * inputs.shape[1]].reshape(2, -1)
    bias_grad = vectors[2 * inputs.shape[1] :]
    gains_m = MOMENTUM * gains_moment + gains_grad
    bias_m = MOMENTUM * bias_moment + bias_grad
    layer_out = hidden1 + (layer.astype(FLOAT) + after(layer_came, solved).astype(FLOAT))
    gate_up_update = jnp.stack([solved[:, :units], solved[:, units : 2 * units]]).astype(FLOAT)
    down_update = solved[:, 2 * units : 3 * units].astype(FLOAT)
    last = solved[:, 3 * units :].astype(FLOAT)
    qkv_update = jnp.concatenate([last[:, :pair], last[:, pair + query_width :]], axis=1)
    out_update = last[:, pair : pair + query_width]
    gains_new = vector_step(norm_gains, gains_m, LR_VECTOR)
    bias_new = vector_step(qkv_bias, bias_m, LR_BIAS)
    return (
        layer_out,
        tokens_grad,
        gains_grad,
        qkv_shard,
        bias_grad,
        out_shard,
        gate_up_shard,
        down_shard,
        gains_new,
        qkv_weight - LR_MATRIX * qkv_update,
        bias_new,
        out_weight - LR_OUT * out_update,
        gate_up_weight - LR_MATRIX * gate_up_update,
        down_weight - LR_MATRIX * down_update,
        gains_m,
        qkv_m,
        bias_m,
        out_m,
        gate_up_m,
        down_m,
    )


def solution(mesh):
    placed = (
        P("dp", None),
        P("dp", None),
        P("dp"),
        P(),
        P("dp", "tensor"),
        P("tensor"),
        P("dp", "tensor"),
        P(None, "dp", "tensor"),
        P("dp", "tensor"),
        P(),
        P("dp", "tensor"),
        P("tensor"),
        P("dp", "tensor"),
        P(None, "dp", "tensor"),
        P("dp", "tensor"),
    )
    return jax.shard_map(
        shards,
        mesh=mesh,
        in_specs=placed,
        out_specs=(
            P("dp", None),
            P("dp", None),
            P(),
            P("dp", "tensor"),
            P("tensor"),
            P("dp", "tensor"),
            P(None, "dp", "tensor"),
            P("dp", "tensor"),
            P(),
            P("dp", "tensor"),
            P("tensor"),
            P("dp", "tensor"),
            P(None, "dp", "tensor"),
            P("dp", "tensor"),
            P(),
            P("dp", "tensor"),
            P("tensor"),
            P("dp", "tensor"),
            P(None, "dp", "tensor"),
            P("dp", "tensor"),
        ),
        check_vma=False,
    )
```

```python
import functools

import jax
import jax.numpy as jnp
from jax import lax
from jax.experimental import pallas as pl
from jax.experimental.pallas import tpu as pltpu
from jax.sharding import PartitionSpec as P

HD = 128
FFB = 896
NSI = 5


EPS = 1e-06
THETA = 1000000.0
MOMENTUM = 0.5
LR_MATRIX = 0.2
LR_OUT = 0.8
LR_VECTOR = 0.1
LR_BIAS = 1.0
NS_A = 3.4445
NS_B = -4.775
NS_C = 2.0315
FLOAT = jnp.float32
BFLOAT = jnp.bfloat16


def contract(left, right, left_dim, right_dim):
    return lax.dot_general(
        left, right, (((left_dim,), (right_dim,)), ((), ())), preferred_element_type=FLOAT
    )


def positions_of(block_ids):
    index = jnp.arange(block_ids.shape[0], dtype=jnp.int32)
    change = jnp.concatenate([jnp.ones((1,), dtype=bool), block_ids[1:] != block_ids[:-1]])
    start = lax.cummax(jnp.where(change, index, jnp.zeros_like(index)), axis=0)
    return index - start


def rms_scale(values):
    return lax.rsqrt(jnp.mean(values * values, axis=-1, keepdims=True) + EPS)


def norm_back(grad, values, scale, gain):
    scaled = grad * gain
    return scale * scaled - values * scale * scale * scale * jnp.mean(
        scaled * values, axis=-1, keepdims=True
    )


def solve(width, split, depth, wide, tall, tall_low, gram, poly):
    tile = width // 2
    chunk = depth // 3

    def both(sums):
        if split:
            return sums
        total = sums[0] + sums[1]
        return total, total

    def squares(part):
        return jnp.sum(part[:tile] * part[:tile]), jnp.sum(part[tile:] * part[tile:])

    def rows_of(pair, columns):
        if not split:
            return pair[0]
        at = lax.broadcasted_iota(jnp.int32, (width, columns), 0)
        return jnp.where(at < tile, pair[0], pair[1])

    sums = (jnp.float32(0), jnp.float32(0))
    for at in range(3):
        part = wide[at * chunk : (at + 1) * chunk, :width].T
        tall[:width, at * chunk : (at + 1) * chunk] = part
        found = squares(part)
        sums = (sums[0] + found[0], sums[1] + found[1])
    sums = both(sums)
    inverse = tuple(1.0 / (jnp.sqrt(one) + 1e-07) for one in sums)
    factor = rows_of(inverse, chunk)
    for at in range(3):
        part = tall[:width, at * chunk : (at + 1) * chunk] * factor
        tall[:width, at * chunk : (at + 1) * chunk] = part
        tall_low[:width, at * chunk : (at + 1) * chunk] = part.astype(BFLOAT)
    start = tuple(one * by * by for one, by in zip(sums, inverse))

    def step(turn, sums):
        shifts = tuple(one / (tile if split else width) for one in sums)
        for at in range(2):
            mine = slice(at * tile, (at + 1) * tile)
            product = lax.dot_general(
                tall_low[mine, :],
                tall_low[:width, :],
                (((1,), (1,)), ((), ())),
                preferred_element_type=FLOAT,
            )
            row = lax.broadcasted_iota(jnp.int32, (tile, width), 0) + at * tile
            column = lax.broadcasted_iota(jnp.int32, (tile, width), 1)
            product = jnp.where(row == column, product - shifts[at], product)
            if split:
                product = jnp.where((column < tile) == (at == 0), product, 0.0)
            gram[mine, :width] = product.astype(BFLOAT)
        for at in range(2):
            mine = slice(at * tile, (at + 1) * tile)
            product = jnp.dot(
                gram[mine, :width], gram[:width, :width], preferred_element_type=FLOAT
            )
            linear = NS_B + 2.0 * NS_C * shifts[at]
            poly[mine, :width] = (
                linear * gram[mine, :width].astype(FLOAT) + NS_C * product
            ).astype(BFLOAT)
        factor = rows_of(tuple(NS_A + NS_B * s + NS_C * s * s for s in shifts), chunk)
        sums = (jnp.float32(0), jnp.float32(0))
        for at in range(3):
            span = slice(at * chunk, (at + 1) * chunk)
            part = factor * tall[:width, span] + jnp.dot(
                poly[:width, :width], tall_low[:width, span], preferred_element_type=FLOAT
            )
            tall[:width, span] = part
            tall_low[:width, span] = part.astype(BFLOAT)
            found = squares(part)
            sums = (sums[0] + found[0], sums[1] + found[1])
        return both(sums)

    lax.fori_loop(0, NSI, step, start)
    for at in range(3):
        wide[at * chunk : (at + 1) * chunk, :width] = tall[
            :width, at * chunk : (at + 1) * chunk
        ].T


def muon_kernel(
    devices,
    rows,
    blocks,
    query_width,
    keeper,
    units,
    vectors,
    units_new,
    vectors_sum,
    all_vectors,
    first,
    second,
    first_back,
    second_back,
    wide,
    tall,
    tall_low,
    gram,
    poly,
    here_sem,
    go_sem,
    come_sem,
    back_sem,
    home_sem,
    go_vector,
    come_vector,
):
    me = lax.axis_index("dp")
    depth = devices * rows
    mine = jnp.where(me < keeper, me, me - 1)
    keeps = me == keeper
    holds = jnp.logical_and(me != keeper, mine < blocks)
    key_width = FFB - query_width

    def block_of(device):
        return jnp.where(device < keeper, device, device - 1)

    def owner_of(block):
        return jnp.where(block < keeper, block, block + 1)

    def rows_of(array, unit):
        return array.at[:, pl.ds(pl.multiple_of(unit * FFB, 128), FFB)]

    def remote(source, target, send, receive, device):
        return pltpu.make_async_remote_copy(
            src_ref=source,
            dst_ref=target,
            send_sem=send,
            recv_sem=receive,
            device_id={"dp": device},
            device_id_type=pl.DeviceIdType.MESH,
        )

    def others(body):
        def step(turn, carry):
            body(lax.rem(me + turn, devices))
            return carry

        lax.fori_loop(1, devices, step, 0)

    barrier = pltpu.get_barrier_semaphore()

    def greet(device):
        pl.semaphore_signal(
            barrier, inc=1, device_id={"dp": device}, device_id_type=pl.DeviceIdType.MESH
        )

    others(greet)
    pl.semaphore_wait(barrier, devices - 1)

    def way_in(unit, at, sender, device):
        return remote(
            rows_of(units, unit),
            (first, second)[at].at[sender],
            go_sem.at[device, at],
            come_sem.at[sender, at],
            device,
        )

    def to_owner(device, what):
        @pl.when(device == keeper)
        def _():
            what(way_in(blocks, 0, me, device))
            what(way_in(blocks + 1, 1, me, device))

        @pl.when(jnp.logical_and(device != keeper, block_of(device) < blocks))
        def _():
            what(way_in(block_of(device), 0, me, device))

    def share(sender, device):
        return remote(
            vectors, all_vectors.at[sender], go_vector.at[device], come_vector.at[sender], device
        )

    others(lambda device: to_owner(device, lambda copy: copy.start()))
    others(lambda device: share(me, device).start())

    def own_in(what):
        @pl.when(keeps)
        def _():
            what(pltpu.make_async_copy(rows_of(units, blocks), first.at[me], here_sem.at[0]))
            what(pltpu.make_async_copy(rows_of(units, blocks + 1), second.at[me], here_sem.at[1]))

        @pl.when(holds)
        def _():
            what(pltpu.make_async_copy(rows_of(units, mine), first.at[me], here_sem.at[0]))

    own_in(lambda copy: copy.start())
    own_in(lambda copy: copy.wait())

    def arrived(device):
        @pl.when(jnp.logical_or(keeps, holds))
        def _():
            way_in(0, 0, device, me).wait_recv()

        @pl.when(keeps)
        def _():
            way_in(0, 1, device, me).wait_recv()

    others(arrived)

    def load(buffer, source_at, size, target_at):
        def step(at, carry):
            wide[pl.ds(pl.multiple_of(at * rows, 8), rows), target_at : target_at + size] = buffer[
                at, :, source_at : source_at + size
            ].astype(FLOAT)
            return carry

        lax.fori_loop(0, devices, step, 0)

    def store(buffer, source_at, size, target_at):
        def step(at, carry):
            buffer[at, :, target_at : target_at + size] = wide[
                pl.ds(pl.multiple_of(at * rows, 8), rows), source_at : source_at + size
            ].astype(buffer.dtype)
            return carry

        lax.fori_loop(0, devices, step, 0)

    def way_back(unit, at, device):
        return remote(
            (first_back, second_back)[at].at[device],
            rows_of(units_new, unit),
            back_sem.at[device, at],
            home_sem.at[unit],
            device,
        )

    def own_back(unit, at):
        return pltpu.make_async_copy(
            (first_back, second_back)[at].at[me], rows_of(units_new, unit), here_sem.at[at]
        )

    @pl.when(holds)
    def _():
        load(first, 0, FFB, 0)
        solve(FFB, False, depth, wide, tall, tall_low, gram, poly)
        store(first_back, 0, FFB, 0)
        others(lambda device: way_back(mine, 0, device).start())
        own_back(mine, 0).start()
        own_back(mine, 0).wait()

    @pl.when(keeps)
    def _():
        load(first, query_width, key_width, 0)
        load(second, query_width, key_width, key_width)
        solve(2 * key_width, True, depth, wide, tall, tall_low, gram, poly)
        store(first_back, 0, key_width, query_width)
        store(second_back, key_width, key_width, query_width)
        for at, buffer, back in ((0, first, first_back), (1, second, second_back)):
            load(buffer, 0, query_width, 0)
            solve(query_width, False, depth, wide, tall, tall_low, gram, poly)
            store(back, 0, query_width, 0)
            others(lambda device: way_back(blocks + at, at, device).start())
            own_back(blocks + at, at).start()
        own_back(blocks, 0).wait()
        own_back(blocks + 1, 1).wait()

    own_vectors = pltpu.make_async_copy(vectors, all_vectors.at[me], here_sem.at[2])
    own_vectors.start()
    own_vectors.wait()
    others(lambda device: share(device, me).wait_recv())
    vectors_sum[...] = lax.fori_loop(
        1, devices, lambda at, total: total + all_vectors[at], all_vectors[0]
    )
    others(lambda device: share(me, device).wait_send())

    def home(block, carry):
        @pl.when(owner_of(block) != me)
        def _():
            way_back(block, 0, me).wait_recv()

        return carry

    lax.fori_loop(0, blocks, home, 0)

    @pl.when(jnp.logical_not(keeps))
    def _():
        way_back(blocks, 0, me).wait_recv()
        way_back(blocks + 1, 1, me).wait_recv()

    others(lambda device: to_owner(device, lambda copy: copy.wait_send()))

    @pl.when(jnp.logical_or(keeps, holds))
    def _():
        others(lambda device: way_back(0, 0, device).wait_send())

    @pl.when(keeps)
    def _():
        others(lambda device: way_back(0, 1, device).wait_send())


def orthogonalize(units, vectors, query_width, devices):
    rows = units.shape[0]
    blocks = units.shape[1] // FFB - 2
    depth = devices * rows
    wire = units.dtype
    kernel = functools.partial(
        muon_kernel, devices, rows, blocks, query_width, min(devices // 2, blocks)
    )
    hbm = pl.BlockSpec(memory_space=pltpu.HBM)
    return pl.pallas_call(
        kernel,
        out_shape=[
            jax.ShapeDtypeStruct(units.shape, wire),
            jax.ShapeDtypeStruct(vectors.shape, FLOAT),
        ],
        in_specs=[hbm, pl.BlockSpec(memory_space=pltpu.VMEM)],
        out_specs=[hbm, pl.BlockSpec(memory_space=pltpu.VMEM)],
        scratch_shapes=[
            pltpu.VMEM((devices,) + vectors.shape, FLOAT),
            pltpu.VMEM((devices, rows, FFB), wire),
            pltpu.VMEM((devices, rows, FFB), wire),
            pltpu.VMEM((devices, rows, FFB), wire),
            pltpu.VMEM((devices, rows, FFB), wire),
            pltpu.VMEM((depth, FFB), FLOAT),
            pltpu.VMEM((FFB, depth), FLOAT),
            pltpu.VMEM((FFB, depth), BFLOAT),
            pltpu.VMEM((FFB, FFB), BFLOAT),
            pltpu.VMEM((FFB, FFB), BFLOAT),
            pltpu.SemaphoreType.DMA((3,)),
            pltpu.SemaphoreType.DMA((devices, 2)),
            pltpu.SemaphoreType.DMA((devices, 2)),
            pltpu.SemaphoreType.DMA((devices, 2)),
            pltpu.SemaphoreType.DMA((blocks + 2,)),
            pltpu.SemaphoreType.DMA((devices,)),
            pltpu.SemaphoreType.DMA((devices,)),
        ],
        compiler_params=pltpu.CompilerParams(
            collective_id=0, has_side_effects=True, vmem_limit_bytes=52 * 2**20
        ),
        cost_estimate=pl.CostEstimate(
            flops=64 * 10**9, bytes_accessed=16 * 2**20, transcendentals=0
        ),
    )(units, vectors)


LIGHT = pl.CostEstimate(flops=1024, bytes_accessed=1024, transcendentals=0)


def call_light(body, grid, ins, outs):
    return pl.pallas_call(
        body,
        grid=grid,
        in_specs=[pl.BlockSpec(block, at) for _, block, at in ins],
        out_specs=[pl.BlockSpec(block, at) for _, _, block, at in outs],
        out_shape=[jax.ShapeDtypeStruct(shape, dtype) for shape, dtype, _, _ in outs],
        compiler_params=pltpu.CompilerParams(vmem_limit_bytes=56 * 2**20),
        cost_estimate=LIGHT,
    )(*[array for array, _, _ in ins])


def spans(size, step):
    return [slice(at, min(at + step, size)) for at in range(0, size, step)]


def hidden_units(tokens, grads, weights, block=256):
    count, depth = tokens.shape
    part = weights.shape[1] // 3

    def body(x, y, w_gate, w_up, gate, up, hid, turned_x, turned_y):
        turned_x[...] = x[...].astype(FLOAT).T.astype(BFLOAT)
        turned_y[...] = y[...].astype(FLOAT).T.astype(BFLOAT)
        for span in spans(part, 512):
            g = jnp.dot(x[...], w_gate[:, span], preferred_element_type=FLOAT)
            u = jnp.dot(x[...], w_up[:, span], preferred_element_type=FLOAT)
            gate[:, span] = g
            up[:, span] = u
            hid[:, span] = (g * jax.nn.sigmoid(g) * u).astype(BFLOAT)

    rows = lambda at: (at, 0)
    columns = lambda at: (0, at)
    return call_light(
        body,
        (count // block,),
        [
            (tokens, (block, depth), rows),
            (grads, (block, depth), rows),
            (weights, (depth, part), lambda at: (0, 0)),
            (weights, (depth, part), lambda at: (0, 1)),
        ],
        [
            ((count, part), FLOAT, (block, part), rows),
            ((count, part), FLOAT, (block, part), rows),
            ((count, part), BFLOAT, (block, part), rows),
            ((depth, count), BFLOAT, (depth, block), columns),
            ((depth, count), BFLOAT, (depth, block), columns),
        ],
    )


def hidden_back(grads, weights, gate, up, block=256):
    count, depth = grads.shape
    part = weights.shape[1] // 3

    def body(x, w, gate, up, both):
        for span in spans(part, 512):
            dhid = jnp.dot(x[...], w[:, span], preferred_element_type=FLOAT)
            g = gate[:, span]
            sigma = jax.nn.sigmoid(g)
            both[:, span] = (dhid * up[:, span] * sigma * (1.0 + g * (1.0 - sigma))).astype(BFLOAT)
            both[:, part + span.start : part + span.stop] = (dhid * (g * sigma)).astype(BFLOAT)

    rows = lambda at: (at, 0)
    return call_light(
        body,
        (count // block,),
        [
            (grads, (block, depth), rows),
            (weights, (depth, part), lambda at: (0, 2)),
            (gate, (block, part), rows),
            (up, (block, part), rows),
        ],
        [((count, 2 * part), BFLOAT, (block, 2 * part), rows)],
    )[0]


def rows_by_width(units, weights, places, first, last, block=256):
    width = weights.shape[0]
    part = weights.shape[1] // 3

    def body(x, *refs):
        out = refs[-1]
        for span in spans(width, 512):
            out[:, span] = sum(
                lax.dot_general(
                    x[:, at * part : (at + 1) * part],
                    refs[at][span, :],
                    (((1,), (1,)), ((), ())),
                    preferred_element_type=FLOAT,
                )
                for at in range(len(places))
            ).astype(BFLOAT)

    def column(place):
        return (weights, (width, part), lambda at: (0, place))

    return call_light(
        body,
        ((last - first) // block,),
        [(units, (block, len(places) * part), lambda at: (at + first // block, 0))]
        + [column(place) for place in places],
        [((last - first, width), BFLOAT, (block, width), lambda at: (at, 0))],
    )[0]


def weight_term(left, right, blocks, place, width):
    count = left.shape[1]
    picked = blocks.shape[0]
    tall = left.shape[0] // (2 * picked)

    def body(blocks, x, y, out):
        for span in spans(width, 512):
            out[:, span] = jnp.dot(
                x[...], y[:, span], preferred_element_type=FLOAT
            ).astype(BFLOAT)

    return pl.pallas_call(
        body,
        grid_spec=pltpu.PrefetchScalarGridSpec(
            num_scalar_prefetch=1,
            grid=(picked,),
            in_specs=[
                pl.BlockSpec((tall, count), lambda at, blocks: (blocks[at], 0)),
                pl.BlockSpec((count, width), lambda at, blocks: (0, place)),
            ],
            out_specs=pl.BlockSpec((tall, width), lambda at, blocks: (at, 0)),
        ),
        out_shape=jax.ShapeDtypeStruct((picked * tall, width), BFLOAT),
        compiler_params=pltpu.CompilerParams(vmem_limit_bytes=48 * 2**20),
        cost_estimate=LIGHT,
    )(blocks, left, right)


def turned(value, cosine, sine):
    return value * cosine + pltpu.roll(value, HD // 2, 1) * sine


def softmax_of(query, keys, ids, key_ids, first):
    scores = lax.dot_general(
        query, keys, (((1,), (1,)), ((), ())), preferred_element_type=FLOAT
    ) * (HD ** (-0.5))
    row = lax.broadcasted_iota(jnp.int32, scores.shape, 0) + first
    column = lax.broadcasted_iota(jnp.int32, scores.shape, 1)
    scores = jnp.where((ids == key_ids) & (column <= row), scores, -1e30)
    expo = jnp.exp(scores - jnp.max(scores, axis=-1, keepdims=True))
    return expo / jnp.sum(expo, axis=-1, keepdims=True)


def attend(qkv, cosine, sine, doc_ids, heads, kv_heads):
    count = qkv.shape[0]
    share = heads // kv_heads
    half = count // 2

    def body(q, k, v, cosine, sine, ids, key_ids, attn, query, keys, values):
        query[...] = turned(q[...], cosine[...], sine[...]).astype(BFLOAT)
        keys[...] = turned(k[...], cosine[...], sine[...]).astype(BFLOAT)
        values[...] = v[...].astype(BFLOAT)
        for first in (0, half):
            last = first + half
            probs = softmax_of(
                query[first:last, :], keys[:last, :], ids[first:last, :], key_ids[:, :last], first
            )
            attn[first:last, :] = jnp.dot(
                probs.astype(BFLOAT), values[:last, :], preferred_element_type=FLOAT
            ).astype(BFLOAT)

    one = lambda at: (0, 0)
    head = lambda at: (0, at)
    group = lambda at: (0, at // share)
    block = (count, HD)
    return pl.pallas_call(
        body,
        grid=(heads,),
        in_specs=[
            pl.BlockSpec(block, head),
            pl.BlockSpec(block, lambda at: (0, heads + at // share)),
            pl.BlockSpec(block, lambda at: (0, heads + kv_heads + at // share)),
            pl.BlockSpec(block, one),
            pl.BlockSpec(block, one),
            pl.BlockSpec((count, 1), one),
            pl.BlockSpec((1, count), one),
        ],
        out_specs=[
            pl.BlockSpec(block, head),
            pl.BlockSpec(block, head),
            pl.BlockSpec(block, group),
            pl.BlockSpec(block, group),
        ],
        out_shape=[
            jax.ShapeDtypeStruct((count, heads * HD), BFLOAT),
            jax.ShapeDtypeStruct((count, heads * HD), BFLOAT),
            jax.ShapeDtypeStruct((count, kv_heads * HD), BFLOAT),
            jax.ShapeDtypeStruct((count, kv_heads * HD), BFLOAT),
        ],
        compiler_params=pltpu.CompilerParams(vmem_limit_bytes=32 * 2**20),
        cost_estimate=LIGHT,
    )(qkv, qkv, qkv, cosine, sine, doc_ids[:, None], doc_ids[None, :])


def forward_kernel(
    devices,
    heads,
    kv_heads,
    tokens,
    gains,
    bias,
    cosine,
    sine,
    ids,
    key_ids,
    shard,
    units,
    grads,
    normed,
    hidden,
    attn,
    query,
    keys,
    values,
    attention_out,
    ffn_full,
    tokens_all,
    grads_all,
    attention_full,
    qkv,
    branch,
    branch_came,
    normed_two,
    here_sem,
    z_send,
    z_come,
    x_send,
    x_come,
    core_send,
    core_come,
    group_send,
    group_come,
    right_send,
    left_send,
    plane_come,
    pair_send,
    pair_come,
):
    me = lax.axis_index("dp")
    side = lax.axis_index("tensor")
    planes = devices // 4
    rows = shard.shape[0]
    count = tokens.shape[0]
    place, plane = lax.rem(me, 4), me // 4
    across = me + 2 - 4 * (place // 2)
    beside = me + 1 - 2 * lax.rem(me, 2)
    part = ffn_full.shape[1] // 3
    share = heads // kv_heads
    depth = tokens.shape[1]
    half = count // 2

    def remote(source, target, send, come, device):
        return pltpu.make_async_remote_copy(
            src_ref=source,
            dst_ref=target,
            send_sem=send,
            recv_sem=come,
            device_id={"dp": device},
            device_id_type=pl.DeviceIdType.MESH,
        )

    def loop(first, last, body):
        def step(turn, carry):
            body(turn)
            return carry

        lax.fori_loop(first, last, step, 0)

    barrier = pltpu.get_barrier_semaphore()

    def greet(where):
        pl.semaphore_signal(barrier, inc=1, device_id=where, device_id_type=pl.DeviceIdType.MESH)

    def peer(turn):
        return lax.rem(plane + turn, planes) * 4 + place

    def plane_peer(turn):
        return plane * 4 + lax.rem(place + turn, 4)

    loop(1, planes, lambda turn: greet({"dp": peer(turn)}))
    loop(1, 4, lambda turn: greet({"dp": plane_peer(turn)}))
    greet({"tensor": 1 - side})
    pl.semaphore_wait(barrier, planes + 3)

    def block(owner):
        return attention_full.at[pl.ds(pl.multiple_of(owner * rows, 16), rows)]

    def owner_at(turn):
        return lax.rem(plane + planes - turn, planes) * 4

    def to_column(turn):
        return remote(shard, block(me), z_send.at[turn], z_come.at[turn], peer(turn))

    def from_column(turn):
        owner = owner_at(turn) + place
        return remote(block(owner), block(owner), z_send.at[turn], z_come.at[turn], me)

    def x_copy(turn):
        owner = owner_at(turn) + place
        return remote(block(owner), block(owner), x_send.at[turn], x_come.at[turn], across)

    def x_wait(turn):
        owner = owner_at(turn) + lax.rem(across, 4)
        return remote(block(owner), block(owner), x_send.at[turn], x_come.at[turn], across)

    def core_copy(turn, far):
        owner = owner_at(turn) + (lax.rem(across, 4) if far else place)
        return remote(
            block(owner), block(owner), core_send.at[turn, far], core_come.at[turn, far], beside
        )

    def core_wait(turn, far):
        owner = owner_at(turn) + lax.rem(beside, 4) + (2 - 4 * (place // 2) if far else 0)
        return remote(
            block(owner), block(owner), core_send.at[turn, far], core_come.at[turn, far], beside
        )

    def unit_rows(owner):
        return ffn_full.at[pl.ds(pl.multiple_of(owner * rows, 16), rows)]

    def group_copy(turn):
        return remote(
            units.at[lax.rem(place + turn, 4)],
            unit_rows(me),
            group_send.at[turn],
            group_come.at[turn],
            plane_peer(turn),
        )

    def group_wait(turn):
        owner = plane * 4 + lax.rem(place + 4 - turn, 4)
        return remote(
            units.at[0], unit_rows(owner), group_send.at[turn], group_come.at[turn], me
        )

    def slab(origin, third):
        return ffn_full.at[
            pl.ds(pl.multiple_of(origin * 4 * rows, 16), 4 * rows), third * part : (third + 1) * part
        ]

    def move(origin, third, right):
        send = right_send if right else left_send
        return remote(
            slab(origin, third),
            slab(origin, third),
            send.at[origin, third],
            plane_come.at[origin, third],
            me + 4 if right else me - 4,
        )

    def pump(hop, third):
        behind, ahead = plane - hop, plane + hop

        @pl.when(behind >= 0)
        def _():
            move(behind, third, True).wait_recv()

            @pl.when(plane < planes - 1)
            def _():
                move(behind, third, True).start()

        @pl.when(ahead < planes)
        def _():
            move(ahead, third, False).wait_recv()

            @pl.when(plane > 0)
            def _():
                move(ahead, third, False).start()

    def x_rows(array, at):
        return remote(
            array.at[0:count], array.at[count : 2 * count], pair_send.at[at], pair_come.at[at], across
        )

    def core_rows(array, at):
        return remote(
            array.at[0 : 2 * count],
            array.at[2 * count : 4 * count],
            pair_send.at[at],
            pair_come.at[at],
            beside,
        )

    loop(1, planes, lambda turn: to_column(turn).start())
    own_block = pltpu.make_async_copy(shard, block(me), here_sem.at[0])
    own_block.start()
    loop(1, 4, lambda turn: group_copy(turn).start())
    own_units = pltpu.make_async_copy(units.at[place], unit_rows(me), here_sem.at[1])
    own_units.start()
    own_grads = pltpu.make_async_copy(grads, grads_all.at[0:count], here_sem.at[2])
    own_grads.start()

    def norm(value, gain):
        scale = lax.rsqrt(jnp.mean(value * value, axis=-1, keepdims=True) + EPS)
        return (value * scale * gain).astype(BFLOAT)

    for first in range(0, count, 128):
        normed[first : first + 128, :] = norm(
            tokens[first : first + 128, :].astype(FLOAT), gains[0:1, :]
        )

    own_block.wait()
    x_copy(0).start()
    core_copy(0, 0).start()

    def forward(turn):
        from_column(turn).wait_recv()
        x_copy(turn).start()
        core_copy(turn, 0).start()

    loop(1, planes, forward)
    own_units.wait()
    loop(1, 4, lambda turn: group_wait(turn).wait_recv())
    for third in range(3):

        @pl.when(plane < planes - 1)
        def _():
            move(plane, third, True).start()

        @pl.when(plane > 0)
        def _():
            move(plane, third, False).start()

    own_grads.wait()
    x_rows(grads_all, 0).start()

    def forward_far(turn):
        x_wait(turn).wait_recv()
        core_copy(turn, 1).start()

    loop(0, planes, forward_far)
    pump(1, 0)

    def arrive(turn):
        core_wait(turn, 0).wait_recv()
        core_wait(turn, 1).wait_recv()

    loop(0, planes, arrive)
    attention_copy = pltpu.make_async_copy(attention_full, attention_out, here_sem.at[0])
    attention_copy.start()

    query_width = heads * HD
    group_width = qkv.shape[1]
    for first in range(0, group_width, 256):
        qkv[:, first : first + 256] = (
            jnp.dot(
                normed[...], attention_full[:, first : first + 256], preferred_element_type=FLOAT
            )
            + bias[:, first : first + 256]
        )

    def columns(at):
        return pl.ds(pl.multiple_of(at * HD, HD), HD)

    def key_head(at):
        keys[:, columns(at)] = turned(
            qkv[:, columns(heads + at)], cosine[...], sine[...]
        ).astype(BFLOAT)
        values[:, columns(at)] = qkv[:, columns(heads + kv_heads + at)].astype(BFLOAT)

    loop(0, kv_heads, key_head)

    def head(at):
        query[:, columns(at)] = turned(qkv[:, columns(at)], cosine[...], sine[...]).astype(BFLOAT)
        group = columns(at // share)
        for first in (0, half):
            last = first + half
            probs = softmax_of(
                query[first:last, columns(at)],
                keys[:last, group],
                ids[first:last, :],
                key_ids[:, :last],
                first,
            )
            attn[first:last, columns(at)] = jnp.dot(
                probs.astype(BFLOAT), values[:last, group], preferred_element_type=FLOAT
            ).astype(BFLOAT)

    loop(0, heads, head)
    for first in range(0, depth, 256):
        branch[:, first : first + 256] = lax.dot_general(
            attn[...],
            attention_full[first : first + 256, group_width:],
            (((1,), (1,)), ((), ())),
            preferred_element_type=FLOAT,
        ).astype(BFLOAT)
    sum_copy = pltpu.make_async_remote_copy(
        src_ref=branch,
        dst_ref=branch_came,
        send_sem=here_sem.at[3],
        recv_sem=here_sem.at[4],
        device_id={"tensor": 1 - side},
        device_id_type=pl.DeviceIdType.MESH,
    )
    sum_copy.start()
    pump(1, 1)
    pump(1, 2)
    x_rows(grads_all, 0).wait()
    core_rows(grads_all, 1).start()
    pump(2, 0)
    sum_copy.wait()
    for first in range(0, count, 128):
        span = slice(first, first + 128)
        value = tokens[span, :].astype(FLOAT) + (
            branch[span, :].astype(FLOAT) + branch_came[span, :].astype(FLOAT)
        )
        hidden[span, :] = value
        normed_two[span, :] = norm(value, gains[1:2, :])
    own_tokens = pltpu.make_async_copy(normed_two, tokens_all.at[0:count], here_sem.at[1])
    own_tokens.start()
    own_tokens.wait()
    x_rows(tokens_all, 2).start()
    pump(2, 1)
    pump(2, 2)
    x_rows(tokens_all, 2).wait()
    core_rows(tokens_all, 3).start()
    for hop in range(3, planes):
        for third in range(3):
            pump(hop, third)
    core_rows(grads_all, 1).wait()
    core_rows(tokens_all, 3).wait()
    attention_copy.wait()

    loop(1, planes, lambda turn: to_column(turn).wait_send())

    def sent(turn):
        x_copy(turn).wait_send()
        core_copy(turn, 0).wait_send()
        core_copy(turn, 1).wait_send()

    loop(0, planes, sent)
    loop(1, 4, lambda turn: group_copy(turn).wait_send())
    for third in range(3):

        @pl.when(plane < planes - 1)
        def _():
            loop(0, plane + 1, lambda origin: move(origin, third, True).wait_send())

        @pl.when(plane > 0)
        def _():
            loop(plane, planes, lambda origin: move(origin, third, False).wait_send())


def forward_part(
    tokens, gains, bias, cosine, sine, doc_ids, shard, units, grads, devices, heads, kv_heads
):
    count, depth = tokens.shape
    rows, width = shard.shape
    planes = devices // 4
    group_width = bias.shape[0]
    query_width = heads * HD
    hbm = pl.BlockSpec(memory_space=pltpu.HBM)
    vmem = pl.BlockSpec(memory_space=pltpu.VMEM)
    dma = pltpu.SemaphoreType.DMA
    return pl.pallas_call(
        functools.partial(forward_kernel, devices, heads, kv_heads),
        out_shape=[
            jax.ShapeDtypeStruct((count, depth), BFLOAT),
            jax.ShapeDtypeStruct((count, depth), FLOAT),
            jax.ShapeDtypeStruct((count, query_width), BFLOAT),
            jax.ShapeDtypeStruct((count, query_width), BFLOAT),
            jax.ShapeDtypeStruct((count, kv_heads * HD), BFLOAT),
            jax.ShapeDtypeStruct((count, kv_heads * HD), BFLOAT),
            jax.ShapeDtypeStruct((devices * rows, width), BFLOAT),
            jax.ShapeDtypeStruct((devices * rows, units.shape[2]), BFLOAT),
            jax.ShapeDtypeStruct((4 * count, depth), BFLOAT),
            jax.ShapeDtypeStruct((4 * count, depth), BFLOAT),
        ],
        in_specs=[vmem] * 7 + [hbm] * 3,
        out_specs=[vmem] * 6 + [hbm] * 4,
        scratch_shapes=[
            pltpu.VMEM((devices * rows, width), BFLOAT),
            pltpu.VMEM((count, group_width), FLOAT),
            pltpu.VMEM((count, depth), BFLOAT),
            pltpu.VMEM((count, depth), BFLOAT),
            pltpu.VMEM((count, depth), BFLOAT),
            dma((5,)),
            dma((planes,)),
            dma((planes,)),
            dma((planes,)),
            dma((planes,)),
            dma((planes, 2)),
            dma((planes, 2)),
            dma((4,)),
            dma((4,)),
            dma((planes, 3)),
            dma((planes, 3)),
            dma((planes, 3)),
            dma((4,)),
            dma((4,)),
        ],
        compiler_params=pltpu.CompilerParams(
            collective_id=1, has_side_effects=True, vmem_limit_bytes=48 * 2**20
        ),
        cost_estimate=LIGHT,
    )(
        tokens,
        gains,
        bias[None, :],
        cosine,
        sine,
        doc_ids[:, None],
        doc_ids[None, :],
        shard,
        units,
        grads,
    )


def exchange_kernel(
    near, far, pieces, total, joined, came, work, chain_send, chain_come, group_send, group_come, here_sem
):
    me = lax.axis_index("dp")
    place, plane = lax.rem(me, 4), me // 4
    size = pieces.shape[3]
    width = near.shape[2] // 2

    def flip(stride):
        return me + stride - 2 * stride * lax.rem(me // stride, 2)

    def plane_peer(turn):
        return plane * 4 + lax.rem(place + turn, 4)

    def remote(source, target, send, receive, device):
        return pltpu.make_async_remote_copy(
            src_ref=source,
            dst_ref=target,
            send_sem=send,
            recv_sem=receive,
            device_id={"dp": device},
            device_id_type=pl.DeviceIdType.MESH,
        )

    barrier = pltpu.get_barrier_semaphore()
    for device in [plane_peer(turn) for turn in (1, 2, 3)] + [flip(stride) for stride in HALVES[0][2:]]:
        pl.semaphore_signal(
            barrier, inc=1, device_id={"dp": device}, device_id_type=pl.DeviceIdType.MESH
        )
    pl.semaphore_wait(barrier, 3 + len(HALVES[0][2:]))

    def columns(at):
        return slice(at * width, (at + 1) * width)

    def blocks(step):
        return near.shape[0] >> step

    def offset(step):
        return 2 * near.shape[0] - 2 * blocks(step)

    def move(step, at):
        count = blocks(step)
        if step == 0:
            source = far.at[:, :, columns(at)]
        else:
            first = offset(step - 1) + count
            source = work.at[first : first + count, :, columns(at)]
        first = offset(step)
        return remote(
            source,
            came.at[first : first + count, :, columns(at)],
            chain_send.at[step, at],
            chain_come.at[step, at],
            flip(HALVES[at][step]),
        )

    def regroup(kind, turn):
        owner = lax.rem(place + turn, 4)
        return remote(
            pieces.at[kind, owner],
            joined.at[kind, :, pl.ds(pl.multiple_of(place * size, 128), size)],
            group_send.at[kind, turn],
            group_come.at[kind, turn],
            plane_peer(turn),
        )

    def regroup_wait(kind, turn):
        sender = lax.rem(place + 4 - turn, 4)
        return remote(
            pieces.at[kind, 0],
            joined.at[kind, :, pl.ds(pl.multiple_of(sender * size, 128), size)],
            group_send.at[kind, turn],
            group_come.at[kind, turn],
            me,
        )

    def own(kind):
        return pltpu.make_async_copy(
            pieces.at[kind, place],
            joined.at[kind, :, pl.ds(pl.multiple_of(place * size, 128), size)],
            here_sem.at[kind],
        )

    steps = len(HALVES[0])
    for at in range(2):
        move(0, at).start()
    kinds = range(pieces.shape[0])
    for kind in kinds:
        for turn in (1, 2, 3):
            regroup(kind, turn).start()
        own(kind).start()
    for step in range(steps):
        for at in range(2):
            move(step, at).wait()
            count = blocks(step)
            first = offset(step)
            held = near if step == 0 else work
            begin = 0 if step == 0 else offset(step - 1)
            for block in range(count):
                value = held[begin + block, :, columns(at)].astype(FLOAT) + came[
                    first + block, :, columns(at)
                ].astype(FLOAT)
                if step == steps - 1:
                    total[:, columns(at)] = value
                else:
                    work[first + block, :, columns(at)] = value.astype(BFLOAT)
            if step < steps - 1:
                move(step + 1, at).start()
    for kind in kinds:
        for turn in (1, 2, 3):
            regroup_wait(kind, turn).wait_recv()
            regroup(kind, turn).wait_send()
        own(kind).wait()


HALVES = ((1, 2, 4, 8), (1, 4, 8, 2))


def exchange(near, far, pieces):
    count, rows, width = near.shape
    kinds, _, _, size = pieces.shape
    hbm = pl.BlockSpec(memory_space=pltpu.HBM)
    vmem = pl.BlockSpec(memory_space=pltpu.VMEM)
    dma = pltpu.SemaphoreType.DMA
    return pl.pallas_call(
        exchange_kernel,
        out_shape=[
            jax.ShapeDtypeStruct((rows, width), FLOAT),
            jax.ShapeDtypeStruct((kinds, rows, 4 * size), BFLOAT),
        ],
        in_specs=[vmem, vmem, hbm],
        out_specs=[vmem, hbm],
        scratch_shapes=[
            pltpu.VMEM((2 * count, rows, width), BFLOAT),
            pltpu.VMEM((2 * count, rows, width), BFLOAT),
            dma((4, 2)),
            dma((4, 2)),
            dma((kinds, 4)),
            dma((kinds, 4)),
            dma((kinds,)),
        ],
        compiler_params=pltpu.CompilerParams(
            collective_id=2, has_side_effects=True, vmem_limit_bytes=40 * 2**20
        ),
        cost_estimate=LIGHT,
    )(near, far, pieces)


def backward_part(
    back,
    came,
    hidden,
    cotangent,
    live,
    gain,
    weights,
    normed,
    attn,
    query,
    keys,
    values,
    cosine,
    sine,
    doc_ids,
    devices,
    orders,
):
    count, depth = hidden.shape
    rows = depth // devices
    heads, kv_heads = query.shape[1] // HD, keys.shape[1] // HD
    share = heads // kv_heads
    query_width = heads * HD
    group_width = (heads + 2 * kv_heads) * HD
    width = weights.shape[1]
    half = count // 2
    scale = HD ** (-0.5)

    def body(
        back,
        came,
        hidden,
        cotangent,
        live,
        gain,
        weights,
        normed,
        attn,
        query,
        keys,
        values,
        cosine,
        sine,
        ids,
        key_ids,
        dhidden,
        gain_term,
        bias_term,
        dnormed,
        near,
        far,
        dbranch,
        dattn,
        dqkv,
        dkeys,
        dvalues,
        term,
    ):
        total = jnp.zeros((1, depth), FLOAT)
        for first in range(0, count, 128):
            span = slice(first, first + 128)
            grad = back[span, :].astype(FLOAT) + came[span, :].astype(FLOAT)
            value = hidden[span, :]
            root = lax.rsqrt(jnp.mean(value * value, axis=-1, keepdims=True) + EPS)
            scaled = grad * gain[...]
            result = cotangent[span, :].astype(FLOAT) * live[span, :] + (
                root * scaled
                - value * root * root * root * jnp.mean(scaled * value, axis=-1, keepdims=True)
            )
            dhidden[span, :] = result
            dbranch[span, :] = result.astype(BFLOAT)
            total = total + jnp.sum(grad * value * root, axis=0, keepdims=True)
        gain_term[...] = total
        for first in range(0, query_width, 256):
            dattn[:, first : first + 256] = jnp.dot(
                dbranch[...],
                weights[:, group_width + first : group_width + first + 256],
                preferred_element_type=FLOAT,
            ).astype(BFLOAT)

        def columns(at):
            return pl.ds(pl.multiple_of(at * HD, HD), HD)

        def one_head(at, carry):
            group = at // share

            @pl.when(lax.rem(at, share) == 0)
            def _():
                dkeys[...] = jnp.zeros_like(dkeys)
                dvalues[...] = jnp.zeros_like(dvalues)

            for first in (0, half):
                last = first + half
                rows_here = slice(first, last)
                probs = softmax_of(
                    query[rows_here, columns(at)],
                    keys[:last, columns(group)],
                    ids[rows_here, :],
                    key_ids[:, :last],
                    first,
                )
                dprobs = lax.dot_general(
                    dattn[rows_here, columns(at)],
                    values[:last, columns(group)],
                    (((1,), (1,)), ((), ())),
                    preferred_element_type=FLOAT,
                )
                dscores = (
                    probs * (dprobs - jnp.sum(probs * dprobs, axis=-1, keepdims=True))
                ).astype(BFLOAT)
                dquery = scale * jnp.dot(
                    dscores, keys[:last, columns(group)], preferred_element_type=FLOAT
                )
                dqkv[rows_here, columns(at)] = turned(
                    dquery, cosine[rows_here, :], -sine[rows_here, :]
                ).astype(BFLOAT)
                dkeys[:last, :] += lax.dot_general(
                    dscores,
                    query[rows_here, columns(at)],
                    (((0,), (0,)), ((), ())),
                    preferred_element_type=FLOAT,
                )
                dvalues[:last, :] += lax.dot_general(
                    probs.astype(BFLOAT),
                    dattn[rows_here, columns(at)],
                    (((0,), (0,)), ((), ())),
                    preferred_element_type=FLOAT,
                )

            @pl.when(lax.rem(at, share) == share - 1)
            def _():
                dqkv[:, columns(heads + group)] = turned(
                    dkeys[...] * scale, cosine[...], -sine[...]
                ).astype(BFLOAT)
                dqkv[:, columns(heads + kv_heads + group)] = dvalues[...].astype(BFLOAT)

            return carry

        lax.fori_loop(0, heads, one_head, 0)
        bias_term[...] = jnp.sum(dqkv[...].astype(FLOAT), axis=0, keepdims=True)
        for first in range(0, depth, 256):
            span = slice(first, first + 256)
            dnormed[:, span] = lax.dot_general(
                dqkv[...],
                weights[span, :group_width],
                (((1,), (1,)), ((), ())),
                preferred_element_type=FLOAT,
            ).astype(BFLOAT)
            term[span, :group_width] = lax.dot_general(
                normed[:, span], dqkv[...], (((0,), (0,)), ((), ())), preferred_element_type=FLOAT
            )
            term[span, group_width:] = lax.dot_general(
                dbranch[:, span], attn[...], (((0,), (0,)), ((), ())), preferred_element_type=FLOAT
            )
        me = lax.axis_index("dp")
        for side, order in enumerate(orders):
            span = slice(side * width // 2, (side + 1) * width // 2)
            for place in range(devices):
                block = 0
                for at, stride in enumerate(order):
                    bit = (place >> (len(order) - 1 - at)) & 1
                    block = block + lax.rem(me // stride + bit, 2) * stride
                target = near if place < devices // 2 else far
                target[place % (devices // 2), :, span] = term[
                    pl.ds(pl.multiple_of(block * rows, 8), rows), span
                ].astype(BFLOAT)

    vmem = pl.BlockSpec(memory_space=pltpu.VMEM)
    outs = pl.pallas_call(
        body,
        out_shape=[
            jax.ShapeDtypeStruct((count, depth), FLOAT),
            jax.ShapeDtypeStruct((1, depth), FLOAT),
            jax.ShapeDtypeStruct((1, group_width), FLOAT),
            jax.ShapeDtypeStruct((count, depth), BFLOAT),
            jax.ShapeDtypeStruct((devices // 2, rows, width), BFLOAT),
            jax.ShapeDtypeStruct((devices // 2, rows, width), BFLOAT),
        ],
        in_specs=[vmem] * 16,
        out_specs=[vmem] * 6,
        scratch_shapes=[
            pltpu.VMEM((count, depth), BFLOAT),
            pltpu.VMEM((count, query_width), BFLOAT),
            pltpu.VMEM((count, group_width), BFLOAT),
            pltpu.VMEM((count, HD), FLOAT),
            pltpu.VMEM((count, HD), FLOAT),
            pltpu.VMEM((depth, width), FLOAT),
        ],
        compiler_params=pltpu.CompilerParams(vmem_limit_bytes=56 * 2**20),
        cost_estimate=LIGHT,
    )(
        back,
        came,
        hidden,
        cotangent,
        live,
        gain,
        weights,
        normed,
        attn,
        query,
        keys,
        values,
        cosine,
        sine,
        doc_ids[:, None],
        doc_ids[None, :],
    )
    dhidden, gain_term, bias_term, dnormed, near, far = outs
    return (
        dhidden,
        gain_term[0],
        bias_term[0],
        dnormed,
        near,
        far,
    )


def vector_step(param, moment_new, rate):
    return param - rate * moment_new * lax.rsqrt(
        jnp.mean(moment_new * moment_new, axis=-1, keepdims=True) + EPS
    )


def bits_of(count):
    return [1 << bit for bit in range(count.bit_length() - 1)]


def swap(value, axis, stride):
    count = lax.axis_size(axis)
    return lax.ppermute(value, axis, [(at, at ^ stride) for at in range(count)])


def low_add(one, other):
    return (one.astype(FLOAT) + other.astype(FLOAT)).astype(BFLOAT)


def after(value, *others):
    return lax.optimization_barrier((value,) + others)[0]


def by_distance(value, order):
    me = lax.axis_index("dp")
    down = sorted(order, reverse=True)
    bits = len(order)
    value = value.reshape((2,) * bits + (value.shape[0] >> bits,) + value.shape[1:])
    for at, stride in enumerate(down):
        value = jnp.where((me // stride) % 2 == 1, jnp.flip(value, at), value)
    places = [down.index(stride) for stride in order]
    value = value.transpose(tuple(places) + tuple(range(bits, value.ndim)))
    return value.reshape((-1,) + value.shape[bits + 1 :])


def by_index(value, order):
    me = lax.axis_index("dp")
    down = sorted(order, reverse=True)
    bits = len(order)
    value = value.reshape((2,) * bits + (value.shape[0] >> bits,) + value.shape[1:])
    places = [order.index(stride) for stride in down]
    value = value.transpose(tuple(places) + tuple(range(bits, value.ndim)))
    for at, stride in enumerate(down):
        value = jnp.where((me // stride) % 2 == 1, jnp.flip(value, at), value)
    return value.reshape((-1,) + value.shape[bits + 1 :])


def gather_plane(value, strides):
    for stride in reversed(strides):
        value = jnp.concatenate([value, swap(value, "dp", stride)])
    return value


def regroup(value, strides):
    order = tuple(reversed(strides))
    count = value.shape[0]
    value = by_distance(value, order)
    came = [value[:1]] + [swap(value[at : at + 1], "dp", at) for at in range(1, count)]
    return by_distance(jnp.concatenate(came), order)


def halves_by_distance(order):
    me = lax.axis_index("dp")
    down = sorted(order, reverse=True)
    blocks = []
    for place in range(1 << len(order)):
        block = 0
        for at, stride in enumerate(order):
            far = (place >> (len(order) - 1 - at)) & 1
            bit = (me // stride + far) % 2
            block = block + (bit << (len(order) - 1 - down.index(stride)))
        blocks.append(block)
    blocks = jnp.stack(blocks).astype(jnp.int32)
    half = len(order) and (1 << (len(order) - 1))
    return blocks[:half], blocks[half:]


class Chain:
    def __init__(self, kept, sent, order):
        self.kept, self.order = kept, list(order)
        self.send(sent)

    def send(self, sent):
        self.sent = sent
        self.coming = swap(sent, "dp", self.order.pop(0))

    def come(self, *others):
        came = after(self.coming, *others)
        if not self.order:
            self.total = self.kept.astype(FLOAT) + came.astype(FLOAT)
            return self.total
        half = self.kept.shape[0] // 2
        sent = low_add(self.kept[half:], came[half:])
        self.kept = low_add(self.kept[:half], came[:half])
        self.send(sent)
        return sent

    def finish(self, *others):
        while self.order:
            self.come(*others)
            others = ()
        return self.come(*others)


def shards(
    tokens,
    cotangent,
    doc_ids,
    norm_gains,
    qkv_weight,
    qkv_bias,
    out_weight,
    gate_up_weight,
    down_weight,
    gains_moment,
    qkv_moment,
    bias_moment,
    out_moment,
    gate_up_moment,
    down_moment,
):
    rows = qkv_weight.shape[0]
    count = tokens.shape[0]
    query_width = out_weight.shape[1]
    heads = query_width // HD
    group_width = qkv_weight.shape[1]
    kv_heads = (group_width - query_width) // (2 * HD)
    devices = lax.axis_size("dp")
    me = lax.axis_index("dp")
    strides = bits_of(devices)
    every = tuple(strides)
    plane = 4
    near = strides[:2]
    far = tuple(strides[2:])
    units = down_weight.shape[1]
    part = -(-units // (plane * 128)) * 128
    extra = part * plane - units

    def fetch_rows(value, order):
        for stride in reversed(order):
            value = jnp.concatenate([value, swap(value, "dp", stride)])
        return by_index(value, order)

    def split_units(matrix):
        matrix = jnp.pad(matrix, ((0, 0), (0, extra)))
        return matrix.reshape(rows, plane, part).transpose(1, 0, 2)

    def join_units(value):
        value = value.transpose(1, 0, 2).reshape(rows, plane * part)
        return value[:, :units]

    attention_low = jnp.concatenate([qkv_weight.astype(BFLOAT), out_weight.astype(BFLOAT)], axis=1)
    unit_weights = jnp.concatenate(
        [split_units(one.astype(BFLOAT)) for one in (gate_up_weight[0], gate_up_weight[1], down_weight)],
        axis=2,
    )
    live = (doc_ids >= 0).astype(FLOAT)
    grad_out = cotangent.astype(FLOAT) * live[:, None]
    grad_low = grad_out.astype(BFLOAT)
    near_blocks, far_blocks = halves_by_distance(far)
    positions = positions_of(doc_ids)
    freq = THETA ** (-(2.0 / HD) * jnp.arange(HD // 2, dtype=FLOAT))
    angle = positions.astype(FLOAT)[:, None] * freq[None, :]
    cosine = jnp.cos(angle)
    sine = jnp.sin(angle)
    cosine_two = jnp.concatenate([cosine, cosine], axis=1)
    sine_two = jnp.concatenate([-sine, sine], axis=1)
    inputs = tokens.astype(FLOAT)
    scale_one = rms_scale(inputs)
    if rows % 16 == 0:
        (
            normed,
            hidden1,
            attn,
            query,
            keys,
            values,
            attention_full,
            ffn_full,
            normed2_all,
            grad_all,
        ) = forward_part(
            tokens,
            norm_gains,
            qkv_bias,
            cosine_two,
            sine_two,
            doc_ids,
            attention_low,
            unit_weights,
            grad_low,
            devices,
            heads,
            kv_heads,
        )
    else:
        attention_full = fetch_rows(attention_low, every)
        ffn_full = fetch_rows(regroup(unit_weights, near).reshape(plane * rows, -1), far)
        normed = (inputs * scale_one * norm_gains[0]).astype(BFLOAT)
        qkv = contract(normed, attention_full[:, :group_width], 1, 0) + qkv_bias
        attn, query, keys, values = attend(qkv, cosine_two, sine_two, doc_ids, heads, kv_heads)
        branch = contract(attn, attention_full[:, group_width:], 1, 1).astype(BFLOAT)
        hidden1 = inputs + (branch.astype(FLOAT) + swap(branch, "tensor", 1).astype(FLOAT))
        normed2_all = gather_plane(
            (hidden1 * rms_scale(hidden1) * norm_gains[1]).astype(BFLOAT), near
        )
        grad_all = gather_plane(grad_low, near)
    gate, up, hid, normed2_rows, grad_rows = hidden_units(normed2_all, grad_all, ffn_full)
    down_sent = weight_term(grad_rows, hid, far_blocks, 0, part)
    down_kept = weight_term(grad_rows, after(hid, down_sent), near_blocks, 0, part)
    down_chain = Chain(down_kept, down_sent, far)
    both = hidden_back(after(grad_all, down_kept), ffn_full, gate, up)
    gate_sent = weight_term(normed2_rows, both, far_blocks, 0, part)
    up_sent = weight_term(after(normed2_rows, gate_sent), both, far_blocks, 1, part)
    down_sent = down_chain.come(up_sent)
    both = after(both, down_sent)
    half = plane * count // 2
    back_sent = rows_by_width(both, ffn_full, (0, 1), half, 2 * half)
    back_kept = rows_by_width(after(both, back_sent), ffn_full, (0, 1), 0, half)
    back_chain = Chain(back_kept, back_sent, near)
    back_sent = back_chain.come(back_kept)
    gate_kept = weight_term(after(normed2_rows, back_sent), both, near_blocks, 0, part)
    gate_chain = Chain(gate_kept, gate_sent, far)
    gate_sent = gate_chain.come(gate_kept)
    up_kept = weight_term(after(normed2_rows, gate_sent), both, near_blocks, 1, part)
    up_chain = Chain(up_kept, up_sent, far)
    back = back_chain.come(up_kept).astype(BFLOAT)
    back_came = swap(back, "tensor", 1)
    layer_sent = rows_by_width(after(hid, back), ffn_full, (2,), half, 2 * half)
    layer_kept = rows_by_width(after(hid, layer_sent), ffn_full, (2,), 0, half)
    layer_chain = Chain(layer_kept, layer_sent, near)
    layer_sent = layer_chain.come(layer_kept)
    down_total = down_chain.finish(layer_sent)
    up_sent = up_chain.come(down_total)

    def own_rows(value):
        return join_units(regroup(value.astype(BFLOAT).reshape(plane, rows, part), near)).astype(FLOAT)

    down_shard = own_rows(down_total)
    dhidden1, gain_two, bias_term, dnormed, kept, sent = backward_part(
        back,
        after(back_came, up_sent),
        hidden1,
        cotangent,
        live[:, None],
        norm_gains[1:2],
        attention_full,
        normed,
        attn,
        query,
        keys,
        values,
        cosine_two,
        sine_two,
        doc_ids,
        devices,
        HALVES if devices == 16 else (every, every),
    )
    dnormed_came = swap(dnormed, "tensor", 1)
    if devices == 16:
        gate_total = gate_chain.finish(dnormed)
        layer = layer_chain.come(gate_total).astype(BFLOAT)
        layer_came = swap(layer, "tensor", 1)
        up_total = up_chain.finish(layer)
        pieces = jnp.stack([gate_total, up_total]).astype(BFLOAT)
        attention_shard, joined = exchange(kept, sent, pieces.reshape(2, plane, rows, part))
        layer_came = after(layer_came, attention_shard)
        attention_shard = after(attention_shard, layer_came)
        joined = joined[:, :, :units].astype(FLOAT)
        gate_shard, up_shard = joined[0], joined[1]
        token = attention_shard
    else:
        chain = Chain(kept.reshape(-1, kept.shape[2]), sent.reshape(-1, sent.shape[2]), every)
        gate_total, up_total = gate_chain.finish(dnormed), up_chain.finish(dnormed)
        gate_shard, up_shard = own_rows(gate_total), own_rows(up_total)
        layer = layer_chain.come(up_total).astype(BFLOAT)
        layer_came = swap(layer, "tensor", 1)
        token = attention_shard = chain.finish(layer)
    dnormed = dnormed.astype(FLOAT) + after(dnormed_came, token).astype(FLOAT)
    qkv_shard = attention_shard[:, :group_width]
    out_shard = attention_shard[:, group_width:]
    tokens_grad = dhidden1 + norm_back(dnormed, inputs, scale_one, norm_gains[0])
    gain_one = jnp.sum(dnormed * inputs * scale_one, axis=0)
    gate_up_shard = jnp.stack([gate_shard, up_shard])
    qkv_m = MOMENTUM * qkv_moment + qkv_shard
    out_m = MOMENTUM * out_moment + out_shard
    gate_up_m = MOMENTUM * gate_up_moment + gate_up_shard
    down_m = MOMENTUM * down_moment + down_shard
    wire = BFLOAT if rows % 16 == 0 else FLOAT
    pair = query_width + (group_width - query_width) // 2
    vectors = jnp.concatenate([gain_one, gain_two, bias_term])
    solved, vectors = orthogonalize(
        jnp.concatenate(
            [gate_up_m[0], gate_up_m[1], down_m, qkv_m[:, :pair], out_m, qkv_m[:, pair:]], axis=1
        ).astype(wire),
        vectors.reshape(-1, 128),
        query_width,
        devices,
    )
    vectors = vectors.reshape(-1)
    gains_grad = vectors[: 2 * inputs.shape[1]].reshape(2, -1)
    bias_grad = vectors[2 * inputs.shape[1] :]
    gains_m = MOMENTUM * gains_moment + gains_grad
    bias_m = MOMENTUM * bias_moment + bias_grad
    layer_out = hidden1 + (layer.astype(FLOAT) + layer_came.astype(FLOAT))
    gate_up_update = jnp.stack([solved[:, :units], solved[:, units : 2 * units]]).astype(FLOAT)
    down_update = solved[:, 2 * units : 3 * units].astype(FLOAT)
    last = solved[:, 3 * units :].astype(FLOAT)
    qkv_update = jnp.concatenate([last[:, :pair], last[:, pair + query_width :]], axis=1)
    out_update = last[:, pair : pair + query_width]
    gains_new = vector_step(norm_gains, gains_m, LR_VECTOR)
    bias_new = vector_step(qkv_bias, bias_m, LR_BIAS)
    return (
        layer_out,
        tokens_grad,
        gains_grad,
        qkv_shard,
        bias_grad,
        out_shard,
        gate_up_shard,
        down_shard,
        gains_new,
        qkv_weight - LR_MATRIX * qkv_update,
        bias_new,
        out_weight - LR_OUT * out_update,
        gate_up_weight - LR_MATRIX * gate_up_update,
        down_weight - LR_MATRIX * down_update,
        gains_m,
        qkv_m,
        bias_m,
        out_m,
        gate_up_m,
        down_m,
    )


def solution(mesh):
    placed = (
        P("dp", None),
        P("dp", None),
        P("dp"),
        P(),
        P("dp", "tensor"),
        P("tensor"),
        P("dp", "tensor"),
        P(None, "dp", "tensor"),
        P("dp", "tensor"),
        P(),
        P("dp", "tensor"),
        P("tensor"),
        P("dp", "tensor"),
        P(None, "dp", "tensor"),
        P("dp", "tensor"),
    )
    return jax.shard_map(
        shards,
        mesh=mesh,
        in_specs=placed,
        out_specs=(
            P("dp", None),
            P("dp", None),
            P(),
            P("dp", "tensor"),
            P("tensor"),
            P("dp", "tensor"),
            P(None, "dp", "tensor"),
            P("dp", "tensor"),
            P(),
            P("dp", "tensor"),
            P("tensor"),
            P("dp", "tensor"),
            P(None, "dp", "tensor"),
            P("dp", "tensor"),
            P(),
            P("dp", "tensor"),
            P("tensor"),
            P("dp", "tensor"),
            P(None, "dp", "tensor"),
            P("dp", "tensor"),
        ),
        check_vma=False,
    )
```

```python
import functools

import jax
import jax.numpy as jnp
from jax import lax
from jax.experimental import pallas as pl
from jax.experimental.pallas import tpu as pltpu
from jax.sharding import PartitionSpec as P

HD = 128
FFB = 896
NSI = 5


EPS = 1e-06
THETA = 1000000.0
MOMENTUM = 0.5
LR_MATRIX = 0.2
LR_OUT = 0.8
LR_VECTOR = 0.1
LR_BIAS = 1.0
NS_A = 3.4445
NS_B = -4.775
NS_C = 2.0315
FLOAT = jnp.float32
BFLOAT = jnp.bfloat16


def contract(left, right, left_dim, right_dim):
    return lax.dot_general(
        left, right, (((left_dim,), (right_dim,)), ((), ())), preferred_element_type=FLOAT
    )


def positions_of(block_ids):
    index = jnp.arange(block_ids.shape[0], dtype=jnp.int32)
    change = jnp.concatenate([jnp.ones((1,), dtype=bool), block_ids[1:] != block_ids[:-1]])
    start = lax.cummax(jnp.where(change, index, jnp.zeros_like(index)), axis=0)
    return index - start


def rms_scale(values):
    return lax.rsqrt(jnp.mean(values * values, axis=-1, keepdims=True) + EPS)


def norm_back(grad, values, scale, gain):
    scaled = grad * gain
    return scale * scaled - values * scale * scale * scale * jnp.mean(
        scaled * values, axis=-1, keepdims=True
    )


def solve(width, split, depth, wide, tall, tall_low, gram, poly):
    tile = width // 2
    chunk = depth // 3

    def both(sums):
        if split:
            return sums
        total = sums[0] + sums[1]
        return total, total

    def squares(part):
        return jnp.sum(part[:tile] * part[:tile]), jnp.sum(part[tile:] * part[tile:])

    def rows_of(pair, columns):
        if not split:
            return pair[0]
        at = lax.broadcasted_iota(jnp.int32, (width, columns), 0)
        return jnp.where(at < tile, pair[0], pair[1])

    sums = (jnp.float32(0), jnp.float32(0))
    for at in range(3):
        part = wide[at * chunk : (at + 1) * chunk, :width].T
        tall[:width, at * chunk : (at + 1) * chunk] = part
        found = squares(part)
        sums = (sums[0] + found[0], sums[1] + found[1])
    sums = both(sums)
    inverse = tuple(1.0 / (jnp.sqrt(one) + 1e-07) for one in sums)
    factor = rows_of(inverse, chunk)
    for at in range(3):
        part = tall[:width, at * chunk : (at + 1) * chunk] * factor
        tall[:width, at * chunk : (at + 1) * chunk] = part
        tall_low[:width, at * chunk : (at + 1) * chunk] = part.astype(BFLOAT)
    start = tuple(one * by * by for one, by in zip(sums, inverse))

    def step(turn, sums):
        shifts = tuple(one / (tile if split else width) for one in sums)
        for at in range(2):
            mine = slice(at * tile, (at + 1) * tile)
            product = lax.dot_general(
                tall_low[mine, :],
                tall_low[:width, :],
                (((1,), (1,)), ((), ())),
                preferred_element_type=FLOAT,
            )
            row = lax.broadcasted_iota(jnp.int32, (tile, width), 0) + at * tile
            column = lax.broadcasted_iota(jnp.int32, (tile, width), 1)
            product = jnp.where(row == column, product - shifts[at], product)
            if split:
                product = jnp.where((column < tile) == (at == 0), product, 0.0)
            gram[mine, :width] = product.astype(BFLOAT)
        for at in range(2):
            mine = slice(at * tile, (at + 1) * tile)
            product = jnp.dot(
                gram[mine, :width], gram[:width, :width], preferred_element_type=FLOAT
            )
            linear = NS_B + 2.0 * NS_C * shifts[at]
            poly[mine, :width] = (
                linear * gram[mine, :width].astype(FLOAT) + NS_C * product
            ).astype(BFLOAT)
        factor = rows_of(tuple(NS_A + NS_B * s + NS_C * s * s for s in shifts), chunk)
        sums = (jnp.float32(0), jnp.float32(0))
        for at in range(3):
            span = slice(at * chunk, (at + 1) * chunk)
            part = factor * tall[:width, span] + jnp.dot(
                poly[:width, :width], tall_low[:width, span], preferred_element_type=FLOAT
            )
            tall[:width, span] = part
            tall_low[:width, span] = part.astype(BFLOAT)
            found = squares(part)
            sums = (sums[0] + found[0], sums[1] + found[1])
        return both(sums)

    lax.fori_loop(0, NSI, step, start)
    for at in range(3):
        wide[at * chunk : (at + 1) * chunk, :width] = tall[
            :width, at * chunk : (at + 1) * chunk
        ].T


def muon_kernel(
    devices,
    rows,
    blocks,
    query_width,
    keeper,
    units,
    vectors,
    units_new,
    vectors_sum,
    all_vectors,
    first,
    second,
    first_back,
    second_back,
    wide,
    tall,
    tall_low,
    gram,
    poly,
    here_sem,
    go_sem,
    come_sem,
    back_sem,
    home_sem,
    go_vector,
    come_vector,
):
    me = lax.axis_index("dp")
    depth = devices * rows
    mine = jnp.where(me < keeper, me, me - 1)
    keeps = me == keeper
    holds = jnp.logical_and(me != keeper, mine < blocks)
    key_width = FFB - query_width

    def block_of(device):
        return jnp.where(device < keeper, device, device - 1)

    def owner_of(block):
        return jnp.where(block < keeper, block, block + 1)

    def rows_of(array, unit):
        return array.at[:, pl.ds(pl.multiple_of(unit * FFB, 128), FFB)]

    def remote(source, target, send, receive, device):
        return pltpu.make_async_remote_copy(
            src_ref=source,
            dst_ref=target,
            send_sem=send,
            recv_sem=receive,
            device_id={"dp": device},
            device_id_type=pl.DeviceIdType.MESH,
        )

    def others(body):
        def step(turn, carry):
            body(lax.rem(me + turn, devices))
            return carry

        lax.fori_loop(1, devices, step, 0)

    barrier = pltpu.get_barrier_semaphore()

    def greet(device):
        pl.semaphore_signal(
            barrier, inc=1, device_id={"dp": device}, device_id_type=pl.DeviceIdType.MESH
        )

    others(greet)
    pl.semaphore_wait(barrier, devices - 1)

    def way_in(unit, at, sender, device):
        return remote(
            rows_of(units, unit),
            (first, second)[at].at[sender],
            go_sem.at[device, at],
            come_sem.at[sender, at],
            device,
        )

    def to_keeper(what):
        @pl.when(jnp.logical_not(keeps))
        def _():
            what(way_in(blocks, 0, me, keeper))
            what(way_in(blocks + 1, 1, me, keeper))

    def to_owner(device, what):
        @pl.when(jnp.logical_and(device != keeper, block_of(device) < blocks))
        def _():
            what(way_in(block_of(device), 0, me, device))

    def share(sender, device):
        return remote(
            vectors, all_vectors.at[sender], go_vector.at[device], come_vector.at[sender], device
        )

    to_keeper(lambda copy: copy.start())
    others(lambda device: to_owner(device, lambda copy: copy.start()))
    others(lambda device: share(me, device).start())

    def own_in(what):
        @pl.when(keeps)
        def _():
            what(pltpu.make_async_copy(rows_of(units, blocks), first.at[me], here_sem.at[0]))
            what(pltpu.make_async_copy(rows_of(units, blocks + 1), second.at[me], here_sem.at[1]))

        @pl.when(holds)
        def _():
            what(pltpu.make_async_copy(rows_of(units, mine), first.at[me], here_sem.at[0]))

    own_in(lambda copy: copy.start())
    own_in(lambda copy: copy.wait())

    def arrived(device):
        @pl.when(jnp.logical_or(keeps, holds))
        def _():
            way_in(0, 0, device, me).wait_recv()

        @pl.when(keeps)
        def _():
            way_in(0, 1, device, me).wait_recv()

    others(arrived)

    def load(buffer, source_at, size, target_at):
        def step(at, carry):
            wide[pl.ds(pl.multiple_of(at * rows, 8), rows), target_at : target_at + size] = buffer[
                at, :, source_at : source_at + size
            ].astype(FLOAT)
            return carry

        lax.fori_loop(0, devices, step, 0)

    def store(buffer, source_at, size, target_at):
        def step(at, carry):
            buffer[at, :, target_at : target_at + size] = wide[
                pl.ds(pl.multiple_of(at * rows, 8), rows), source_at : source_at + size
            ].astype(buffer.dtype)
            return carry

        lax.fori_loop(0, devices, step, 0)

    def way_back(unit, at, device):
        return remote(
            (first_back, second_back)[at].at[device],
            rows_of(units_new, unit),
            back_sem.at[device, at],
            home_sem.at[unit],
            device,
        )

    def own_back(unit, at):
        return pltpu.make_async_copy(
            (first_back, second_back)[at].at[me], rows_of(units_new, unit), here_sem.at[at]
        )

    @pl.when(holds)
    def _():
        load(first, 0, FFB, 0)
        solve(FFB, False, depth, wide, tall, tall_low, gram, poly)
        store(first_back, 0, FFB, 0)
        others(lambda device: way_back(mine, 0, device).start())
        own_back(mine, 0).start()
        own_back(mine, 0).wait()

    @pl.when(keeps)
    def _():
        load(first, query_width, key_width, 0)
        load(second, query_width, key_width, key_width)
        solve(2 * key_width, True, depth, wide, tall, tall_low, gram, poly)
        store(first_back, 0, key_width, query_width)
        store(second_back, key_width, key_width, query_width)
        for at, buffer, back in ((0, first, first_back), (1, second, second_back)):
            load(buffer, 0, query_width, 0)
            solve(query_width, False, depth, wide, tall, tall_low, gram, poly)
            store(back, 0, query_width, 0)
            others(lambda device: way_back(blocks + at, at, device).start())
            own_back(blocks + at, at).start()
        own_back(blocks, 0).wait()
        own_back(blocks + 1, 1).wait()

    own_vectors = pltpu.make_async_copy(vectors, all_vectors.at[me], here_sem.at[2])
    own_vectors.start()
    own_vectors.wait()
    others(lambda device: share(device, me).wait_recv())
    vectors_sum[...] = lax.fori_loop(
        1, devices, lambda at, total: total + all_vectors[at], all_vectors[0]
    )
    others(lambda device: share(me, device).wait_send())

    def home(block, carry):
        @pl.when(owner_of(block) != me)
        def _():
            way_back(block, 0, me).wait_recv()

        return carry

    lax.fori_loop(0, blocks, home, 0)

    @pl.when(jnp.logical_not(keeps))
    def _():
        way_back(blocks, 0, me).wait_recv()
        way_back(blocks + 1, 1, me).wait_recv()

    to_keeper(lambda copy: copy.wait_send())
    others(lambda device: to_owner(device, lambda copy: copy.wait_send()))

    @pl.when(jnp.logical_or(keeps, holds))
    def _():
        others(lambda device: way_back(0, 0, device).wait_send())

    @pl.when(keeps)
    def _():
        others(lambda device: way_back(0, 1, device).wait_send())


def orthogonalize(units, vectors, query_width, devices):
    rows = units.shape[0]
    blocks = units.shape[1] // FFB - 2
    depth = devices * rows
    wire = units.dtype
    kernel = functools.partial(
        muon_kernel, devices, rows, blocks, query_width, min(devices // 2, blocks)
    )
    hbm = pl.BlockSpec(memory_space=pltpu.HBM)
    return pl.pallas_call(
        kernel,
        out_shape=[
            jax.ShapeDtypeStruct(units.shape, wire),
            jax.ShapeDtypeStruct(vectors.shape, FLOAT),
        ],
        in_specs=[hbm, pl.BlockSpec(memory_space=pltpu.VMEM)],
        out_specs=[hbm, pl.BlockSpec(memory_space=pltpu.VMEM)],
        scratch_shapes=[
            pltpu.VMEM((devices,) + vectors.shape, FLOAT),
            pltpu.VMEM((devices, rows, FFB), wire),
            pltpu.VMEM((devices, rows, FFB), wire),
            pltpu.VMEM((devices, rows, FFB), wire),
            pltpu.VMEM((devices, rows, FFB), wire),
            pltpu.VMEM((depth, FFB), FLOAT),
            pltpu.VMEM((FFB, depth), FLOAT),
            pltpu.VMEM((FFB, depth), BFLOAT),
            pltpu.VMEM((FFB, FFB), BFLOAT),
            pltpu.VMEM((FFB, FFB), BFLOAT),
            pltpu.SemaphoreType.DMA((3,)),
            pltpu.SemaphoreType.DMA((devices, 2)),
            pltpu.SemaphoreType.DMA((devices, 2)),
            pltpu.SemaphoreType.DMA((devices, 2)),
            pltpu.SemaphoreType.DMA((blocks + 2,)),
            pltpu.SemaphoreType.DMA((devices,)),
            pltpu.SemaphoreType.DMA((devices,)),
        ],
        compiler_params=pltpu.CompilerParams(
            collective_id=0, has_side_effects=True, vmem_limit_bytes=52 * 2**20
        ),
        cost_estimate=pl.CostEstimate(
            flops=64 * 10**9, bytes_accessed=16 * 2**20, transcendentals=0
        ),
    )(units, vectors)


LIGHT = pl.CostEstimate(flops=1024, bytes_accessed=1024, transcendentals=0)


def call_light(body, grid, ins, outs):
    return pl.pallas_call(
        body,
        grid=grid,
        in_specs=[pl.BlockSpec(block, at) for _, block, at in ins],
        out_specs=[pl.BlockSpec(block, at) for _, _, block, at in outs],
        out_shape=[jax.ShapeDtypeStruct(shape, dtype) for shape, dtype, _, _ in outs],
        compiler_params=pltpu.CompilerParams(vmem_limit_bytes=56 * 2**20),
        cost_estimate=LIGHT,
    )(*[array for array, _, _ in ins])


def spans(size, step):
    return [slice(at, min(at + step, size)) for at in range(0, size, step)]


def hidden_units(tokens, grads, weights, block=256):
    count, depth = tokens.shape
    part = weights.shape[1] // 3

    def body(x, y, w_gate, w_up, gate, up, hid, turned_x, turned_y):
        turned_x[...] = x[...].astype(FLOAT).T.astype(BFLOAT)
        turned_y[...] = y[...].astype(FLOAT).T.astype(BFLOAT)
        for span in spans(part, 512):
            g = jnp.dot(x[...], w_gate[:, span], preferred_element_type=FLOAT)
            u = jnp.dot(x[...], w_up[:, span], preferred_element_type=FLOAT)
            gate[:, span] = g
            up[:, span] = u
            hid[:, span] = (g * jax.nn.sigmoid(g) * u).astype(BFLOAT)

    rows = lambda at: (at, 0)
    columns = lambda at: (0, at)
    return call_light(
        body,
        (count // block,),
        [
            (tokens, (block, depth), rows),
            (grads, (block, depth), rows),
            (weights, (depth, part), lambda at: (0, 0)),
            (weights, (depth, part), lambda at: (0, 1)),
        ],
        [
            ((count, part), FLOAT, (block, part), rows),
            ((count, part), FLOAT, (block, part), rows),
            ((count, part), BFLOAT, (block, part), rows),
            ((depth, count), BFLOAT, (depth, block), columns),
            ((depth, count), BFLOAT, (depth, block), columns),
        ],
    )


def hidden_back(grads, weights, gate, up, block=256):
    count, depth = grads.shape
    part = weights.shape[1] // 3

    def body(x, w, gate, up, both):
        for span in spans(part, 512):
            dhid = jnp.dot(x[...], w[:, span], preferred_element_type=FLOAT)
            g = gate[:, span]
            sigma = jax.nn.sigmoid(g)
            both[:, span] = (dhid * up[:, span] * sigma * (1.0 + g * (1.0 - sigma))).astype(BFLOAT)
            both[:, part + span.start : part + span.stop] = (dhid * (g * sigma)).astype(BFLOAT)

    rows = lambda at: (at, 0)
    return call_light(
        body,
        (count // block,),
        [
            (grads, (block, depth), rows),
            (weights, (depth, part), lambda at: (0, 2)),
            (gate, (block, part), rows),
            (up, (block, part), rows),
        ],
        [((count, 2 * part), BFLOAT, (block, 2 * part), rows)],
    )[0]


def rows_by_width(units, weights, places, first, last, block=256):
    width = weights.shape[0]
    part = weights.shape[1] // 3

    def body(x, *refs):
        out = refs[-1]
        for span in spans(width, 512):
            out[:, span] = sum(
                lax.dot_general(
                    x[:, at * part : (at + 1) * part],
                    refs[at][span, :],
                    (((1,), (1,)), ((), ())),
                    preferred_element_type=FLOAT,
                )
                for at in range(len(places))
            ).astype(BFLOAT)

    def column(place):
        return (weights, (width, part), lambda at: (0, place))

    return call_light(
        body,
        ((last - first) // block,),
        [(units, (block, len(places) * part), lambda at: (at + first // block, 0))]
        + [column(place) for place in places],
        [((last - first, width), BFLOAT, (block, width), lambda at: (at, 0))],
    )[0]


def weight_term(left, right, blocks, place, width):
    count = left.shape[1]
    picked = blocks.shape[0]
    tall = left.shape[0] // (2 * picked)

    def body(blocks, x, y, out):
        for span in spans(width, 512):
            out[:, span] = jnp.dot(
                x[...], y[:, span], preferred_element_type=FLOAT
            ).astype(BFLOAT)

    return pl.pallas_call(
        body,
        grid_spec=pltpu.PrefetchScalarGridSpec(
            num_scalar_prefetch=1,
            grid=(picked,),
            in_specs=[
                pl.BlockSpec((tall, count), lambda at, blocks: (blocks[at], 0)),
                pl.BlockSpec((count, width), lambda at, blocks: (0, place)),
            ],
            out_specs=pl.BlockSpec((tall, width), lambda at, blocks: (at, 0)),
        ),
        out_shape=jax.ShapeDtypeStruct((picked * tall, width), BFLOAT),
        compiler_params=pltpu.CompilerParams(vmem_limit_bytes=48 * 2**20),
        cost_estimate=LIGHT,
    )(blocks, left, right)


def turned(value, cosine, sine):
    return value * cosine + pltpu.roll(value, HD // 2, 1) * sine


def softmax_of(query, keys, ids, key_ids, first):
    scores = lax.dot_general(
        query, keys, (((1,), (1,)), ((), ())), preferred_element_type=FLOAT
    ) * (HD ** (-0.5))
    row = lax.broadcasted_iota(jnp.int32, scores.shape, 0) + first
    column = lax.broadcasted_iota(jnp.int32, scores.shape, 1)
    scores = jnp.where((ids == key_ids) & (column <= row), scores, -1e30)
    expo = jnp.exp(scores - jnp.max(scores, axis=-1, keepdims=True))
    return expo / jnp.sum(expo, axis=-1, keepdims=True)


def attend(qkv, cosine, sine, doc_ids, heads, kv_heads):
    count = qkv.shape[0]
    share = heads // kv_heads
    half = count // 2

    def body(q, k, v, cosine, sine, ids, key_ids, attn, query, keys, values):
        query[...] = turned(q[...], cosine[...], sine[...]).astype(BFLOAT)
        keys[...] = turned(k[...], cosine[...], sine[...]).astype(BFLOAT)
        values[...] = v[...].astype(BFLOAT)
        for first in (0, half):
            last = first + half
            probs = softmax_of(
                query[first:last, :], keys[:last, :], ids[first:last, :], key_ids[:, :last], first
            )
            attn[first:last, :] = jnp.dot(
                probs.astype(BFLOAT), values[:last, :], preferred_element_type=FLOAT
            ).astype(BFLOAT)

    one = lambda at: (0, 0)
    head = lambda at: (0, at)
    group = lambda at: (0, at // share)
    block = (count, HD)
    return pl.pallas_call(
        body,
        grid=(heads,),
        in_specs=[
            pl.BlockSpec(block, head),
            pl.BlockSpec(block, lambda at: (0, heads + at // share)),
            pl.BlockSpec(block, lambda at: (0, heads + kv_heads + at // share)),
            pl.BlockSpec(block, one),
            pl.BlockSpec(block, one),
            pl.BlockSpec((count, 1), one),
            pl.BlockSpec((1, count), one),
        ],
        out_specs=[
            pl.BlockSpec(block, head),
            pl.BlockSpec(block, head),
            pl.BlockSpec(block, group),
            pl.BlockSpec(block, group),
        ],
        out_shape=[
            jax.ShapeDtypeStruct((count, heads * HD), BFLOAT),
            jax.ShapeDtypeStruct((count, heads * HD), BFLOAT),
            jax.ShapeDtypeStruct((count, kv_heads * HD), BFLOAT),
            jax.ShapeDtypeStruct((count, kv_heads * HD), BFLOAT),
        ],
        compiler_params=pltpu.CompilerParams(vmem_limit_bytes=32 * 2**20),
        cost_estimate=LIGHT,
    )(qkv, qkv, qkv, cosine, sine, doc_ids[:, None], doc_ids[None, :])


def forward_kernel(
    devices,
    heads,
    kv_heads,
    tokens,
    gains,
    bias,
    cosine,
    sine,
    ids,
    key_ids,
    shard,
    units,
    grads,
    normed,
    hidden,
    attn,
    query,
    keys,
    values,
    attention_out,
    ffn_full,
    tokens_all,
    grads_all,
    attention_full,
    qkv,
    branch,
    branch_came,
    normed_two,
    here_sem,
    z_send,
    z_come,
    x_send,
    x_come,
    core_send,
    core_come,
    group_send,
    group_come,
    right_send,
    left_send,
    plane_come,
    pair_send,
    pair_come,
):
    me = lax.axis_index("dp")
    side = lax.axis_index("tensor")
    planes = devices // 4
    rows = shard.shape[0]
    count = tokens.shape[0]
    place, plane = lax.rem(me, 4), me // 4
    across = me + 2 - 4 * (place // 2)
    beside = me + 1 - 2 * lax.rem(me, 2)
    part = ffn_full.shape[1] // 3
    share = heads // kv_heads
    depth = tokens.shape[1]
    half = count // 2

    def remote(source, target, send, come, device):
        return pltpu.make_async_remote_copy(
            src_ref=source,
            dst_ref=target,
            send_sem=send,
            recv_sem=come,
            device_id={"dp": device},
            device_id_type=pl.DeviceIdType.MESH,
        )

    def loop(first, last, body):
        def step(turn, carry):
            body(turn)
            return carry

        lax.fori_loop(first, last, step, 0)

    barrier = pltpu.get_barrier_semaphore()

    def greet(where):
        pl.semaphore_signal(barrier, inc=1, device_id=where, device_id_type=pl.DeviceIdType.MESH)

    def peer(turn):
        return lax.rem(plane + turn, planes) * 4 + place

    def plane_peer(turn):
        return plane * 4 + lax.rem(place + turn, 4)

    loop(1, planes, lambda turn: greet({"dp": peer(turn)}))
    loop(1, 4, lambda turn: greet({"dp": plane_peer(turn)}))
    greet({"tensor": 1 - side})
    pl.semaphore_wait(barrier, planes + 3)

    def block(owner):
        return attention_full.at[pl.ds(pl.multiple_of(owner * rows, 16), rows)]

    def owner_at(turn):
        return lax.rem(plane + planes - turn, planes) * 4

    def to_column(turn):
        return remote(shard, block(me), z_send.at[turn], z_come.at[turn], peer(turn))

    def from_column(turn):
        owner = owner_at(turn) + place
        return remote(block(owner), block(owner), z_send.at[turn], z_come.at[turn], me)

    def x_copy(turn):
        owner = owner_at(turn) + place
        return remote(block(owner), block(owner), x_send.at[turn], x_come.at[turn], across)

    def x_wait(turn):
        owner = owner_at(turn) + lax.rem(across, 4)
        return remote(block(owner), block(owner), x_send.at[turn], x_come.at[turn], across)

    def core_copy(turn, far):
        owner = owner_at(turn) + (lax.rem(across, 4) if far else place)
        return remote(
            block(owner), block(owner), core_send.at[turn, far], core_come.at[turn, far], beside
        )

    def core_wait(turn, far):
        owner = owner_at(turn) + lax.rem(beside, 4) + (2 - 4 * (place // 2) if far else 0)
        return remote(
            block(owner), block(owner), core_send.at[turn, far], core_come.at[turn, far], beside
        )

    def third_of(owner, third):
        return ffn_full.at[
            pl.ds(pl.multiple_of(owner * rows, 16), rows), third * part : (third + 1) * part
        ]

    def group_copy(turn, third):
        return remote(
            units.at[lax.rem(place + turn, 4), :, third * part : (third + 1) * part],
            third_of(me, third),
            group_send.at[turn, third],
            group_come.at[turn, third],
            plane_peer(turn),
        )

    def group_wait(turn, third):
        owner = plane * 4 + lax.rem(place + 4 - turn, 4)
        return remote(
            third_of(owner, third),
            third_of(owner, third),
            group_send.at[turn, third],
            group_come.at[turn, third],
            me,
        )

    def slab(origin, third):
        return ffn_full.at[
            pl.ds(pl.multiple_of(origin * 4 * rows, 16), 4 * rows), third * part : (third + 1) * part
        ]

    def move(origin, third, right):
        send = right_send if right else left_send
        return remote(
            slab(origin, third),
            slab(origin, third),
            send.at[origin, third],
            plane_come.at[origin, third],
            me + 4 if right else me - 4,
        )

    def pump(hop, third):
        behind, ahead = plane - hop, plane + hop

        @pl.when(behind >= 0)
        def _():
            move(behind, third, True).wait_recv()

            @pl.when(plane < planes - 1)
            def _():
                move(behind, third, True).start()

        @pl.when(ahead < planes)
        def _():
            move(ahead, third, False).wait_recv()

            @pl.when(plane > 0)
            def _():
                move(ahead, third, False).start()

    def x_rows(array, at):
        return remote(
            array.at[0:count], array.at[count : 2 * count], pair_send.at[at], pair_come.at[at], across
        )

    def core_rows(array, at):
        return remote(
            array.at[0 : 2 * count],
            array.at[2 * count : 4 * count],
            pair_send.at[at],
            pair_come.at[at],
            beside,
        )

    loop(1, planes, lambda turn: to_column(turn).start())
    own_block = pltpu.make_async_copy(shard, block(me), here_sem.at[0])
    own_block.start()
    for third in range(3):
        loop(1, 4, lambda turn: group_copy(turn, third).start())
    own_units = pltpu.make_async_copy(
        units.at[place], ffn_full.at[pl.ds(pl.multiple_of(me * rows, 16), rows)], here_sem.at[1]
    )
    own_units.start()
    own_grads = pltpu.make_async_copy(grads, grads_all.at[0:count], here_sem.at[2])
    own_grads.start()

    def norm(value, gain):
        scale = lax.rsqrt(jnp.mean(value * value, axis=-1, keepdims=True) + EPS)
        return (value * scale * gain).astype(BFLOAT)

    for first in range(0, count, 128):
        normed[first : first + 128, :] = norm(
            tokens[first : first + 128, :].astype(FLOAT), gains[0:1, :]
        )

    def slabs(third):
        loop(1, 4, lambda turn: group_wait(turn, third).wait_recv())

        @pl.when(plane < planes - 1)
        def _():
            move(plane, third, True).start()

        @pl.when(plane > 0)
        def _():
            move(plane, third, False).start()

    own_units.wait()
    slabs(0)
    own_block.wait()
    x_copy(0).start()
    core_copy(0, 0).start()

    def forward(turn):
        from_column(turn).wait_recv()
        x_copy(turn).start()
        core_copy(turn, 0).start()

    loop(1, planes, forward)
    slabs(1)
    slabs(2)
    own_grads.wait()
    x_rows(grads_all, 0).start()

    def forward_far(turn):
        x_wait(turn).wait_recv()
        core_copy(turn, 1).start()

    loop(0, planes, forward_far)
    pump(1, 0)

    def arrive(turn):
        core_wait(turn, 0).wait_recv()
        core_wait(turn, 1).wait_recv()

    loop(0, planes, arrive)
    attention_copy = pltpu.make_async_copy(attention_full, attention_out, here_sem.at[0])
    attention_copy.start()

    query_width = heads * HD
    group_width = qkv.shape[1]
    for first in range(0, group_width, 256):
        qkv[:, first : first + 256] = (
            jnp.dot(
                normed[...], attention_full[:, first : first + 256], preferred_element_type=FLOAT
            )
            + bias[:, first : first + 256]
        )

    def columns(at):
        return pl.ds(pl.multiple_of(at * HD, HD), HD)

    def key_head(at):
        keys[:, columns(at)] = turned(
            qkv[:, columns(heads + at)], cosine[...], sine[...]
        ).astype(BFLOAT)
        values[:, columns(at)] = qkv[:, columns(heads + kv_heads + at)].astype(BFLOAT)

    loop(0, kv_heads, key_head)

    def head(at):
        query[:, columns(at)] = turned(qkv[:, columns(at)], cosine[...], sine[...]).astype(BFLOAT)
        group = columns(at // share)
        for first in (0, half):
            last = first + half
            probs = softmax_of(
                query[first:last, columns(at)],
                keys[:last, group],
                ids[first:last, :],
                key_ids[:, :last],
                first,
            )
            attn[first:last, columns(at)] = jnp.dot(
                probs.astype(BFLOAT), values[:last, group], preferred_element_type=FLOAT
            ).astype(BFLOAT)

    loop(0, heads, head)
    for first in range(0, depth, 256):
        branch[:, first : first + 256] = lax.dot_general(
            attn[...],
            attention_full[first : first + 256, group_width:],
            (((1,), (1,)), ((), ())),
            preferred_element_type=FLOAT,
        ).astype(BFLOAT)
    sum_copy = pltpu.make_async_remote_copy(
        src_ref=branch,
        dst_ref=branch_came,
        send_sem=here_sem.at[3],
        recv_sem=here_sem.at[4],
        device_id={"tensor": 1 - side},
        device_id_type=pl.DeviceIdType.MESH,
    )
    sum_copy.start()
    pump(1, 1)
    pump(1, 2)
    x_rows(grads_all, 0).wait()
    core_rows(grads_all, 1).start()
    pump(2, 0)
    sum_copy.wait()
    for first in range(0, count, 128):
        span = slice(first, first + 128)
        value = tokens[span, :].astype(FLOAT) + (
            branch[span, :].astype(FLOAT) + branch_came[span, :].astype(FLOAT)
        )
        hidden[span, :] = value
        normed_two[span, :] = norm(value, gains[1:2, :])
    own_tokens = pltpu.make_async_copy(normed_two, tokens_all.at[0:count], here_sem.at[1])
    own_tokens.start()
    own_tokens.wait()
    x_rows(tokens_all, 2).start()
    pump(2, 1)
    pump(2, 2)
    x_rows(tokens_all, 2).wait()
    core_rows(tokens_all, 3).start()
    for hop in range(3, planes):
        for third in range(3):
            pump(hop, third)
    core_rows(grads_all, 1).wait()
    core_rows(tokens_all, 3).wait()
    attention_copy.wait()

    loop(1, planes, lambda turn: to_column(turn).wait_send())

    def sent(turn):
        x_copy(turn).wait_send()
        core_copy(turn, 0).wait_send()
        core_copy(turn, 1).wait_send()

    loop(0, planes, sent)
    for third in range(3):
        loop(1, 4, lambda turn: group_copy(turn, third).wait_send())
    for third in range(3):

        @pl.when(plane < planes - 1)
        def _():
            loop(0, plane + 1, lambda origin: move(origin, third, True).wait_send())

        @pl.when(plane > 0)
        def _():
            loop(plane, planes, lambda origin: move(origin, third, False).wait_send())


def forward_part(
    tokens, gains, bias, cosine, sine, doc_ids, shard, units, grads, devices, heads, kv_heads
):
    count, depth = tokens.shape
    rows, width = shard.shape
    planes = devices // 4
    group_width = bias.shape[0]
    query_width = heads * HD
    hbm = pl.BlockSpec(memory_space=pltpu.HBM)
    vmem = pl.BlockSpec(memory_space=pltpu.VMEM)
    dma = pltpu.SemaphoreType.DMA
    return pl.pallas_call(
        functools.partial(forward_kernel, devices, heads, kv_heads),
        out_shape=[
            jax.ShapeDtypeStruct((count, depth), BFLOAT),
            jax.ShapeDtypeStruct((count, depth), FLOAT),
            jax.ShapeDtypeStruct((count, query_width), BFLOAT),
            jax.ShapeDtypeStruct((count, query_width), BFLOAT),
            jax.ShapeDtypeStruct((count, kv_heads * HD), BFLOAT),
            jax.ShapeDtypeStruct((count, kv_heads * HD), BFLOAT),
            jax.ShapeDtypeStruct((devices * rows, width), BFLOAT),
            jax.ShapeDtypeStruct((devices * rows, units.shape[2]), BFLOAT),
            jax.ShapeDtypeStruct((4 * count, depth), BFLOAT),
            jax.ShapeDtypeStruct((4 * count, depth), BFLOAT),
        ],
        in_specs=[vmem] * 7 + [hbm] * 3,
        out_specs=[vmem] * 6 + [hbm] * 4,
        scratch_shapes=[
            pltpu.VMEM((devices * rows, width), BFLOAT),
            pltpu.VMEM((count, group_width), FLOAT),
            pltpu.VMEM((count, depth), BFLOAT),
            pltpu.VMEM((count, depth), BFLOAT),
            pltpu.VMEM((count, depth), BFLOAT),
            dma((5,)),
            dma((planes,)),
            dma((planes,)),
            dma((planes,)),
            dma((planes,)),
            dma((planes, 2)),
            dma((planes, 2)),
            dma((4, 3)),
            dma((4, 3)),
            dma((planes, 3)),
            dma((planes, 3)),
            dma((planes, 3)),
            dma((4,)),
            dma((4,)),
        ],
        compiler_params=pltpu.CompilerParams(
            collective_id=1, has_side_effects=True, vmem_limit_bytes=48 * 2**20
        ),
        cost_estimate=LIGHT,
    )(
        tokens,
        gains,
        bias[None, :],
        cosine,
        sine,
        doc_ids[:, None],
        doc_ids[None, :],
        shard,
        units,
        grads,
    )


def exchange_kernel(
    near, far, pieces, total, joined, came, work, chain_send, chain_come, group_send, group_come, here_sem
):
    me = lax.axis_index("dp")
    place, plane = lax.rem(me, 4), me // 4
    size = pieces.shape[3]
    width = near.shape[2] // 2

    def flip(stride):
        return me + stride - 2 * stride * lax.rem(me // stride, 2)

    def plane_peer(turn):
        return plane * 4 + lax.rem(place + turn, 4)

    def remote(source, target, send, receive, device):
        return pltpu.make_async_remote_copy(
            src_ref=source,
            dst_ref=target,
            send_sem=send,
            recv_sem=receive,
            device_id={"dp": device},
            device_id_type=pl.DeviceIdType.MESH,
        )

    barrier = pltpu.get_barrier_semaphore()
    for device in [plane_peer(turn) for turn in (1, 2, 3)] + [flip(stride) for stride in HALVES[0][2:]]:
        pl.semaphore_signal(
            barrier, inc=1, device_id={"dp": device}, device_id_type=pl.DeviceIdType.MESH
        )
    pl.semaphore_wait(barrier, 3 + len(HALVES[0][2:]))

    def columns(at):
        return slice(at * width, (at + 1) * width)

    def blocks(step):
        return near.shape[0] >> step

    def offset(step):
        return 2 * near.shape[0] - 2 * blocks(step)

    def move(step, at):
        count = blocks(step)
        if step == 0:
            source = far.at[:, :, columns(at)]
        else:
            first = offset(step - 1) + count
            source = work.at[first : first + count, :, columns(at)]
        first = offset(step)
        return remote(
            source,
            came.at[first : first + count, :, columns(at)],
            chain_send.at[step, at],
            chain_come.at[step, at],
            flip(HALVES[at][step]),
        )

    def regroup(kind, turn):
        owner = lax.rem(place + turn, 4)
        return remote(
            pieces.at[kind, owner],
            joined.at[kind, :, pl.ds(pl.multiple_of(place * size, 128), size)],
            group_send.at[kind, turn],
            group_come.at[kind, turn],
            plane_peer(turn),
        )

    def regroup_wait(kind, turn):
        sender = lax.rem(place + 4 - turn, 4)
        return remote(
            pieces.at[kind, 0],
            joined.at[kind, :, pl.ds(pl.multiple_of(sender * size, 128), size)],
            group_send.at[kind, turn],
            group_come.at[kind, turn],
            me,
        )

    def own(kind):
        return pltpu.make_async_copy(
            pieces.at[kind, place],
            joined.at[kind, :, pl.ds(pl.multiple_of(place * size, 128), size)],
            here_sem.at[kind],
        )

    steps = len(HALVES[0])
    for at in range(2):
        move(0, at).start()
    kinds = range(pieces.shape[0])
    for kind in kinds:
        for turn in (1, 2, 3):
            regroup(kind, turn).start()
        own(kind).start()
    for step in range(steps):
        for at in range(2):
            move(step, at).wait()
            count = blocks(step)
            first = offset(step)
            held = near if step == 0 else work
            begin = 0 if step == 0 else offset(step - 1)
            for block in range(count):
                value = held[begin + block, :, columns(at)].astype(FLOAT) + came[
                    first + block, :, columns(at)
                ].astype(FLOAT)
                if step == steps - 1:
                    total[:, columns(at)] = value
                else:
                    work[first + block, :, columns(at)] = value.astype(BFLOAT)
            if step < steps - 1:
                move(step + 1, at).start()
    for kind in kinds:
        for turn in (1, 2, 3):
            regroup_wait(kind, turn).wait_recv()
            regroup(kind, turn).wait_send()
        own(kind).wait()


HALVES = ((1, 2, 4, 8), (1, 4, 8, 2))


def exchange(near, far, pieces):
    count, rows, width = near.shape
    kinds, _, _, size = pieces.shape
    hbm = pl.BlockSpec(memory_space=pltpu.HBM)
    vmem = pl.BlockSpec(memory_space=pltpu.VMEM)
    dma = pltpu.SemaphoreType.DMA
    return pl.pallas_call(
        exchange_kernel,
        out_shape=[
            jax.ShapeDtypeStruct((rows, width), FLOAT),
            jax.ShapeDtypeStruct((kinds, rows, 4 * size), BFLOAT),
        ],
        in_specs=[vmem, vmem, hbm],
        out_specs=[vmem, hbm],
        scratch_shapes=[
            pltpu.VMEM((2 * count, rows, width), BFLOAT),
            pltpu.VMEM((2 * count, rows, width), BFLOAT),
            dma((4, 2)),
            dma((4, 2)),
            dma((kinds, 4)),
            dma((kinds, 4)),
            dma((kinds,)),
        ],
        compiler_params=pltpu.CompilerParams(
            collective_id=2, has_side_effects=True, vmem_limit_bytes=40 * 2**20
        ),
        cost_estimate=LIGHT,
    )(near, far, pieces)


def backward_part(
    back,
    came,
    hidden,
    cotangent,
    live,
    gain,
    weights,
    normed,
    attn,
    query,
    keys,
    values,
    cosine,
    sine,
    doc_ids,
    devices,
    orders,
):
    count, depth = hidden.shape
    rows = depth // devices
    heads, kv_heads = query.shape[1] // HD, keys.shape[1] // HD
    share = heads // kv_heads
    query_width = heads * HD
    group_width = (heads + 2 * kv_heads) * HD
    width = weights.shape[1]
    half = count // 2
    scale = HD ** (-0.5)

    def body(
        back,
        came,
        hidden,
        cotangent,
        live,
        gain,
        weights,
        normed,
        attn,
        query,
        keys,
        values,
        cosine,
        sine,
        ids,
        key_ids,
        dhidden,
        gain_term,
        bias_term,
        dnormed,
        near,
        far,
        dbranch,
        dattn,
        dqkv,
        dkeys,
        dvalues,
        term,
    ):
        total = jnp.zeros((1, depth), FLOAT)
        for first in range(0, count, 128):
            span = slice(first, first + 128)
            grad = back[span, :].astype(FLOAT) + came[span, :].astype(FLOAT)
            value = hidden[span, :]
            root = lax.rsqrt(jnp.mean(value * value, axis=-1, keepdims=True) + EPS)
            scaled = grad * gain[...]
            result = cotangent[span, :].astype(FLOAT) * live[span, :] + (
                root * scaled
                - value * root * root * root * jnp.mean(scaled * value, axis=-1, keepdims=True)
            )
            dhidden[span, :] = result
            dbranch[span, :] = result.astype(BFLOAT)
            total = total + jnp.sum(grad * value * root, axis=0, keepdims=True)
        gain_term[...] = total
        for first in range(0, query_width, 256):
            dattn[:, first : first + 256] = jnp.dot(
                dbranch[...],
                weights[:, group_width + first : group_width + first + 256],
                preferred_element_type=FLOAT,
            ).astype(BFLOAT)

        def columns(at):
            return pl.ds(pl.multiple_of(at * HD, HD), HD)

        def one_head(at, carry):
            group = at // share

            @pl.when(lax.rem(at, share) == 0)
            def _():
                dkeys[...] = jnp.zeros_like(dkeys)
                dvalues[...] = jnp.zeros_like(dvalues)

            for first in (0, half):
                last = first + half
                rows_here = slice(first, last)
                probs = softmax_of(
                    query[rows_here, columns(at)],
                    keys[:last, columns(group)],
                    ids[rows_here, :],
                    key_ids[:, :last],
                    first,
                )
                dprobs = lax.dot_general(
                    dattn[rows_here, columns(at)],
                    values[:last, columns(group)],
                    (((1,), (1,)), ((), ())),
                    preferred_element_type=FLOAT,
                )
                dscores = (
                    probs * (dprobs - jnp.sum(probs * dprobs, axis=-1, keepdims=True))
                ).astype(BFLOAT)
                dquery = scale * jnp.dot(
                    dscores, keys[:last, columns(group)], preferred_element_type=FLOAT
                )
                dqkv[rows_here, columns(at)] = turned(
                    dquery, cosine[rows_here, :], -sine[rows_here, :]
                ).astype(BFLOAT)
                dkeys[:last, :] += lax.dot_general(
                    dscores,
                    query[rows_here, columns(at)],
                    (((0,), (0,)), ((), ())),
                    preferred_element_type=FLOAT,
                )
                dvalues[:last, :] += lax.dot_general(
                    probs.astype(BFLOAT),
                    dattn[rows_here, columns(at)],
                    (((0,), (0,)), ((), ())),
                    preferred_element_type=FLOAT,
                )

            @pl.when(lax.rem(at, share) == share - 1)
            def _():
                dqkv[:, columns(heads + group)] = turned(
                    dkeys[...] * scale, cosine[...], -sine[...]
                ).astype(BFLOAT)
                dqkv[:, columns(heads + kv_heads + group)] = dvalues[...].astype(BFLOAT)

            return carry

        lax.fori_loop(0, heads, one_head, 0)
        bias_term[...] = jnp.sum(dqkv[...].astype(FLOAT), axis=0, keepdims=True)
        for first in range(0, depth, 256):
            span = slice(first, first + 256)
            dnormed[:, span] = lax.dot_general(
                dqkv[...],
                weights[span, :group_width],
                (((1,), (1,)), ((), ())),
                preferred_element_type=FLOAT,
            ).astype(BFLOAT)
            term[span, :group_width] = lax.dot_general(
                normed[:, span], dqkv[...], (((0,), (0,)), ((), ())), preferred_element_type=FLOAT
            )
            term[span, group_width:] = lax.dot_general(
                dbranch[:, span], attn[...], (((0,), (0,)), ((), ())), preferred_element_type=FLOAT
            )
        me = lax.axis_index("dp")
        for side, order in enumerate(orders):
            span = slice(side * width // 2, (side + 1) * width // 2)
            for place in range(devices):
                block = 0
                for at, stride in enumerate(order):
                    bit = (place >> (len(order) - 1 - at)) & 1
                    block = block + lax.rem(me // stride + bit, 2) * stride
                target = near if place < devices // 2 else far
                target[place % (devices // 2), :, span] = term[
                    pl.ds(pl.multiple_of(block * rows, 8), rows), span
                ].astype(BFLOAT)

    vmem = pl.BlockSpec(memory_space=pltpu.VMEM)
    outs = pl.pallas_call(
        body,
        out_shape=[
            jax.ShapeDtypeStruct((count, depth), FLOAT),
            jax.ShapeDtypeStruct((1, depth), FLOAT),
            jax.ShapeDtypeStruct((1, group_width), FLOAT),
            jax.ShapeDtypeStruct((count, depth), BFLOAT),
            jax.ShapeDtypeStruct((devices // 2, rows, width), BFLOAT),
            jax.ShapeDtypeStruct((devices // 2, rows, width), BFLOAT),
        ],
        in_specs=[vmem] * 16,
        out_specs=[vmem] * 6,
        scratch_shapes=[
            pltpu.VMEM((count, depth), BFLOAT),
            pltpu.VMEM((count, query_width), BFLOAT),
            pltpu.VMEM((count, group_width), BFLOAT),
            pltpu.VMEM((count, HD), FLOAT),
            pltpu.VMEM((count, HD), FLOAT),
            pltpu.VMEM((depth, width), FLOAT),
        ],
        compiler_params=pltpu.CompilerParams(vmem_limit_bytes=56 * 2**20),
        cost_estimate=LIGHT,
    )(
        back,
        came,
        hidden,
        cotangent,
        live,
        gain,
        weights,
        normed,
        attn,
        query,
        keys,
        values,
        cosine,
        sine,
        doc_ids[:, None],
        doc_ids[None, :],
    )
    dhidden, gain_term, bias_term, dnormed, near, far = outs
    return (
        dhidden,
        gain_term[0],
        bias_term[0],
        dnormed,
        near,
        far,
    )


def vector_step(param, moment_new, rate):
    return param - rate * moment_new * lax.rsqrt(
        jnp.mean(moment_new * moment_new, axis=-1, keepdims=True) + EPS
    )


def bits_of(count):
    return [1 << bit for bit in range(count.bit_length() - 1)]


def swap(value, axis, stride):
    count = lax.axis_size(axis)
    return lax.ppermute(value, axis, [(at, at ^ stride) for at in range(count)])


def low_add(one, other):
    return (one.astype(FLOAT) + other.astype(FLOAT)).astype(BFLOAT)


def after(value, *others):
    return lax.optimization_barrier((value,) + others)[0]


def by_distance(value, order):
    me = lax.axis_index("dp")
    down = sorted(order, reverse=True)
    bits = len(order)
    value = value.reshape((2,) * bits + (value.shape[0] >> bits,) + value.shape[1:])
    for at, stride in enumerate(down):
        value = jnp.where((me // stride) % 2 == 1, jnp.flip(value, at), value)
    places = [down.index(stride) for stride in order]
    value = value.transpose(tuple(places) + tuple(range(bits, value.ndim)))
    return value.reshape((-1,) + value.shape[bits + 1 :])


def by_index(value, order):
    me = lax.axis_index("dp")
    down = sorted(order, reverse=True)
    bits = len(order)
    value = value.reshape((2,) * bits + (value.shape[0] >> bits,) + value.shape[1:])
    places = [order.index(stride) for stride in down]
    value = value.transpose(tuple(places) + tuple(range(bits, value.ndim)))
    for at, stride in enumerate(down):
        value = jnp.where((me // stride) % 2 == 1, jnp.flip(value, at), value)
    return value.reshape((-1,) + value.shape[bits + 1 :])


def gather_plane(value, strides):
    for stride in reversed(strides):
        value = jnp.concatenate([value, swap(value, "dp", stride)])
    return value


def regroup(value, strides):
    order = tuple(reversed(strides))
    count = value.shape[0]
    value = by_distance(value, order)
    came = [value[:1]] + [swap(value[at : at + 1], "dp", at) for at in range(1, count)]
    return by_distance(jnp.concatenate(came), order)


def halves_by_distance(order):
    me = lax.axis_index("dp")
    down = sorted(order, reverse=True)
    blocks = []
    for place in range(1 << len(order)):
        block = 0
        for at, stride in enumerate(order):
            far = (place >> (len(order) - 1 - at)) & 1
            bit = (me // stride + far) % 2
            block = block + (bit << (len(order) - 1 - down.index(stride)))
        blocks.append(block)
    blocks = jnp.stack(blocks).astype(jnp.int32)
    half = len(order) and (1 << (len(order) - 1))
    return blocks[:half], blocks[half:]


class Chain:
    def __init__(self, kept, sent, order):
        self.kept, self.order = kept, list(order)
        self.send(sent)

    def send(self, sent):
        self.sent = sent
        self.coming = swap(sent, "dp", self.order.pop(0))

    def come(self, *others):
        came = after(self.coming, *others)
        if not self.order:
            self.total = self.kept.astype(FLOAT) + came.astype(FLOAT)
            return self.total
        half = self.kept.shape[0] // 2
        sent = low_add(self.kept[half:], came[half:])
        self.kept = low_add(self.kept[:half], came[:half])
        self.send(sent)
        return sent

    def finish(self, *others):
        while self.order:
            self.come(*others)
            others = ()
        return self.come(*others)


def shards(
    tokens,
    cotangent,
    doc_ids,
    norm_gains,
    qkv_weight,
    qkv_bias,
    out_weight,
    gate_up_weight,
    down_weight,
    gains_moment,
    qkv_moment,
    bias_moment,
    out_moment,
    gate_up_moment,
    down_moment,
):
    rows = qkv_weight.shape[0]
    count = tokens.shape[0]
    query_width = out_weight.shape[1]
    heads = query_width // HD
    group_width = qkv_weight.shape[1]
    kv_heads = (group_width - query_width) // (2 * HD)
    devices = lax.axis_size("dp")
    me = lax.axis_index("dp")
    strides = bits_of(devices)
    every = tuple(strides)
    plane = 4
    near = strides[:2]
    far = tuple(strides[2:])
    units = down_weight.shape[1]
    part = -(-units // (plane * 128)) * 128
    extra = part * plane - units

    def fetch_rows(value, order):
        for stride in reversed(order):
            value = jnp.concatenate([value, swap(value, "dp", stride)])
        return by_index(value, order)

    def split_units(matrix):
        matrix = jnp.pad(matrix, ((0, 0), (0, extra)))
        return matrix.reshape(rows, plane, part).transpose(1, 0, 2)

    def join_units(value):
        value = value.transpose(1, 0, 2).reshape(rows, plane * part)
        return value[:, :units]

    attention_low = jnp.concatenate([qkv_weight.astype(BFLOAT), out_weight.astype(BFLOAT)], axis=1)
    unit_weights = jnp.concatenate(
        [split_units(one.astype(BFLOAT)) for one in (gate_up_weight[0], gate_up_weight[1], down_weight)],
        axis=2,
    )
    live = (doc_ids >= 0).astype(FLOAT)
    grad_out = cotangent.astype(FLOAT) * live[:, None]
    grad_low = grad_out.astype(BFLOAT)
    near_blocks, far_blocks = halves_by_distance(far)
    positions = positions_of(doc_ids)
    freq = THETA ** (-(2.0 / HD) * jnp.arange(HD // 2, dtype=FLOAT))
    angle = positions.astype(FLOAT)[:, None] * freq[None, :]
    cosine = jnp.cos(angle)
    sine = jnp.sin(angle)
    cosine_two = jnp.concatenate([cosine, cosine], axis=1)
    sine_two = jnp.concatenate([-sine, sine], axis=1)
    inputs = tokens.astype(FLOAT)
    scale_one = rms_scale(inputs)
    if rows % 16 == 0:
        (
            normed,
            hidden1,
            attn,
            query,
            keys,
            values,
            attention_full,
            ffn_full,
            normed2_all,
            grad_all,
        ) = forward_part(
            tokens,
            norm_gains,
            qkv_bias,
            cosine_two,
            sine_two,
            doc_ids,
            attention_low,
            unit_weights,
            grad_low,
            devices,
            heads,
            kv_heads,
        )
    else:
        attention_full = fetch_rows(attention_low, every)
        ffn_full = fetch_rows(regroup(unit_weights, near).reshape(plane * rows, -1), far)
        normed = (inputs * scale_one * norm_gains[0]).astype(BFLOAT)
        qkv = contract(normed, attention_full[:, :group_width], 1, 0) + qkv_bias
        attn, query, keys, values = attend(qkv, cosine_two, sine_two, doc_ids, heads, kv_heads)
        branch = contract(attn, attention_full[:, group_width:], 1, 1).astype(BFLOAT)
        hidden1 = inputs + (branch.astype(FLOAT) + swap(branch, "tensor", 1).astype(FLOAT))
        normed2_all = gather_plane(
            (hidden1 * rms_scale(hidden1) * norm_gains[1]).astype(BFLOAT), near
        )
        grad_all = gather_plane(grad_low, near)
    gate, up, hid, normed2_rows, grad_rows = hidden_units(normed2_all, grad_all, ffn_full)
    down_sent = weight_term(grad_rows, hid, far_blocks, 0, part)
    down_kept = weight_term(grad_rows, after(hid, down_sent), near_blocks, 0, part)
    down_chain = Chain(down_kept, down_sent, far)
    both = hidden_back(after(grad_all, down_kept), ffn_full, gate, up)
    gate_sent = weight_term(normed2_rows, both, far_blocks, 0, part)
    up_sent = weight_term(after(normed2_rows, gate_sent), both, far_blocks, 1, part)
    down_sent = down_chain.come(up_sent)
    both = after(both, down_sent)
    half = plane * count // 2
    back_sent = rows_by_width(both, ffn_full, (0, 1), half, 2 * half)
    back_kept = rows_by_width(after(both, back_sent), ffn_full, (0, 1), 0, half)
    back_chain = Chain(back_kept, back_sent, near)
    back_sent = back_chain.come(back_kept)
    gate_kept = weight_term(after(normed2_rows, back_sent), both, near_blocks, 0, part)
    gate_chain = Chain(gate_kept, gate_sent, far)
    gate_sent = gate_chain.come(gate_kept)
    up_kept = weight_term(after(normed2_rows, gate_sent), both, near_blocks, 1, part)
    up_chain = Chain(up_kept, up_sent, far)
    back = back_chain.come(up_kept).astype(BFLOAT)
    back_came = swap(back, "tensor", 1)
    layer_sent = rows_by_width(after(hid, back), ffn_full, (2,), half, 2 * half)
    layer_kept = rows_by_width(after(hid, layer_sent), ffn_full, (2,), 0, half)
    layer_chain = Chain(layer_kept, layer_sent, near)
    layer_sent = layer_chain.come(layer_kept)
    down_total = down_chain.finish(layer_sent)
    up_sent = up_chain.come(down_total)

    def own_rows(value):
        return join_units(regroup(value.astype(BFLOAT).reshape(plane, rows, part), near)).astype(FLOAT)

    down_shard = own_rows(down_total)
    dhidden1, gain_two, bias_term, dnormed, kept, sent = backward_part(
        back,
        after(back_came, up_sent),
        hidden1,
        cotangent,
        live[:, None],
        norm_gains[1:2],
        attention_full,
        normed,
        attn,
        query,
        keys,
        values,
        cosine_two,
        sine_two,
        doc_ids,
        devices,
        HALVES if devices == 16 else (every, every),
    )
    dnormed_came = swap(dnormed, "tensor", 1)
    if devices == 16:
        gate_total = gate_chain.finish(dnormed)
        layer = layer_chain.come(gate_total).astype(BFLOAT)
        layer_came = swap(layer, "tensor", 1)
        up_total = up_chain.finish(layer)
        pieces = jnp.stack([gate_total, up_total]).astype(BFLOAT)
        attention_shard, joined = exchange(kept, sent, pieces.reshape(2, plane, rows, part))
        layer_came = after(layer_came, attention_shard)
        attention_shard = after(attention_shard, layer_came)
        joined = joined[:, :, :units].astype(FLOAT)
        gate_shard, up_shard = joined[0], joined[1]
        token = attention_shard
    else:
        chain = Chain(kept.reshape(-1, kept.shape[2]), sent.reshape(-1, sent.shape[2]), every)
        gate_total, up_total = gate_chain.finish(dnormed), up_chain.finish(dnormed)
        gate_shard, up_shard = own_rows(gate_total), own_rows(up_total)
        layer = layer_chain.come(up_total).astype(BFLOAT)
        layer_came = swap(layer, "tensor", 1)
        token = attention_shard = chain.finish(layer)
    dnormed = dnormed.astype(FLOAT) + after(dnormed_came, token).astype(FLOAT)
    qkv_shard = attention_shard[:, :group_width]
    out_shard = attention_shard[:, group_width:]
    tokens_grad = dhidden1 + norm_back(dnormed, inputs, scale_one, norm_gains[0])
    gain_one = jnp.sum(dnormed * inputs * scale_one, axis=0)
    gate_up_shard = jnp.stack([gate_shard, up_shard])
    qkv_m = MOMENTUM * qkv_moment + qkv_shard
    out_m = MOMENTUM * out_moment + out_shard
    gate_up_m = MOMENTUM * gate_up_moment + gate_up_shard
    down_m = MOMENTUM * down_moment + down_shard
    wire = BFLOAT if rows % 16 == 0 else FLOAT
    pair = query_width + (group_width - query_width) // 2
    vectors = jnp.concatenate([gain_one, gain_two, bias_term])
    solved, vectors = orthogonalize(
        jnp.concatenate(
            [gate_up_m[0], gate_up_m[1], down_m, qkv_m[:, :pair], out_m, qkv_m[:, pair:]], axis=1
        ).astype(wire),
        vectors.reshape(-1, 128),
        query_width,
        devices,
    )
    vectors = vectors.reshape(-1)
    gains_grad = vectors[: 2 * inputs.shape[1]].reshape(2, -1)
    bias_grad = vectors[2 * inputs.shape[1] :]
    gains_m = MOMENTUM * gains_moment + gains_grad
    bias_m = MOMENTUM * bias_moment + bias_grad
    layer_out = hidden1 + (layer.astype(FLOAT) + layer_came.astype(FLOAT))
    gate_up_update = jnp.stack([solved[:, :units], solved[:, units : 2 * units]]).astype(FLOAT)
    down_update = solved[:, 2 * units : 3 * units].astype(FLOAT)
    last = solved[:, 3 * units :].astype(FLOAT)
    qkv_update = jnp.concatenate([last[:, :pair], last[:, pair + query_width :]], axis=1)
    out_update = last[:, pair : pair + query_width]
    gains_new = vector_step(norm_gains, gains_m, LR_VECTOR)
    bias_new = vector_step(qkv_bias, bias_m, LR_BIAS)
    return (
        layer_out,
        tokens_grad,
        gains_grad,
        qkv_shard,
        bias_grad,
        out_shard,
        gate_up_shard,
        down_shard,
        gains_new,
        qkv_weight - LR_MATRIX * qkv_update,
        bias_new,
        out_weight - LR_OUT * out_update,
        gate_up_weight - LR_MATRIX * gate_up_update,
        down_weight - LR_MATRIX * down_update,
        gains_m,
        qkv_m,
        bias_m,
        out_m,
        gate_up_m,
        down_m,
    )


def solution(mesh):
    placed = (
        P("dp", None),
        P("dp", None),
        P("dp"),
        P(),
        P("dp", "tensor"),
        P("tensor"),
        P("dp", "tensor"),
        P(None, "dp", "tensor"),
        P("dp", "tensor"),
        P(),
        P("dp", "tensor"),
        P("tensor"),
        P("dp", "tensor"),
        P(None, "dp", "tensor"),
        P("dp", "tensor"),
    )
    return jax.shard_map(
        shards,
        mesh=mesh,
        in_specs=placed,
        out_specs=(
            P("dp", None),
            P("dp", None),
            P(),
            P("dp", "tensor"),
            P("tensor"),
            P("dp", "tensor"),
            P(None, "dp", "tensor"),
            P("dp", "tensor"),
            P(),
            P("dp", "tensor"),
            P("tensor"),
            P("dp", "tensor"),
            P(None, "dp", "tensor"),
            P("dp", "tensor"),
            P(),
            P("dp", "tensor"),
            P("tensor"),
            P("dp", "tensor"),
            P(None, "dp", "tensor"),
            P("dp", "tensor"),
        ),
        check_vma=False,
    )
```
